256 devices in a mesh: seq: 8 (over x_lo, y), head: 32 (over z, x_hi, core).
Axes of the slice: x: 4 (x_hi: 2, x_lo: 2; x = x_hi * 2 + x_lo), y: 4, z: 8, core: 2. Of those that a mesh axis runs over, the one named last changes fastest.
Arguments:
- q_nope: bfloat16 [2048, 16384], P('seq', 'head'), may hold values from -6 to 6
- q_rope: bfloat16 [2048, 8192], P('seq', 'head'), may hold values from -16 to 16
- latent: bfloat16 [4096, 512], P('seq'), may hold values from -6 to 6
- key_rope: bfloat16 [2048, 128], P('seq'), may hold values from -6 to 6
- q_pos: int32 [2048], P('seq'), may hold values from 2048 to 4095, as said below
- k_pos: int32 [4096], P('seq'), may hold values from 0 to 4095, as said below
- w_uk: bfloat16 [128, 128, 512], P('head'), may hold values from -0.5 to 0.5
- w_uv: bfloat16 [128, 512, 128], P('head'), may hold values from -2 to 2
- w_o: bfloat16 [16384, 7168], P('head'), may hold values from -0.046875 to 0.046875
Outputs:
- attention_out: bfloat16 [2048, 7168], P('seq')
The draws below stay inside these ranges and needn't reach their ends.
Inputs may be any that keep to these rules, and one draw needn't show every extreme that they name: `k_pos`: each aligned block b of 512 entries holds the positions b * 512 to (b + 1) * 512 - 1, each once, in any order. `q_pos`: each aligned block b of 256 entries holds the positions 2048 + b * 256 to 2048 + (b + 1) * 256 - 1, each once, in any order.
All inputs are finite; a program needn't handle non-finite values.
Results may differ from the reference program's by a relative error of at most 0.03.
Values may be sent and summed in bfloat16 or wider, within the bound.
No kernel may reach another device: no remote copies, remote signals or barrier semaphores. Data moves between devices by JAX's collectives and lax.ppermute only.
A program may use at most 64 MiB of HBM per device.

```python
import math
import jax
import jax.numpy as jnp
from jax import lax

D = 7168
LATENT = 512
NOPE = 128
ROPE = 64
VDIM = 128
Q_DEV = 256
KEY_DEV = 512
HEADS = 128
QUERIES = 2048
KEYS = 4096


def draw_q_nope(key, part):
    key = jax.random.fold_in(key, 11)
    values = jnp.clip(jax.random.normal(key, (QUERIES, HEADS * NOPE), jnp.float32), -6.0, 6.0)
    return values.astype(jnp.bfloat16)


def draw_q_rope(key, part):
    key = jax.random.fold_in(key, 12)
    values = jnp.clip(jax.random.normal(key, (QUERIES, HEADS * ROPE), jnp.float32), -6.0, 6.0)
    return values.astype(jnp.bfloat16)


def draw_key_rope(key, part):
    key = jax.random.fold_in(key, 13)
    values = jnp.clip(jax.random.normal(key, (KEYS, ROPE), jnp.float32), -6.0, 6.0)
    return values.reshape(KEYS // 2, 2 * ROPE).astype(jnp.bfloat16)


def block_permutations(key, blocks, width, offset):
    block_keys = jax.random.split(key, blocks)
    shuffled = jax.vmap(lambda single: jax.random.permutation(single, width))(block_keys)
    starts = jnp.arange(blocks, dtype=jnp.int32) * width + offset
    return (shuffled.astype(jnp.int32) + starts[:, None]).reshape(blocks * width).astype(jnp.int32)


def draw_k_pos(key, part):
    key = jax.random.fold_in(key, 21)
    return block_permutations(key, KEYS // KEY_DEV, KEY_DEV, 0)


def draw_q_pos(key, part):
    key = jax.random.fold_in(key, 22)
    return block_permutations(key, QUERIES // Q_DEV, Q_DEV, KEYS - QUERIES)


def level_of(rng, shape, cuts, low, largest):
    def one(axis_at, blocks):
        heights = jax.random.uniform(jax.random.fold_in(jax.random.fold_in(rng, 6), axis_at), (blocks,), jnp.float32, low / len(cuts), largest / len(cuts))
        return jnp.repeat(jnp.exp(heights), shape[axis_at] // blocks).reshape((-1,) + (1,) * (len(shape) - axis_at - 1))

    loudness = one(*cuts[0])
    for cut in cuts[1:]:
        loudness = loudness * one(*cut)
    return loudness


def normal_values(stream_key, shape, spread, bound, cuts=(), held_as=jnp.bfloat16):
    values = spread * jax.random.normal(stream_key, shape, jnp.float32)
    if cuts:
        values = values * level_of(stream_key, shape, cuts, -0.22, 0.18)
    return jnp.clip(values, -bound, bound).astype(held_as)


def setup_inputs(seed: int = 0) -> dict:
    key_list = jax.random.split(jax.random.key(seed), 10)
    q_nope = draw_q_nope(jax.random.fold_in(key_list[9], 71), 0)
    q_rope = draw_q_rope(jax.random.fold_in(key_list[9], 71), 0)
    latent = normal_values(key_list[2], (KEYS, LATENT), 1.0, 6.0, ((0, 8),))
    key_rope = draw_key_rope(jax.random.fold_in(key_list[9], 71), 0)
    q_pos = draw_q_pos(jax.random.fold_in(key_list[9], 71), 0)
    k_pos = draw_k_pos(jax.random.fold_in(key_list[9], 71), 0)
    w_uk = normal_values(key_list[6], (HEADS, NOPE, LATENT), NOPE ** -0.5, 0.5, ((0, 32),))
    w_uv = normal_values(key_list[7], (HEADS, LATENT, VDIM), (max(LATENT // 64, 1)) ** -0.5, 2.0, ((0, 32),))
    w_o = normal_values(key_list[8], (HEADS * VDIM, D), (HEADS * VDIM) ** -0.5, 0.046875, ((0, 32),))
    return dict(q_nope=q_nope, q_rope=q_rope, latent=latent, key_rope=key_rope, q_pos=q_pos, k_pos=k_pos, w_uk=w_uk, w_uv=w_uv, w_o=w_o)


def reference(q_nope, q_rope, latent, key_rope, q_pos, k_pos, w_uk, w_uv, w_o):
    score_scale = 1.0 / math.sqrt(NOPE + ROPE)
    nope_heads = q_nope.reshape(QUERIES, HEADS, NOPE).transpose(1, 0, 2)
    rope_heads = q_rope.reshape(QUERIES, HEADS, ROPE).transpose(1, 0, 2)
    rope_keys = key_rope.reshape(KEYS, ROPE)
    visible = k_pos[None, :] <= q_pos[:, None]

    def one_head(operands):
        nope_rows, rope_rows, key_weight, value_weight = operands
        query_latent = jnp.dot(nope_rows, key_weight, preferred_element_type=jnp.float32).astype(jnp.bfloat16)
        scores = jnp.dot(query_latent, latent.T, preferred_element_type=jnp.float32)
        scores = (scores + jnp.dot(rope_rows, rope_keys.T, preferred_element_type=jnp.float32)) * score_scale
        scores = jnp.where(visible, scores, -1e+30)
        highest = lax.optimization_barrier(jnp.max(scores, axis=1, keepdims=True))
        exponent = jnp.where(visible, jnp.exp(scores - highest), 0.0)
        totals = lax.optimization_barrier(jnp.sum(exponent, axis=1, keepdims=True))
        summed = jnp.dot(exponent.astype(jnp.bfloat16), latent, preferred_element_type=jnp.float32)
        context = (summed / totals).astype(jnp.bfloat16)
        return jnp.dot(context, value_weight, preferred_element_type=jnp.float32).astype(jnp.bfloat16)
    head_rows = lax.map(one_head, (nope_heads, rope_heads, w_uk, w_uv))
    flat_rows = head_rows.transpose(1, 0, 2).reshape(QUERIES, HEADS * VDIM)
    return jnp.dot(flat_rows, w_o, preferred_element_type=jnp.float32).astype(jnp.bfloat16)
```

```python
import functools
import math

import jax
import jax.numpy as jnp
from jax import lax
from jax.experimental import pallas as pl
from jax.experimental.pallas import tpu as pltpu
from jax.sharding import Mesh, PartitionSpec as P

F32, BF16, I32 = jnp.float32, jnp.bfloat16, jnp.int32
LOW = -1e30
LANES = 128
SEQ = ("xl", "y")
HEAD = ("z", "xh", "core")
VMEM = pl.BlockSpec(memory_space=pltpu.VMEM)
SMEM = pl.BlockSpec(memory_space=pltpu.SMEM)


def call(kernel, outs, args, specs=None, scratch=(), flops=0, moved=0, vmem=24):
    return pl.pallas_call(
        kernel,
        out_shape=outs,
        in_specs=specs or [VMEM] * len(args),
        out_specs=jax.tree.map(lambda _: VMEM, outs),
        scratch_shapes=list(scratch),
        compiler_params=pltpu.CompilerParams(vmem_limit_bytes=vmem * 2**20),
        cost_estimate=pl.CostEstimate(flops=flops, bytes_accessed=moved, transcendentals=0),
    )(*args)


def shape(dims, dtype=BF16):
    return jax.ShapeDtypeStruct(tuple(dims), dtype)


def pack_kernel(place, latent, rope, pos, pack, half):
    keys, width = latent.shape
    pairs, two = rope.shape
    rope_width = two // 2
    local = pos[...] % keys
    order = (lax.broadcasted_iota(I32, (keys, keys), 0) == local).astype(BF16)
    sorted_latent = jnp.dot(order, latent[...], preferred_element_type=F32)
    token = lax.broadcasted_iota(I32, (keys, pairs), 0)
    pair = lax.broadcasted_iota(I32, (keys, pairs), 1)
    even = (token == 2 * pair).astype(BF16)
    odd = (token == 2 * pair + 1).astype(BF16)
    spread_even = jnp.dot(even, rope[...], preferred_element_type=F32)
    spread_odd = jnp.dot(odd, rope[...], preferred_element_type=F32)
    rows = jnp.concatenate(
        [spread_even[:, :rope_width], spread_odd[:, rope_width:]], axis=1
    ).astype(BF16)
    ordered = jnp.dot(order, rows, preferred_element_type=F32)
    turned = jnp.transpose(ordered)
    pack[pl.ds(0, keys), :] = sorted_latent.astype(BF16)
    pack[pl.ds(keys, rope_width), :] = (turned[:rope_width] + turned[rope_width:]).astype(BF16)
    span = half.shape[0]
    half[...] = pack[pl.ds(pl.multiple_of(place[0] * span, span), span), :]


def pack_keys(core, latent, key_rope, k_pos):
    keys, width = latent.shape
    rope_width = key_rope.shape[0] * key_rope.shape[1] // keys
    rows = keys + rope_width
    return call(
        pack_kernel,
        [shape((rows, width)), shape((rows // 2, width))],
        [core.reshape(1), latent, key_rope, k_pos.reshape(1, keys)],
        [SMEM, VMEM, VMEM, VMEM],
        flops=2 * keys * keys * width,
        moved=3 * keys * width * 2,
    )


def query_kernel(scale, q_nope, q_rope, w_uk, out):
    heads, nope, width = w_uk.shape
    queries = q_nope.shape[0]
    rope = q_rope.shape[1] // heads
    for h in range(heads):
        rows = pl.ds(h * queries, queries)
        absorbed = jnp.dot(
            q_nope[:, h * nope : (h + 1) * nope], w_uk[h], preferred_element_type=F32
        )
        out[rows, pl.ds(0, width)] = (absorbed * scale).astype(BF16)
        rotary = q_rope[:, h * rope : (h + 1) * rope].astype(F32) * scale
        out[rows, pl.ds(width, rope)] = rotary.astype(BF16)


def absorb(q_nope, q_rope, w_uk):
    heads, nope, width = w_uk.shape
    queries = q_nope.shape[0]
    rope = q_rope.shape[1] // heads
    scale = math.log2(math.e) / math.sqrt(nope + rope)
    return call(
        functools.partial(query_kernel, scale),
        shape((heads * queries, width + rope)),
        [q_nope, q_rope, w_uk],
        flops=2 * queries * heads * nope * width,
        moved=2 * heads * queries * (nope + width),
    )


def attend_kernel(layout, first, last, heads, ids, *refs):
    pieces = sum(len(block) for block in layout)
    blocks, refs = refs[:pieces], refs[pieces:]
    query, positions = refs[:2]
    refs = refs[2:]
    if not first:
        old_top, old_total, old_acc = refs[:3]
        refs = refs[3:]
    if last:
        w_uv, out, top, total, acc, keys_in, turned = refs
    else:
        top, total, acc, keys_in, turned = refs
    count, rows, width = keys_in.shape
    keys = width
    queries = query.shape[0] // heads
    rope = rows - keys
    if first:
        top[...] = jnp.full_like(top, LOW)
        total[...] = jnp.zeros_like(total)
        acc[...] = jnp.zeros_like(acc)
    else:
        top[...] = old_top[...]
        total[...] = old_total[...]
        acc[...] = old_acc[...]
    diagonal, core = ids[0], ids[1]
    at = 0
    for b, block in enumerate(layout):
        for side, start, size in block:
            offset = start
            if side != 2:
                offset = pl.multiple_of(
                    (core if side == 0 else 1 - core) * (rows // 2) + start, 16
                )
            keys_in[b, pl.ds(offset, size), :] = blocks[at][...]
            at += 1

    def work(b, masked):
        latents = keys_in[b, pl.ds(0, keys), :]
        turned[pl.ds(0, width), :] = jnp.transpose(latents)
        turned[pl.ds(width, rope), :] = keys_in[b, pl.ds(keys, rope), :]
        for h in range(heads):
            part = pl.ds(h * queries, queries)
            scores = jnp.dot(query[part, :], turned[...], preferred_element_type=F32)
            if masked:
                limit = positions[...] - diagonal * keys
                where = lax.broadcasted_iota(I32, (queries, keys), 1)
                scores = jnp.where(where <= limit, scores, LOW)
            before = top[part, :]
            now = jnp.maximum(before, jnp.max(scores, axis=1, keepdims=True))
            factor = jnp.exp2(before - now)
            wide = jnp.concatenate([now] * (keys // LANES), axis=1)
            exps = jnp.exp2(scores - wide)
            sums = exps[:, :LANES]
            for t in range(1, keys // LANES):
                sums = sums + exps[:, t * LANES : (t + 1) * LANES]
            top[part, :] = now
            total[part, :] = total[part, :] * factor + sums
            stretch = jnp.concatenate([factor] * (width // LANES), axis=1)
            acc[part, :] = acc[part, :] * stretch + jnp.dot(
                exps.astype(BF16), latents, preferred_element_type=F32
            )

    def step(b, unused):
        block_id = ids[2 + b]

        @pl.when(block_id < diagonal)
        def _():
            work(b, False)

        @pl.when(block_id == diagonal)
        def _():
            work(b, True)

        return unused

    lax.fori_loop(0, count, step, 0)
    if last:
        for h in range(heads):
            part = pl.ds(h * queries, queries)
            sums = jnp.sum(total[part, :], axis=1, keepdims=True)
            context = (acc[part, :] / sums).astype(BF16)
            value = w_uv.shape[2]
            out[:, pl.ds(h * value, value)] = jnp.dot(
                context, w_uv[h], preferred_element_type=F32
            ).astype(BF16)


def attend(layout, pieces, ids, query, positions, state, w_uv, heads, rows):
    width = pieces[0].shape[1]
    total_rows = query.shape[0]
    queries = total_rows // heads
    first, last = state is None, w_uv is not None
    stats = [((total_rows, LANES), F32), ((total_rows, LANES), F32), ((total_rows, width), F32)]
    args = [ids, *pieces, query, positions]
    if not first:
        args += list(state)
    scratch = [
        pltpu.VMEM((len(layout), rows, width), BF16),
        pltpu.VMEM((query.shape[1], width), BF16),
    ]
    if last:
        args.append(w_uv)
        outs = shape((queries, heads * w_uv.shape[2]))
        scratch = [pltpu.VMEM(*s) for s in stats] + scratch
    else:
        outs = [shape(*s) for s in stats]
    return call(
        functools.partial(attend_kernel, layout, first, last, heads),
        outs,
        args,
        [SMEM] + [VMEM] * (len(args) - 1),
        scratch,
        flops=4 * total_rows * width * width * len(layout),
        moved=2 * total_rows * width * 4,
        vmem=32,
    )


def project_kernel(core, mine, other, w_mine, w_other, out):
    out[...] = (
        jnp.dot(mine[...], w_mine[...], preferred_element_type=F32)
        + jnp.dot(other[...], w_other[...], preferred_element_type=F32)
    ).astype(BF16)


def project(core, mine, other, w_o, w_other):
    queries, depth = mine.shape
    columns = w_other.shape[1]
    tile = 512
    tiles = columns // tile
    return pl.pallas_call(
        project_kernel,
        out_shape=shape((queries, columns)),
        grid_spec=pltpu.PrefetchScalarGridSpec(
            num_scalar_prefetch=1,
            grid=(tiles,),
            in_specs=[
                pl.BlockSpec((queries, depth), lambda i, c: (0, 0)),
                pl.BlockSpec((queries, depth), lambda i, c: (0, 0)),
                pl.BlockSpec((depth, tile), lambda i, c: (0, c[0] * tiles + i)),
                pl.BlockSpec((depth, tile), lambda i, c: (0, i)),
            ],
            out_specs=pl.BlockSpec((queries, tile), lambda i, c: (0, i)),
        ),
        compiler_params=pltpu.CompilerParams(vmem_limit_bytes=16 * 2**20),
        cost_estimate=pl.CostEstimate(
            flops=4 * queries * depth * columns, bytes_accessed=4 * depth * columns, transcendentals=0
        ),
    )(core.reshape(1), mine, other, w_o, w_other)


def shift(x, axes, by, n):
    return lax.ppermute(x, axes, [(i, (i + by) % n) for i in range(n)])


def per_device(sizes, q_nope, q_rope, latent, key_rope, q_pos, k_pos, w_uk, w_uv, w_o):
    heads = w_uk.shape[0]
    queries = q_nope.shape[0]
    keys = latent.shape[0]
    columns = w_o.shape[1] // 2
    core, xl, y = lax.axis_index("core"), lax.axis_index("xl"), lax.axis_index("y")
    swap = lambda a: shift(a, "core", 1, 2)
    ny, nx = sizes["y"], sizes["xl"] * sizes["xh"]
    spot = lambda x: (x % nx % sizes["xl"]) * sizes["xh"] + x % nx // sizes["xl"]
    shift_x = lambda a, by: lax.ppermute(
        a, ("xl", "xh"), [(spot(x), spot(x + by)) for x in range(nx)]
    )

    pack, half = pack_keys(core, latent, key_rope, k_pos)
    rows = pack.shape[0]
    span = rows // 2
    below = shift(half, "y", 1, ny)
    above = shift(half, "y", -1, ny)
    across = shift_x(half, 1)
    w_other = swap(lax.dynamic_slice(w_o, (0, (1 - core) * columns), (w_o.shape[0], columns)))
    query = absorb(q_nope, q_rope, w_uk)
    positions = q_pos.reshape(queries, 1)
    far = shift(below, "y", 1, ny)
    across_below = shift_x(below, 1)
    across_above = shift_x(above, -1)
    cut = span // 2
    across_far = (shift_x(far[:cut], 1), shift_x(far[cut:], -1))

    own_id = xl * ny + y
    near = lambda d: xl * ny + (y + d) % ny
    over = lambda d: (1 - xl) * ny + (y + d) % ny
    first_query = sizes["q0"] + own_id * queries
    diagonal = first_query // keys
    ids = lambda *b: jnp.stack([diagonal, core, *b]).astype(I32)
    both = [(0, 0, span), (1, 0, span)]
    state = attend(
        [[(2, 0, rows)], both, both, both],
        [pack, below, swap(below), above, swap(above), across, swap(across)],
        ids(own_id, near(-1), near(1), over(0)),
        query, positions, None, None, heads, rows,
    )
    state = attend(
        [both, both, both],
        [far, swap(far), across_below, swap(across_below), across_above, swap(across_above)],
        ids(near(2), over(-1), over(1)),
        query, positions, state, None, heads, rows,
    )
    quarters = [(0, 0, cut), (1, 0, cut), (0, cut, span - cut), (1, cut, span - cut)]
    head_out = attend(
        [quarters],
        [across_far[0], swap(across_far[0]), across_far[1], swap(across_far[1])],
        ids(over(2)),
        query, positions, state, w_uv, heads, rows,
    )
    partial_out = project(core, head_out, swap(head_out), w_o, w_other)
    piece = lax.psum_scatter(partial_out, "z", scatter_dimension=0, tiled=True)
    piece = (piece.astype(F32) + shift(piece, "xh", 1, 2).astype(F32)).astype(BF16)
    mine = lax.all_gather(piece, "z", axis=0, tiled=True)
    other = swap(mine)
    return jnp.concatenate(
        [jnp.where(core == 0, mine, other), jnp.where(core == 0, other, mine)], axis=1
    )


def solution(mesh):
    sizes = {"xl": 2, "y": 4, "z": 8, "xh": 2, "core": 2, "q0": 2048}
    names = ("xl", "y", "z", "xh", "core")
    fine = Mesh(mesh.devices.reshape([sizes[n] for n in names]), names)
    return jax.shard_map(
        functools.partial(per_device, sizes),
        mesh=fine,
        in_specs=(
            P(SEQ, HEAD),
            P(SEQ, HEAD),
            P(SEQ, None),
            P(SEQ, None),
            P(SEQ),
            P(SEQ),
            P(HEAD, None, None),
            P(HEAD, None, None),
            P(HEAD, None),
        ),
        out_specs=P(SEQ, None),
        check_vma=False,
    )
```

```python
import functools
import math

import jax
import jax.numpy as jnp
from jax import lax
from jax.experimental import pallas as pl
from jax.experimental.pallas import tpu as pltpu
from jax.sharding import Mesh, PartitionSpec as P

F32, BF16, I32 = jnp.float32, jnp.bfloat16, jnp.int32
LOW = -1e30
LANES = 128
SEQ = ("xl", "y")
HEAD = ("z", "xh", "core")
VMEM = pl.BlockSpec(memory_space=pltpu.VMEM)
SMEM = pl.BlockSpec(memory_space=pltpu.SMEM)


def call(kernel, outs, args, specs=None, scratch=(), flops=0, moved=0, vmem=24):
    return pl.pallas_call(
        kernel,
        out_shape=outs,
        in_specs=specs or [VMEM] * len(args),
        out_specs=jax.tree.map(lambda _: VMEM, outs),
        scratch_shapes=list(scratch),
        compiler_params=pltpu.CompilerParams(vmem_limit_bytes=vmem * 2**20),
        cost_estimate=pl.CostEstimate(flops=flops, bytes_accessed=moved, transcendentals=0),
    )(*args)


def shape(dims, dtype=BF16):
    return jax.ShapeDtypeStruct(tuple(dims), dtype)


def pack_kernel(place, latent, rope, pos, pack, half):
    keys, width = latent.shape
    pairs, two = rope.shape
    rope_width = two // 2
    local = pos[...] % keys
    order = (lax.broadcasted_iota(I32, (keys, keys), 0) == local).astype(BF16)
    sorted_latent = jnp.dot(order, latent[...], preferred_element_type=F32)
    token = lax.broadcasted_iota(I32, (keys, pairs), 0)
    pair = lax.broadcasted_iota(I32, (keys, pairs), 1)
    even = (token == 2 * pair).astype(BF16)
    odd = (token == 2 * pair + 1).astype(BF16)
    spread_even = jnp.dot(even, rope[...], preferred_element_type=F32)
    spread_odd = jnp.dot(odd, rope[...], preferred_element_type=F32)
    rows = jnp.concatenate(
        [spread_even[:, :rope_width], spread_odd[:, rope_width:]], axis=1
    ).astype(BF16)
    ordered = jnp.dot(order, rows, preferred_element_type=F32)
    turned = jnp.transpose(ordered)
    pack[pl.ds(0, keys), :] = sorted_latent.astype(BF16)
    pack[pl.ds(keys, rope_width), :] = (turned[:rope_width] + turned[rope_width:]).astype(BF16)
    span = half.shape[0]
    half[...] = pack[pl.ds(pl.multiple_of(place[0] * span, span), span), :]


def pack_keys(core, latent, key_rope, k_pos):
    keys, width = latent.shape
    rope_width = key_rope.shape[0] * key_rope.shape[1] // keys
    rows = keys + rope_width
    return call(
        pack_kernel,
        [shape((rows, width)), shape((rows // 2, width))],
        [core.reshape(1), latent, key_rope, k_pos.reshape(1, keys)],
        [SMEM, VMEM, VMEM, VMEM],
        flops=2 * keys * keys * width,
        moved=3 * keys * width * 2,
    )


def query_kernel(scale, q_nope, q_rope, w_uk, out):
    heads, nope, width = w_uk.shape
    queries = q_nope.shape[0]
    rope = q_rope.shape[1] // heads
    for h in range(heads):
        rows = pl.ds(h * queries, queries)
        absorbed = jnp.dot(
            q_nope[:, h * nope : (h + 1) * nope], w_uk[h], preferred_element_type=F32
        )
        out[rows, pl.ds(0, width)] = (absorbed * scale).astype(BF16)
        rotary = q_rope[:, h * rope : (h + 1) * rope].astype(F32) * scale
        out[rows, pl.ds(width, rope)] = rotary.astype(BF16)


def absorb(q_nope, q_rope, w_uk):
    heads, nope, width = w_uk.shape
    queries = q_nope.shape[0]
    rope = q_rope.shape[1] // heads
    scale = math.log2(math.e) / math.sqrt(nope + rope)
    return call(
        functools.partial(query_kernel, scale),
        shape((heads * queries, width + rope)),
        [q_nope, q_rope, w_uk],
        flops=2 * queries * heads * nope * width,
        moved=2 * heads * queries * (nope + width),
    )


def attend_kernel(layout, first, last, heads, ids, *refs):
    pieces = sum(len(block) for block in layout)
    blocks, refs = refs[:pieces], refs[pieces:]
    query, positions = refs[:2]
    refs = refs[2:]
    if not first:
        old_top, old_total, old_acc = refs[:3]
        refs = refs[3:]
    if last:
        w_uv, out, top, total, acc, keys_in, turned = refs
    else:
        top, total, acc, keys_in, turned = refs
    count, rows, width = keys_in.shape
    keys = width
    queries = query.shape[0] // heads
    rope = rows - keys
    if first:
        top[...] = jnp.full_like(top, LOW)
        total[...] = jnp.zeros_like(total)
        acc[...] = jnp.zeros_like(acc)
    else:
        top[...] = old_top[...]
        total[...] = old_total[...]
        acc[...] = old_acc[...]
    diagonal, core = ids[0], ids[1]
    at = 0
    for b, block in enumerate(layout):
        for side, start, size in block:
            offset = start
            if side != 2:
                offset = pl.multiple_of(
                    (core if side == 0 else 1 - core) * (rows // 2) + start, 16
                )
            keys_in[b, pl.ds(offset, size), :] = blocks[at][...]
            at += 1

    def work(b, masked):
        latents = keys_in[b, pl.ds(0, keys), :]
        turned[pl.ds(0, width), :] = jnp.transpose(latents)
        turned[pl.ds(width, rope), :] = keys_in[b, pl.ds(keys, rope), :]
        for h in range(heads):
            part = pl.ds(h * queries, queries)
            scores = jnp.dot(query[part, :], turned[...], preferred_element_type=F32)
            if masked:
                limit = positions[...] - diagonal * keys
                where = lax.broadcasted_iota(I32, (queries, keys), 1)
                scores = jnp.where(where <= limit, scores, LOW)
            before = top[part, :]
            now = jnp.maximum(before, jnp.max(scores, axis=1, keepdims=True))
            factor = jnp.exp2(before - now)
            wide = jnp.concatenate([now] * (keys // LANES), axis=1)
            exps = jnp.exp2(scores - wide)
            sums = exps[:, :LANES]
            for t in range(1, keys // LANES):
                sums = sums + exps[:, t * LANES : (t + 1) * LANES]
            top[part, :] = now
            total[part, :] = total[part, :] * factor + sums
            stretch = jnp.concatenate([factor] * (width // LANES), axis=1)
            acc[part, :] = acc[part, :] * stretch + jnp.dot(
                exps.astype(BF16), latents, preferred_element_type=F32
            )

    def step(b, unused):
        block_id = ids[2 + b]

        @pl.when(block_id < diagonal)
        def _():
            work(b, False)

        @pl.when(block_id == diagonal)
        def _():
            work(b, True)

        return unused

    lax.fori_loop(0, count, step, 0)
    if last:
        for h in range(heads):
            part = pl.ds(h * queries, queries)
            sums = jnp.sum(total[part, :], axis=1, keepdims=True)
            context = (acc[part, :] / sums).astype(BF16)
            value = w_uv.shape[2]
            out[:, pl.ds(h * value, value)] = jnp.dot(
                context, w_uv[h], preferred_element_type=F32
            ).astype(BF16)


def attend(layout, pieces, ids, query, positions, state, w_uv, heads, rows):
    width = pieces[0].shape[1]
    total_rows = query.shape[0]
    queries = total_rows // heads
    first, last = state is None, w_uv is not None
    stats = [((total_rows, LANES), F32), ((total_rows, LANES), F32), ((total_rows, width), F32)]
    args = [ids, *pieces, query, positions]
    if not first:
        args += list(state)
    scratch = [
        pltpu.VMEM((len(layout), rows, width), BF16),
        pltpu.VMEM((query.shape[1], width), BF16),
    ]
    if last:
        args.append(w_uv)
        outs = shape((queries, heads * w_uv.shape[2]))
        scratch = [pltpu.VMEM(*s) for s in stats] + scratch
    else:
        outs = [shape(*s) for s in stats]
    return call(
        functools.partial(attend_kernel, layout, first, last, heads),
        outs,
        args,
        [SMEM] + [VMEM] * (len(args) - 1),
        scratch,
        flops=4 * total_rows * width * width * len(layout),
        moved=2 * total_rows * width * 4,
        vmem=32,
    )


def project_kernel(ring, place, mine, other, w_mine, w_other, out, left, right):
    chunk = left.shape[0] // ring

    @pl.when(pl.program_id(0) == 0)
    def _():
        for d in range(ring):
            source = pl.ds(pl.multiple_of((place[1] + d) % ring * chunk, chunk), chunk)
            left[pl.ds(d * chunk, chunk), :] = mine[source, :]
            right[pl.ds(d * chunk, chunk), :] = other[source, :]

    out[...] = (
        jnp.dot(left[...], w_mine[...], preferred_element_type=F32)
        + jnp.dot(right[...], w_other[...], preferred_element_type=F32)
    ).astype(BF16)


def project(ring, place, mine, other, w_o, w_other):
    queries, depth = mine.shape
    columns = w_other.shape[1]
    tile = columns // 4
    return pl.pallas_call(
        functools.partial(project_kernel, ring),
        out_shape=shape((queries, columns)),
        grid_spec=pltpu.PrefetchScalarGridSpec(
            num_scalar_prefetch=1,
            grid=(columns // tile,),
            in_specs=[
                pl.BlockSpec((queries, depth), lambda i, c: (0, 0)),
                pl.BlockSpec((queries, depth), lambda i, c: (0, 0)),
                pl.BlockSpec((depth, tile), lambda i, c: (0, c[0] * (columns // tile) + i)),
                pl.BlockSpec((depth, tile), lambda i, c: (0, i)),
            ],
            out_specs=pl.BlockSpec((queries, tile), lambda i, c: (0, i)),
            scratch_shapes=[pltpu.VMEM((queries, depth), BF16)] * 2,
        ),
        compiler_params=pltpu.CompilerParams(vmem_limit_bytes=24 * 2**20),
        cost_estimate=pl.CostEstimate(
            flops=4 * queries * depth * columns, bytes_accessed=4 * depth * columns, transcendentals=0
        ),
    )(place, mine, other, w_o, w_other)


def add_kernel(arrays, terms, *refs):
    outs = refs[arrays:]
    for out, term in zip(outs, terms):
        total = None
        for index, start in term:
            source = refs[index]
            part = source[...].astype(F32)
            size = source.shape[0]
            if size != out.shape[0]:
                part = jnp.concatenate(
                    [jnp.zeros((start, out.shape[1]), F32)] * (start > 0)
                    + [part]
                    + [jnp.zeros((out.shape[0] - start - size, out.shape[1]), F32)]
                    * (start + size < out.shape[0])
                )
            total = part if total is None else total + part
        out[...] = total.astype(BF16)


def add_pieces(arrays, terms, whole=None, blocks=()):
    size = max(a.shape[0] for a in arrays)
    width = arrays[0].shape[1]
    specs = [pl.BlockSpec(a.shape, lambda i: (0, 0)) for a in arrays]
    specs += [pl.BlockSpec((size, width), functools.partial(lambda k, i: (k, 0), k)) for k in blocks]
    args = list(arrays) + [whole] * len(blocks)
    return pl.pallas_call(
        functools.partial(add_kernel, len(args), terms),
        out_shape=[shape((size, width))] * len(terms),
        grid=(1,),
        in_specs=specs,
        out_specs=[pl.BlockSpec((size, width), lambda i: (0, 0))] * len(terms),
        compiler_params=pltpu.CompilerParams(vmem_limit_bytes=16 * 2**20),
        cost_estimate=pl.CostEstimate(flops=0, bytes_accessed=6 * size * width, transcendentals=0),
    )(*args)


def ring_sum(rows, n):
    size = rows.shape[0] // n
    far = n // 2
    cut = size // 2
    up = shift(rows[far * size : far * size + cut], "z", 1, n)
    down = shift(rows[far * size + cut : (far + 1) * size], "z", -1, n)
    offsets = (0, cut)
    for d in range(far - 1, 0, -1):
        up, down = add_pieces_at(up, down, offsets, rows, (d, n - d), size)
        up, down = shift(up, "z", 1, n), shift(down, "z", -1, n)
        offsets = (0, 0)
    return add_pieces([up, down], [[(0, 0), (1, 0), (2, 0)]], rows, (0,))[0]


def add_pieces_at(up, down, offsets, rows, blocks, size):
    width = rows.shape[1]
    specs = [pl.BlockSpec(a.shape, lambda i: (0, 0)) for a in (up, down)]
    specs += [pl.BlockSpec((size, width), functools.partial(lambda k, i: (k, 0), k)) for k in blocks]
    terms = [[(2, 0), (0, offsets[0])], [(3, 0), (1, offsets[1])]]
    return pl.pallas_call(
        functools.partial(add_kernel, 4, terms),
        out_shape=[shape((size, width))] * 2,
        grid=(1,),
        in_specs=specs,
        out_specs=[pl.BlockSpec((size, width), lambda i: (0, 0))] * 2,
        compiler_params=pltpu.CompilerParams(vmem_limit_bytes=16 * 2**20),
        cost_estimate=pl.CostEstimate(flops=0, bytes_accessed=6 * size * width, transcendentals=0),
    )(up, down, rows, rows)


def ring_gather(piece, n):
    far = n // 2
    cut = piece.shape[0] // 2
    found = [(0, 0, piece)]
    up = down = piece
    for d in range(1, far):
        up, down = shift(up, "z", 1, n), shift(down, "z", -1, n)
        found += [(-d, 0, up), (d, 0, down)]
    found.append((far, 0, shift(up[:cut], "z", 1, n)))
    found.append((far, cut, shift(down[cut:], "z", -1, n)))
    return found


def place_kernel(n, where, place, *refs):
    count = len(where)
    mine, other = refs[:count], refs[count : 2 * count]
    out, sems = refs[2 * count :]
    chunk = out.shape[0] // n
    columns = out.shape[1] // 2
    copies = []
    for side, arrays in enumerate((mine, other)):
        half = place[0] if side == 0 else 1 - place[0]
        lanes = pl.ds(pl.multiple_of(half * columns, LANES), columns)
        for (d, row), array in zip(where, arrays):
            start = pl.multiple_of((place[1] + d + n) % n * chunk + row, 16)
            copies.append(
                pltpu.make_async_copy(
                    array, out.at[pl.ds(start, array.shape[0]), lanes], sems.at[len(copies)]
                )
            )
    for copy in copies:
        copy.start()
    for copy in copies:
        copy.wait()


def place_pieces(n, place, where, mine, other, dims):
    hbm = pl.BlockSpec(memory_space=pl.ANY)
    count = len(mine) + len(other)
    return pl.pallas_call(
        functools.partial(place_kernel, n, where),
        out_shape=shape(dims),
        in_specs=[SMEM] + [hbm] * count,
        out_specs=hbm,
        scratch_shapes=[pltpu.SemaphoreType.DMA((count,))],
        compiler_params=pltpu.CompilerParams(vmem_limit_bytes=8 * 2**20),
        cost_estimate=pl.CostEstimate(
            flops=0, bytes_accessed=4 * dims[0] * dims[1], transcendentals=0
        ),
    )(place, *mine, *other)


def shift(x, axes, by, n):
    return lax.ppermute(x, axes, [(i, (i + by) % n) for i in range(n)])


def per_device(sizes, q_nope, q_rope, latent, key_rope, q_pos, k_pos, w_uk, w_uv, w_o):
    heads = w_uk.shape[0]
    queries = q_nope.shape[0]
    keys = latent.shape[0]
    columns = w_o.shape[1] // 2
    core, xl, y = lax.axis_index("core"), lax.axis_index("xl"), lax.axis_index("y")
    swap = lambda a: shift(a, "core", 1, 2)
    ny, nx = sizes["y"], sizes["xl"] * sizes["xh"]
    spot = lambda x: (x % nx % sizes["xl"]) * sizes["xh"] + x % nx // sizes["xl"]
    shift_x = lambda a, by: lax.ppermute(
        a, ("xl", "xh"), [(spot(x), spot(x + by)) for x in range(nx)]
    )

    pack, half = pack_keys(core, latent, key_rope, k_pos)
    rows = pack.shape[0]
    span = rows // 2
    below = shift(half, "y", 1, ny)
    above = shift(half, "y", -1, ny)
    across = shift_x(half, 1)
    w_o, half = lax.optimization_barrier((w_o, half))
    w_other = swap(lax.dynamic_slice(w_o, (0, (1 - core) * columns), (w_o.shape[0], columns)))
    query = absorb(q_nope, q_rope, w_uk)
    positions = q_pos.reshape(queries, 1)
    far = shift(below, "y", 1, ny)
    across_below = shift_x(below, 1)
    across_above = shift_x(above, -1)
    cut = span // 2
    own_id = xl * ny + y
    near = lambda d: xl * ny + (y + d) % ny
    over = lambda d: (1 - xl) * ny + (y + d) % ny
    first_query = sizes["q0"] + own_id * queries
    diagonal = first_query // keys
    ids = lambda *b: jnp.stack([diagonal, core, *b]).astype(I32)
    both = [(0, 0, span), (1, 0, span)]
    state = attend(
        [[(2, 0, rows)], both, both, both],
        [pack, below, swap(below), above, swap(above), across, swap(across)],
        ids(own_id, near(-1), near(1), over(0)),
        query, positions, None, None, heads, rows,
    )
    far, across_below, across_above, state = lax.optimization_barrier(
        (far, across_below, across_above, state)
    )
    across_far = (shift_x(far[:cut], 1), shift_x(far[cut:], -1))
    state = attend(
        [both, both, both],
        [far, swap(far), across_below, swap(across_below), across_above, swap(across_above)],
        ids(near(2), over(-1), over(1)),
        query, positions, state, None, heads, rows,
    )
    across_far, state = lax.optimization_barrier((across_far, state))
    quarters = [(0, 0, cut), (1, 0, cut), (0, cut, span - cut), (1, cut, span - cut)]
    head_out = attend(
        [quarters],
        [across_far[0], swap(across_far[0]), across_far[1], swap(across_far[1])],
        ids(over(2)),
        query, positions, state, w_uv, heads, rows,
    )
    nz = sizes["z"]
    place = jnp.stack([core, lax.axis_index("z")]).astype(I32)
    partial_out = project(nz, place, head_out, swap(head_out), w_o, w_other)
    piece = ring_sum(partial_out, nz)
    piece = add_pieces([piece, shift(piece, "xh", 1, sizes["xh"])], [[(0, 0), (1, 0)]])[0]
    found = ring_gather(piece, nz)
    where = [(d, row) for d, row, _ in found]
    mine = [array for _, _, array in found]
    return place_pieces(
        nz, place, where, mine, [swap(array) for array in mine], (queries, 2 * columns)
    )


def solution(mesh):
    sizes = {"xl": 2, "y": 4, "z": 8, "xh": 2, "core": 2, "q0": 2048}
    names = ("xl", "y", "z", "xh", "core")
    fine = Mesh(mesh.devices.reshape([sizes[n] for n in names]), names)
    return jax.shard_map(
        functools.partial(per_device, sizes),
        mesh=fine,
        in_specs=(
            P(SEQ, HEAD),
            P(SEQ, HEAD),
            P(SEQ, None),
            P(SEQ, None),
            P(SEQ),
            P(SEQ),
            P(HEAD, None, None),
            P(HEAD, None, None),
            P(HEAD, None),
        ),
        out_specs=P(SEQ, None),
        check_vma=False,
    )
```

```python
import functools
import math

import jax
import jax.numpy as jnp
from jax import lax
from jax.experimental import pallas as pl
from jax.experimental.pallas import tpu as pltpu
from jax.sharding import Mesh, PartitionSpec as P

F32, BF16, I32 = jnp.float32, jnp.bfloat16, jnp.int32
LOW = -1e30
LANES = 128
SEQ = ("xl", "y")
HEAD = ("z", "xh", "core")


def call(kernel, outs, args, scratch=(), copies=1, flops=0, moved=0, vmem=24):
    anywhere = pl.BlockSpec(memory_space=pl.ANY)
    return pl.pallas_call(
        kernel,
        out_shape=outs,
        in_specs=[anywhere] * len(args),
        out_specs=jax.tree.map(lambda _: anywhere, outs),
        scratch_shapes=list(scratch) + [pltpu.SemaphoreType.DMA((copies,))],
        compiler_params=pltpu.CompilerParams(vmem_limit_bytes=vmem * 2**20),
        cost_estimate=pl.CostEstimate(flops=flops, bytes_accessed=moved, transcendentals=0),
    )(*args)


def start_all(pairs, sems, first=0):
    copies = [
        pltpu.make_async_copy(source, target, sems.at[first + i])
        for i, (source, target) in enumerate(pairs)
    ]
    for copy in copies:
        copy.start()
    return copies


def wait_all(copies):
    for copy in copies:
        copy.wait()


def room(array):
    return pltpu.VMEM(array.shape, array.dtype)


def shape(dims, dtype=BF16):
    return jax.ShapeDtypeStruct(tuple(dims), dtype)


def pack_kernel(latent_in, rope_in, pos_in, pack_out, half_out, latent, rope, pos, pack, sems):
    copies = start_all([(latent_in, latent), (rope_in, rope), (pos_in, pos)], sems)
    keys, width = latent.shape
    pairs, two = rope.shape
    rope_width = two // 2
    token = lax.broadcasted_iota(I32, (keys, pairs), 0)
    pair = lax.broadcasted_iota(I32, (keys, pairs), 1)
    even = (token == 2 * pair).astype(BF16)
    odd = (token == 2 * pair + 1).astype(BF16)
    wait_all(copies)
    order = (lax.broadcasted_iota(I32, (keys, keys), 0) == pos[...] % keys).astype(BF16)
    sorted_latent = jnp.dot(order, latent[...], preferred_element_type=F32)
    spread_even = jnp.dot(even, rope[...], preferred_element_type=F32)
    spread_odd = jnp.dot(odd, rope[...], preferred_element_type=F32)
    rows = jnp.concatenate(
        [spread_even[:, :rope_width], spread_odd[:, rope_width:]], axis=1
    ).astype(BF16)
    ordered = jnp.dot(order, rows, preferred_element_type=F32)
    turned = jnp.transpose(ordered)
    pack[pl.ds(0, keys), :] = sorted_latent.astype(BF16)
    pack[pl.ds(keys, rope_width), :] = (turned[:rope_width] + turned[rope_width:]).astype(BF16)
    span = half_out.shape[0]
    start = pl.multiple_of(lax.axis_index("core") * span, span)
    wait_all(start_all([(pack.at[pl.ds(start, span), :], half_out), (pack, pack_out)], sems))


def pack_keys(latent, key_rope, k_pos):
    keys, width = latent.shape
    rows = keys + key_rope.shape[0] * key_rope.shape[1] // keys
    args = [latent, key_rope, k_pos.reshape(1, keys)]
    return call(
        pack_kernel,
        [shape((rows, width)), shape((rows // 2, width))],
        args,
        [room(a) for a in args] + [pltpu.VMEM((rows, width), BF16)],
        copies=3,
        flops=2 * keys * keys * width,
        moved=3 * keys * width * 2,
    )


def query_kernel(scale, q_nope_in, q_rope_in, w_uk_in, w_o, after, out, half, q_nope, q_rope, w_uk, query, sems):
    columns = half.shape[1]
    start = pl.multiple_of((1 - lax.axis_index("core")) * columns, LANES)
    pairs = [(q_nope_in, q_nope), (q_rope_in, q_rope), (w_uk_in, w_uk)]
    copies = start_all(pairs, sems)
    slices = start_all([(w_o.at[:, pl.ds(start, columns)], half)], sems, len(pairs))
    wait_all(copies)
    heads, nope, width = w_uk.shape
    queries = q_nope.shape[0]
    rope = q_rope.shape[1] // heads
    for h in range(heads):
        rows = pl.ds(h * queries, queries)
        absorbed = jnp.dot(
            q_nope[:, h * nope : (h + 1) * nope], w_uk[h], preferred_element_type=F32
        )
        query[rows, pl.ds(0, width)] = (absorbed * scale).astype(BF16)
        rotary = q_rope[:, h * rope : (h + 1) * rope].astype(F32) * scale
        query[rows, pl.ds(width, rope)] = rotary.astype(BF16)
    wait_all(slices + start_all([(query, out)], sems))


def absorb(q_nope, q_rope, w_uk, w_o, after):
    heads, nope, width = w_uk.shape
    queries = q_nope.shape[0]
    rope = q_rope.shape[1] // heads
    scale = math.log2(math.e) / math.sqrt(nope + rope)
    result = shape((heads * queries, width + rope))
    return call(
        functools.partial(query_kernel, scale),
        [result, shape((w_o.shape[0], w_o.shape[1] // 2))],
        [q_nope, q_rope, w_uk, w_o, after],
        [room(a) for a in (q_nope, q_rope, w_uk, result)],
        copies=4,
        flops=2 * queries * heads * nope * width,
        moved=2 * heads * queries * (nope + width) + 2 * w_o.shape[0] * w_o.shape[1],
    )


def attend_kernel(layout, first, last, heads, place, *refs):
    pieces = sum(len(block) for block in layout)
    blocks, refs = refs[:pieces], refs[pieces:]
    query_in, positions_in = refs[:2]
    refs = refs[2:]
    if not first:
        old, refs = refs[:3], refs[3:]
    if last:
        w_uv_in, out, refs = refs[0], refs[1], refs[2:]
    else:
        new, refs = refs[:3], refs[3:]
    top, total, acc, keys_in, turned, query, positions, *rest, sems = refs
    state = (top, total, acc)
    count, rows, width = keys_in.shape
    keys = width
    queries = query.shape[0] // heads
    rope = rows - keys
    core = lax.axis_index("core")
    pairs = [(query_in, query), (positions_in, positions)]
    for b, block in enumerate(layout):
        for side, start, size in block:
            offset = start
            if side != 2:
                offset = (core if side == 0 else 1 - core) * (rows // 2) + start
                offset = pl.multiple_of(offset, 16)
            pairs.append((blocks[len(pairs) - 2], keys_in.at[b, pl.ds(offset, size), :]))
    if not first:
        pairs += list(zip(old, state))
    if last:
        w_uv, result = rest
        pairs.append((w_uv_in, w_uv))
    copies = start_all(pairs, sems)
    if first:
        top[...] = jnp.full_like(top, LOW)
        total[...] = jnp.zeros_like(total)
        acc[...] = jnp.zeros_like(acc)
    ids, diagonal = place(keys, queries)
    wait_all(copies)

    def work(b, masked):
        latents = keys_in[b, pl.ds(0, keys), :]
        turned[pl.ds(0, width), :] = jnp.transpose(latents)
        turned[pl.ds(width, rope), :] = keys_in[b, pl.ds(keys, rope), :]
        for h in range(heads):
            part = pl.ds(h * queries, queries)
            scores = jnp.dot(query[part, :], turned[...], preferred_element_type=F32)
            if masked:
                limit = positions[...] - diagonal * keys
                where = lax.broadcasted_iota(I32, (queries, keys), 1)
                scores = jnp.where(where <= limit, scores, LOW)
            before = top[part, :]
            now = jnp.maximum(before, jnp.max(scores, axis=1, keepdims=True))
            factor = jnp.exp2(before - now)
            wide = jnp.concatenate([now] * (keys // LANES), axis=1)
            exps = jnp.exp2(scores - wide)
            sums = exps[:, :LANES]
            for t in range(1, keys // LANES):
                sums = sums + exps[:, t * LANES : (t + 1) * LANES]
            top[part, :] = now
            total[part, :] = total[part, :] * factor + sums
            stretch = jnp.concatenate([factor] * (width // LANES), axis=1)
            acc[part, :] = acc[part, :] * stretch + jnp.dot(
                exps.astype(BF16), latents, preferred_element_type=F32
            )

    def step(b, unused):
        block_id = ids[0]
        for at in range(1, count):
            block_id = jnp.where(b == at, ids[at], block_id)

        @pl.when(block_id < diagonal)
        def _():
            work(b, False)

        @pl.when(block_id == diagonal)
        def _():
            work(b, True)

        return unused

    lax.fori_loop(0, count, step, 0)
    if last:
        for h in range(heads):
            part = pl.ds(h * queries, queries)
            sums = jnp.sum(total[part, :], axis=1, keepdims=True)
            context = (acc[part, :] / sums).astype(BF16)
            value = w_uv.shape[2]
            result[:, pl.ds(h * value, value)] = jnp.dot(
                context, w_uv[h], preferred_element_type=F32
            ).astype(BF16)
        wait_all(start_all([(result, out)], sems))
    else:
        wait_all(start_all(list(zip(state, new)), sems))


def attend(layout, pieces, place, query, positions, state, w_uv, heads, rows):
    width = pieces[0].shape[1]
    total_rows = query.shape[0]
    queries = total_rows // heads
    first, last = state is None, w_uv is not None
    stats = [
        shape((total_rows, LANES), F32),
        shape((total_rows, LANES), F32),
        shape((total_rows, width), F32),
    ]
    args = [*pieces, query, positions]
    if not first:
        args += list(state)
    scratch = [room(s) for s in stats] + [
        pltpu.VMEM((len(layout), rows, width), BF16),
        pltpu.VMEM((query.shape[1], width), BF16),
        room(query),
        room(positions),
    ]
    outs = stats
    if last:
        args.append(w_uv)
        outs = shape((queries, heads * w_uv.shape[2]))
        scratch += [room(w_uv), room(outs)]
    return call(
        functools.partial(attend_kernel, layout, first, last, heads, place),
        outs,
        args,
        scratch,
        copies=len(args),
        flops=16 * total_rows * width * width * len(layout),
        moved=2 * total_rows * width * 4,
        vmem=24,
    )


def project_kernel(ring, tile, mine_in, other_in, w_o, w_other, out, mine, other, w_a, w_b, left, right, result, sems):
    queries, depth = mine.shape
    columns = out.shape[1]
    tiles = columns // tile
    chunk = queries // ring
    inputs = start_all([(mine_in, mine), (other_in, other)], sems)
    base = lax.axis_index("core") * columns
    weights = []
    for t in range(tiles):
        here = pl.ds(t * tile, tile)
        there = pl.ds(pl.multiple_of(base + t * tile, LANES), tile)
        weights.append(
            start_all(
                [(w_o.at[:, there], w_a.at[:, here]), (w_other.at[:, here], w_b.at[:, here])],
                sems,
                2 + 2 * t,
            )
        )
    wait_all(inputs)
    z = lax.axis_index("z")
    for d in range(ring):
        source = pl.ds(pl.multiple_of((z + d) % ring * chunk, chunk), chunk)
        left[pl.ds(d * chunk, chunk), :] = mine[source, :]
        right[pl.ds(d * chunk, chunk), :] = other[source, :]
    done = []
    for t in range(tiles):
        here = pl.ds(t * tile, tile)
        wait_all(weights[t])
        result[:, here] = (
            jnp.dot(left[...], w_a[:, here], preferred_element_type=F32)
            + jnp.dot(right[...], w_b[:, here], preferred_element_type=F32)
        ).astype(BF16)
        done += start_all([(result.at[:, here], out.at[:, here])], sems, 2 + 2 * t)
    wait_all(done)


def project(ring, mine, other, w_o, w_other):
    queries, depth = mine.shape
    columns = w_other.shape[1]
    tile = columns // 4
    result = shape((queries, columns))
    return call(
        functools.partial(project_kernel, ring, tile),
        result,
        [mine, other, w_o, w_other],
        [room(a) for a in (mine, other, w_other, w_other, mine, other, result)],
        copies=2 + 2 * (columns // tile),
        flops=4 * queries * depth * columns,
        moved=4 * depth * columns,
    )


def add_kernel(start, own, arrays, *refs):
    sources, (out, *held, total, sems) = refs[:arrays], refs[arrays:]
    size = out.shape[0]
    pairs = [(source, keep) for source, keep in zip(sources, held)]
    if own is not None:
        pairs[-1] = (sources[-1].at[pl.ds(own * size, size), :], held[-1])
    wait_all(start_all(pairs, sems))
    some = held[0].shape[0]
    if some == size:
        total[...] = sum(keep[...].astype(F32) for keep in held).astype(BF16)
    else:
        total[...] = held[-1][...]
        part = pl.ds(start, some)
        total[part, :] = (held[0][...].astype(F32) + held[-1][part, :].astype(F32)).astype(BF16)
    wait_all(start_all([(total, out)], sems))


def add(arrays, whole=None, own=None, size=None, start=0):
    size = size or arrays[0].shape[0]
    result = shape((size, arrays[0].shape[1]))
    args = list(arrays) + ([] if whole is None else [whole])
    held = [room(a) for a in arrays] + ([] if whole is None else [room(result)])
    return call(
        functools.partial(add_kernel, start, own, len(args)),
        result,
        args,
        held + [room(result)],
        copies=len(args),
        moved=6 * size * result.shape[1],
        vmem=16,
    )


def ring_sum(rows, n):
    size = rows.shape[0] // n
    far = n // 2
    cut = size // 2
    up = shift(rows[far * size : far * size + cut], "z", 1, n)
    down = shift(rows[far * size + cut : (far + 1) * size], "z", -1, n)
    for d in range(far - 1, 0, -1):
        begin = cut if d == far - 1 else 0
        up = shift(add([up], rows, d, size), "z", 1, n)
        down = shift(add([down], rows, n - d, size, begin), "z", -1, n)
    return add([up, down], rows, 0)


def ring_gather(piece, n):
    far = n // 2
    cut = piece.shape[0] // 2
    found = [(0, 0, piece)]
    up = down = piece
    for d in range(1, far):
        up, down = shift(up, "z", 1, n), shift(down, "z", -1, n)
        found += [(-d, 0, up), (d, 0, down)]
    found.append((far, 0, shift(up[:cut], "z", 1, n)))
    found.append((far, cut, shift(down[cut:], "z", -1, n)))
    return found


def place_kernel(n, where, *refs):
    count = len(where)
    mine, other = refs[:count], refs[count : 2 * count]
    out, sems = refs[2 * count :]
    chunk = out.shape[0] // n
    columns = out.shape[1] // 2
    core, z = lax.axis_index("core"), lax.axis_index("z")
    pairs = []
    for half, arrays in ((core, mine), (1 - core, other)):
        lanes = pl.ds(pl.multiple_of(half * columns, LANES), columns)
        for (d, row), array in zip(where, arrays):
            start = pl.multiple_of((z + d + n) % n * chunk + row, 16)
            pairs.append((array, out.at[pl.ds(start, array.shape[0]), lanes]))
    wait_all(start_all(pairs, sems))


def place_pieces(n, where, mine, other, dims):
    args = [*mine, *other]
    return call(
        functools.partial(place_kernel, n, where),
        shape(dims),
        args,
        copies=len(args),
        moved=4 * dims[0] * dims[1],
        vmem=8,
    )


def shift(x, axes, by, n):
    return lax.ppermute(x, axes, [(i, (i + by) % n) for i in range(n)])


def per_device(sizes, q_nope, q_rope, latent, key_rope, q_pos, k_pos, w_uk, w_uv, w_o):
    heads = w_uk.shape[0]
    queries = q_nope.shape[0]
    keys = latent.shape[0]
    columns = w_o.shape[1] // 2
    swap = lambda a: shift(a, "core", 1, 2)
    ny, nx = sizes["y"], sizes["xl"] * sizes["xh"]
    spot = lambda x: (x % nx % sizes["xl"]) * sizes["xh"] + x % nx // sizes["xl"]
    shift_x = lambda a, by: lax.ppermute(
        a, ("xl", "xh"), [(spot(x), spot(x + by)) for x in range(nx)]
    )

    pack, half = pack_keys(latent, key_rope, k_pos)
    rows = pack.shape[0]
    span = rows // 2
    below = shift(half, "y", 1, ny)
    above = shift(half, "y", -1, ny)
    across = shift_x(half, 1)
    query, w_half = absorb(q_nope, q_rope, w_uk, w_o, half)
    w_other = swap(w_half)
    positions = q_pos.reshape(queries, 1)
    far = shift(below, "y", 1, ny)
    across_below = shift_x(below, 1)
    across_above = shift_x(above, -1)
    cut = span // 2
    def place(*blocks):
        def find(keys, queries):
            xl, y = lax.axis_index("xl"), lax.axis_index("y")
            ids = [
                (1 - xl if over else xl) * ny + (y + d + ny) % ny for over, d in blocks
            ]
            return ids, (sizes["q0"] + (xl * ny + y) * queries) // keys

        return find

    both = [(0, 0, span), (1, 0, span)]
    state = attend(
        [[(2, 0, rows)], both, both, both],
        [pack, below, swap(below), above, swap(above), across, swap(across)],
        place((0, 0), (0, -1), (0, 1), (1, 0)),
        query, positions, None, None, heads, rows,
    )
    far, across_below, across_above, state = lax.optimization_barrier(
        (far, across_below, across_above, state)
    )
    across_far = (shift_x(far[:cut], 1), shift_x(far[cut:], -1))
    state = attend(
        [both, both, both],
        [far, swap(far), across_below, swap(across_below), across_above, swap(across_above)],
        place((0, 2), (1, -1), (1, 1)),
        query, positions, state, None, heads, rows,
    )
    across_far, state = lax.optimization_barrier((across_far, state))
    quarters = [(0, 0, cut), (1, 0, cut), (0, cut, span - cut), (1, cut, span - cut)]
    head_out = attend(
        [quarters],
        [across_far[0], swap(across_far[0]), across_far[1], swap(across_far[1])],
        place((1, 2)),
        query, positions, state, w_uv, heads, rows,
    )
    nz = sizes["z"]
    partial_out = project(nz, head_out, swap(head_out), w_o, w_other)
    piece = ring_sum(partial_out, nz)
    piece = add([piece, shift(piece, "xh", 1, sizes["xh"])])
    found = ring_gather(piece, nz)
    mine = lax.optimization_barrier([array for _, _, array in found])
    where = [(d, row) for d, row, _ in found]
    return place_pieces(nz, where, mine, [swap(a) for a in mine], (queries, 2 * columns))


def solution(mesh):
    sizes = {"xl": 2, "y": 4, "z": 8, "xh": 2, "core": 2, "q0": 2048}
    names = ("xl", "y", "z", "xh", "core")
    fine = Mesh(mesh.devices.reshape([sizes[n] for n in names]), names)
    return jax.shard_map(
        functools.partial(per_device, sizes),
        mesh=fine,
        in_specs=(
            P(SEQ, HEAD),
            P(SEQ, HEAD),
            P(SEQ, None),
            P(SEQ, None),
            P(SEQ),
            P(SEQ),
            P(HEAD, None, None),
            P(HEAD, None, None),
            P(HEAD, None),
        ),
        out_specs=P(SEQ, None),
        check_vma=False,
    )
```

```python
import functools
import math

import jax
import jax.numpy as jnp
from jax import lax
from jax.experimental import pallas as pl
from jax.experimental.pallas import tpu as pltpu
from jax.sharding import Mesh, PartitionSpec as P

F32, BF16, I32 = jnp.float32, jnp.bfloat16, jnp.int32
LOW = -1e30
LANES = 128
SEQ = ("xl", "y")
HEAD = ("z", "xh", "core")


def call(kernel, outs, args, scratch=(), copies=1, flops=0, moved=0, vmem=24):
    anywhere = pl.BlockSpec(memory_space=pl.ANY)
    return pl.pallas_call(
        kernel,
        out_shape=outs,
        in_specs=[anywhere] * len(args),
        out_specs=jax.tree.map(lambda _: anywhere, outs),
        scratch_shapes=list(scratch) + [pltpu.SemaphoreType.DMA((copies,))],
        compiler_params=pltpu.CompilerParams(vmem_limit_bytes=vmem * 2**20),
        cost_estimate=pl.CostEstimate(flops=flops, bytes_accessed=moved, transcendentals=0),
    )(*args)


def start_all(pairs, sems, first=0):
    copies = [
        pltpu.make_async_copy(source, target, sems.at[first + i])
        for i, (source, target) in enumerate(pairs)
    ]
    for copy in copies:
        copy.start()
    return copies


def wait_all(copies):
    for copy in copies:
        copy.wait()


def room(array):
    return pltpu.VMEM(array.shape, array.dtype)


def shape(dims, dtype=BF16):
    return jax.ShapeDtypeStruct(tuple(dims), dtype)


def pack_kernel(latent_in, rope_in, pos_in, pack_out, half_out, latent, rope, pos, pack, sems):
    copies = start_all([(latent_in, latent), (rope_in, rope), (pos_in, pos)], sems)
    keys, width = latent.shape
    pairs, two = rope.shape
    rope_width = two // 2
    token = lax.broadcasted_iota(I32, (keys, pairs), 0)
    pair = lax.broadcasted_iota(I32, (keys, pairs), 1)
    even = (token == 2 * pair).astype(BF16)
    odd = (token == 2 * pair + 1).astype(BF16)
    wait_all(copies)
    order = (lax.broadcasted_iota(I32, (keys, keys), 0) == pos[...] % keys).astype(BF16)
    sorted_latent = jnp.dot(order, latent[...], preferred_element_type=F32)
    spread_even = jnp.dot(even, rope[...], preferred_element_type=F32)
    spread_odd = jnp.dot(odd, rope[...], preferred_element_type=F32)
    rows = jnp.concatenate(
        [spread_even[:, :rope_width], spread_odd[:, rope_width:]], axis=1
    ).astype(BF16)
    ordered = jnp.dot(order, rows, preferred_element_type=F32)
    turned = jnp.transpose(ordered)
    pack[pl.ds(0, keys), :] = sorted_latent.astype(BF16)
    pack[pl.ds(keys, rope_width), :] = (turned[:rope_width] + turned[rope_width:]).astype(BF16)
    span = half_out.shape[0]
    start = pl.multiple_of(lax.axis_index("core") * span, span)
    wait_all(start_all([(pack.at[pl.ds(start, span), :], half_out), (pack, pack_out)], sems))


def pack_keys(latent, key_rope, k_pos):
    keys, width = latent.shape
    rows = keys + key_rope.shape[0] * key_rope.shape[1] // keys
    args = [latent, key_rope, k_pos.reshape(1, keys)]
    return call(
        pack_kernel,
        [shape((rows, width)), shape((rows // 2, width))],
        args,
        [room(a) for a in args] + [pltpu.VMEM((rows, width), BF16)],
        copies=3,
        flops=2 * keys * keys * width,
        moved=3 * keys * width * 2,
        vmem=58,
    )


def query_kernel(scale, q_nope_in, q_rope_in, w_uk_in, w_o, after, out, half, q_nope, q_rope, w_uk, query, sems):
    columns = half.shape[1]
    start = pl.multiple_of((1 - lax.axis_index("core")) * columns, LANES)
    pairs = [(q_nope_in, q_nope), (q_rope_in, q_rope), (w_uk_in, w_uk)]
    copies = start_all(pairs, sems)
    slices = start_all([(w_o.at[:, pl.ds(start, columns)], half)], sems, len(pairs))
    wait_all(copies)
    heads, nope, width = w_uk.shape
    queries = q_nope.shape[0]
    rope = q_rope.shape[1] // heads
    for h in range(heads):
        rows = pl.ds(h * queries, queries)
        absorbed = jnp.dot(
            q_nope[:, h * nope : (h + 1) * nope], w_uk[h], preferred_element_type=F32
        )
        query[rows, pl.ds(0, width)] = (absorbed * scale).astype(BF16)
        rotary = q_rope[:, h * rope : (h + 1) * rope].astype(F32) * scale
        query[rows, pl.ds(width, rope)] = rotary.astype(BF16)
    wait_all(slices + start_all([(query, out)], sems))


def absorb(q_nope, q_rope, w_uk, w_o, after):
    heads, nope, width = w_uk.shape
    queries = q_nope.shape[0]
    rope = q_rope.shape[1] // heads
    scale = math.log2(math.e) / math.sqrt(nope + rope)
    result = shape((heads * queries, width + rope))
    return call(
        functools.partial(query_kernel, scale),
        [result, shape((w_o.shape[0], w_o.shape[1] // 2))],
        [q_nope, q_rope, w_uk, w_o, after],
        [room(a) for a in (q_nope, q_rope, w_uk, result)],
        copies=4,
        flops=2 * queries * heads * nope * width,
        moved=2 * heads * queries * (nope + width) + 2 * w_o.shape[0] * w_o.shape[1],
        vmem=58,
    )


def attend_kernel(layout, first, last, heads, place, *refs):
    pieces = sum(len(block) for block in layout)
    blocks, refs = refs[:pieces], refs[pieces:]
    query_in, positions_in = refs[:2]
    refs = refs[2:]
    if not first:
        old, refs = refs[:3], refs[3:]
    if last:
        w_uv_in, out, refs = refs[0], refs[1], refs[2:]
    else:
        new, refs = refs[:3], refs[3:]
    top, total, acc, keys_in, turned, query, positions, *rest, sems = refs
    state = (top, total, acc)
    count, rows, width = keys_in.shape
    keys = width
    queries = query.shape[0] // heads
    rope = rows - keys
    core = lax.axis_index("core")
    pairs = [(query_in, query), (positions_in, positions)]
    for b, block in enumerate(layout):
        for side, start, size in block:
            offset = start
            if side != 2:
                offset = (core if side == 0 else 1 - core) * (rows // 2) + start
                offset = pl.multiple_of(offset, 16)
            pairs.append((blocks[len(pairs) - 2], keys_in.at[b, pl.ds(offset, size), :]))
    if not first:
        pairs += list(zip(old, state))
    if last:
        w_uv, result = rest
        pairs.append((w_uv_in, w_uv))
    copies = start_all(pairs, sems)
    if first:
        top[...] = jnp.full_like(top, LOW)
        total[...] = jnp.zeros_like(total)
        acc[...] = jnp.zeros_like(acc)
    ids, diagonal = place(keys, queries)
    wait_all(copies)

    def work(b, masked):
        latents = keys_in[b, pl.ds(0, keys), :]
        turned[pl.ds(0, width), :] = jnp.transpose(latents)
        turned[pl.ds(width, rope), :] = keys_in[b, pl.ds(keys, rope), :]
        for h in range(heads):
            part = pl.ds(h * queries, queries)
            scores = jnp.dot(query[part, :], turned[...], preferred_element_type=F32)
            if masked:
                limit = positions[...] - diagonal * keys
                where = lax.broadcasted_iota(I32, (queries, keys), 1)
                scores = jnp.where(where <= limit, scores, LOW)
            before = top[part, :]
            now = jnp.maximum(before, jnp.max(scores, axis=1, keepdims=True))
            factor = jnp.exp2(before - now)
            wide = jnp.concatenate([now] * (keys // LANES), axis=1)
            exps = jnp.exp2(scores - wide)
            sums = exps[:, :LANES]
            for t in range(1, keys // LANES):
                sums = sums + exps[:, t * LANES : (t + 1) * LANES]
            top[part, :] = now
            total[part, :] = total[part, :] * factor + sums
            stretch = jnp.concatenate([factor] * (width // LANES), axis=1)
            acc[part, :] = acc[part, :] * stretch + jnp.dot(
                exps.astype(BF16), latents, preferred_element_type=F32
            )

    def step(b, unused):
        block_id = ids[0]
        for at in range(1, count):
            block_id = jnp.where(b == at, ids[at], block_id)

        @pl.when(block_id < diagonal)
        def _():
            work(b, False)

        @pl.when(block_id == diagonal)
        def _():
            work(b, True)

        return unused

    lax.fori_loop(0, count, step, 0)
    if last:
        for h in range(heads):
            part = pl.ds(h * queries, queries)
            sums = jnp.sum(total[part, :], axis=1, keepdims=True)
            context = (acc[part, :] / sums).astype(BF16)
            value = w_uv.shape[2]
            result[:, pl.ds(h * value, value)] = jnp.dot(
                context, w_uv[h], preferred_element_type=F32
            ).astype(BF16)
        wait_all(start_all([(result, out)], sems))
    else:
        wait_all(start_all(list(zip(state, new)), sems))


def attend(layout, pieces, place, query, positions, state, w_uv, heads, rows):
    width = pieces[0].shape[1]
    total_rows = query.shape[0]
    queries = total_rows // heads
    first, last = state is None, w_uv is not None
    stats = [
        shape((total_rows, LANES), F32),
        shape((total_rows, LANES), F32),
        shape((total_rows, width), F32),
    ]
    args = [*pieces, query, positions]
    if not first:
        args += list(state)
    scratch = [room(s) for s in stats] + [
        pltpu.VMEM((len(layout), rows, width), BF16),
        pltpu.VMEM((query.shape[1], width), BF16),
        room(query),
        room(positions),
    ]
    outs = stats
    if last:
        args.append(w_uv)
        outs = shape((queries, heads * w_uv.shape[2]))
        scratch += [room(w_uv), room(outs)]
    return call(
        functools.partial(attend_kernel, layout, first, last, heads, place),
        outs,
        args,
        scratch,
        copies=len(args),
        flops=16 * total_rows * width * width * len(layout),
        moved=2 * total_rows * width * 4,
    )


def project_kernel(ring, tile, mine_in, other_in, w_o, w_other, out, mine, other, w_a, w_b, left, right, result, sems):
    queries, depth = mine.shape
    columns = out.shape[1]
    tiles = columns // tile
    chunk = queries // ring
    inputs = start_all([(mine_in, mine), (other_in, other)], sems)
    base = lax.axis_index("core") * columns
    weights = []
    for t in range(tiles):
        here = pl.ds(t * tile, tile)
        there = pl.ds(pl.multiple_of(base + t * tile, LANES), tile)
        weights.append(
            start_all(
                [(w_o.at[:, there], w_a.at[:, here]), (w_other.at[:, here], w_b.at[:, here])],
                sems,
                2 + 2 * t,
            )
        )
    wait_all(inputs)
    z = lax.axis_index("z")
    for d in range(ring):
        source = pl.ds(pl.multiple_of((z + d) % ring * chunk, chunk), chunk)
        left[pl.ds(d * chunk, chunk), :] = mine[source, :]
        right[pl.ds(d * chunk, chunk), :] = other[source, :]
    done = []
    for t in range(tiles):
        here = pl.ds(t * tile, tile)
        wait_all(weights[t])
        result[:, here] = (
            jnp.dot(left[...], w_a[:, here], preferred_element_type=F32)
            + jnp.dot(right[...], w_b[:, here], preferred_element_type=F32)
        ).astype(BF16)
        done += start_all([(result.at[:, here], out.at[:, here])], sems, 2 + 2 * t)
    wait_all(done)


def project(ring, mine, other, w_o, w_other):
    queries, depth = mine.shape
    columns = w_other.shape[1]
    tile = columns // 4
    result = shape((queries, columns))
    return call(
        functools.partial(project_kernel, ring, tile),
        result,
        [mine, other, w_o, w_other],
        [room(a) for a in (mine, other, w_other, w_other, mine, other, result)],
        copies=2 + 2 * (columns // tile),
        flops=4 * queries * depth * columns,
        moved=4 * depth * columns,
    )


def add_kernel(terms, *refs):
    sources, outs = refs[: len(refs) - len(terms)], refs[len(refs) - len(terms) :]
    for out, term in zip(outs, terms):
        whole = [sources[i] for i, _ in term if sources[i].shape[0] == out.shape[0]]
        total = sum(source[...].astype(F32) for source in whole)
        out[...] = total.astype(BF16)
        for i, start in term:
            some = sources[i].shape[0]
            if some != out.shape[0]:
                part = pl.ds(start, some)
                rest = sum(source[part, :].astype(F32) for source in whole)
                out[part, :] = (rest + sources[i][...].astype(F32)).astype(BF16)


def add(arrays, terms, whole=None, blocks=(), size=None):
    size = size or arrays[0].shape[0]
    width = arrays[0].shape[1]
    specs = [pl.BlockSpec(a.shape, lambda i: (0, 0)) for a in arrays]
    specs += [pl.BlockSpec((size, width), functools.partial(lambda k, i: (k, 0), k)) for k in blocks]
    return pl.pallas_call(
        functools.partial(add_kernel, terms),
        out_shape=[shape((size, width))] * len(terms),
        grid=(1,),
        in_specs=specs,
        out_specs=[pl.BlockSpec((size, width), lambda i: (0, 0))] * len(terms),
        compiler_params=pltpu.CompilerParams(vmem_limit_bytes=16 * 2**20),
        cost_estimate=pl.CostEstimate(flops=0, bytes_accessed=6 * size * width, transcendentals=0),
    )(*arrays, *[whole] * len(blocks))


def ring_sum(rows, n):
    size = rows.shape[0] // n
    far = n // 2
    cut = size // 2
    up = shift(rows[far * size : far * size + cut], "z", 1, n)
    down = shift(rows[far * size + cut : (far + 1) * size], "z", -1, n)
    for d in range(far - 1, 0, -1):
        begin = cut if d == far - 1 else 0
        terms = [[(2, 0), (0, 0)], [(3, 0), (1, begin)]]
        up, down = add([up, down], terms, rows, (d, n - d), size)
        up, down = shift(up, "z", 1, n), shift(down, "z", -1, n)
    return add([up, down], [[(0, 0), (1, 0), (2, 0)]], rows, (0,))[0]


def ring_gather(piece, n):
    far = n // 2
    cut = piece.shape[0] // 2
    found = [(0, 0, piece)]
    up = down = piece
    for d in range(1, far):
        up, down = shift(up, "z", 1, n), shift(down, "z", -1, n)
        found += [(-d, 0, up), (d, 0, down)]
    found.append((far, 0, shift(up[:cut], "z", 1, n)))
    found.append((far, cut, shift(down[cut:], "z", -1, n)))
    return found


def place_kernel(n, where, *refs):
    count = len(where)
    mine, other = refs[:count], refs[count : 2 * count]
    out, sems = refs[2 * count :]
    chunk = out.shape[0] // n
    columns = out.shape[1] // 2
    core, z = lax.axis_index("core"), lax.axis_index("z")
    pairs = []
    for half, arrays in ((core, mine), (1 - core, other)):
        lanes = pl.ds(pl.multiple_of(half * columns, LANES), columns)
        for (d, row), array in zip(where, arrays):
            start = pl.multiple_of((z + d + n) % n * chunk + row, 16)
            pairs.append((array, out.at[pl.ds(start, array.shape[0]), lanes]))
    wait_all(start_all(pairs, sems))


def place_pieces(n, where, mine, other, dims):
    args = [*mine, *other]
    return call(
        functools.partial(place_kernel, n, where),
        shape(dims),
        args,
        copies=len(args),
        moved=4 * dims[0] * dims[1],
        vmem=8,
    )


def shift(x, axes, by, n):
    return lax.ppermute(x, axes, [(i, (i + by) % n) for i in range(n)])


def per_device(sizes, q_nope, q_rope, latent, key_rope, q_pos, k_pos, w_uk, w_uv, w_o):
    heads = w_uk.shape[0]
    queries = q_nope.shape[0]
    keys = latent.shape[0]
    columns = w_o.shape[1] // 2
    swap = lambda a: shift(a, "core", 1, 2)
    ny, nx = sizes["y"], sizes["xl"] * sizes["xh"]
    spot = lambda x: (x % nx % sizes["xl"]) * sizes["xh"] + x % nx // sizes["xl"]
    shift_x = lambda a, by: lax.ppermute(
        a, ("xl", "xh"), [(spot(x), spot(x + by)) for x in range(nx)]
    )

    spot_xy = lambda x, y: (spot(x) // sizes["xh"] * ny + y % ny) * sizes["xh"] + spot(x) % sizes["xh"]
    shift_xy = lambda a, by_x, by_y: lax.ppermute(
        a,
        ("xl", "y", "xh"),
        [(spot_xy(x, y), spot_xy(x + by_x, y + by_y)) for x in range(nx) for y in range(ny)],
    )

    pack, half = pack_keys(latent, key_rope, k_pos)
    rows = pack.shape[0]
    span = rows // 2
    below = shift(half, "y", 1, ny)
    above = shift(half, "y", -1, ny)
    across = shift_x(half, 1)
    query, w_half = absorb(q_nope, q_rope, w_uk, w_o, half)
    positions = q_pos.reshape(queries, 1)
    below, above, across, query, w_half = lax.optimization_barrier(
        (below, above, across, query, w_half)
    )
    across_below = shift_x(below, 1)
    across_above = shift_x(above, -1)
    near = [below, above, across]
    swapped, below, above = lax.optimization_barrier(([swap(a) for a in near], below, above))
    far = shift(below, "y", 1, ny)
    cut = span // 2
    across_far = (
        shift_xy(above[:cut], 1, -1),
        shift_xy(below[cut:], -1, 1),
    )

    def place(*blocks):
        def find(keys, queries):
            xl, y = lax.axis_index("xl"), lax.axis_index("y")
            ids = [
                (1 - xl if over else xl) * ny + (y + d + ny) % ny for over, d in blocks
            ]
            return ids, (sizes["q0"] + (xl * ny + y) * queries) // keys

        return find

    both = [(0, 0, span), (1, 0, span)]
    state = attend(
        [[(2, 0, rows)], both, both, both],
        [pack] + [a for pair in zip(near, swapped) for a in pair],
        place((0, 0), (0, -1), (0, 1), (1, 0)),
        query, positions, None, None, heads, rows,
    )
    later, state = lax.optimization_barrier(
        ([far, across_below, across_above, *across_far], state)
    )
    swapped, w_half = lax.optimization_barrier(([swap(a) for a in later], w_half))
    w_other = swap(w_half)
    quarters = [(0, 0, cut), (1, 0, cut), (0, cut, span - cut), (1, cut, span - cut)]
    head_out = attend(
        [both, both, both, quarters],
        [a for pair in zip(later, swapped) for a in pair],
        place((0, 2), (1, -1), (1, 1), (1, 2)),
        query, positions, state, w_uv, heads, rows,
    )
    nz = sizes["z"]
    partial_out = project(nz, head_out, swap(head_out), w_o, w_other)
    piece = ring_sum(partial_out, nz)
    piece = add([piece, shift(piece, "xh", 1, sizes["xh"])], [[(0, 0), (1, 0)]])[0]
    found = ring_gather(piece, nz)
    mine = lax.optimization_barrier([array for _, _, array in found])
    where = [(d, row) for d, row, _ in found]
    return place_pieces(nz, where, mine, [swap(a) for a in mine], (queries, 2 * columns))


def solution(mesh):
    sizes = {"xl": 2, "y": 4, "z": 8, "xh": 2, "core": 2, "q0": 2048}
    names = ("xl", "y", "z", "xh", "core")
    fine = Mesh(mesh.devices.reshape([sizes[n] for n in names]), names)
    return jax.shard_map(
        functools.partial(per_device, sizes),
        mesh=fine,
        in_specs=(
            P(SEQ, HEAD),
            P(SEQ, HEAD),
            P(SEQ, None),
            P(SEQ, None),
            P(SEQ),
            P(SEQ),
            P(HEAD, None, None),
            P(HEAD, None, None),
            P(HEAD, None),
        ),
        out_specs=P(SEQ, None),
        check_vma=False,
    )
```

```python
import functools
import math

import jax
import jax.numpy as jnp
from jax import lax
from jax.experimental import pallas as pl
from jax.experimental.pallas import tpu as pltpu
from jax.sharding import Mesh, PartitionSpec as P

F32, BF16, I32 = jnp.float32, jnp.bfloat16, jnp.int32
LOW = -1e30
LANES = 128
SEQ = ("xl", "y")
HEAD = ("z", "xh", "core")


def call(kernel, outs, args, scratch=(), copies=1, flops=0, moved=0, vmem=24):
    anywhere = pl.BlockSpec(memory_space=pl.ANY)
    return pl.pallas_call(
        kernel,
        out_shape=outs,
        in_specs=[anywhere] * len(args),
        out_specs=jax.tree.map(lambda _: anywhere, outs),
        scratch_shapes=list(scratch) + [pltpu.SemaphoreType.DMA((copies,))],
        compiler_params=pltpu.CompilerParams(vmem_limit_bytes=vmem * 2**20),
        cost_estimate=pl.CostEstimate(flops=flops, bytes_accessed=moved, transcendentals=0),
    )(*args)


def start_all(pairs, sems, first=0):
    copies = [
        pltpu.make_async_copy(source, target, sems.at[first + i])
        for i, (source, target) in enumerate(pairs)
    ]
    for copy in copies:
        copy.start()
    return copies


def wait_all(copies):
    for copy in copies:
        copy.wait()


def room(array):
    return pltpu.VMEM(array.shape, array.dtype)


def shape(dims, dtype=BF16):
    return jax.ShapeDtypeStruct(tuple(dims), dtype)


def pack_kernel(latent_in, rope_in, pos_in, pack_out, half_out, latent, rope, pos, pack, sems):
    copies = start_all([(latent_in, latent), (rope_in, rope), (pos_in, pos)], sems)
    keys, width = latent.shape
    pairs, two = rope.shape
    rope_width = two // 2
    token = lax.broadcasted_iota(I32, (keys, pairs), 0)
    pair = lax.broadcasted_iota(I32, (keys, pairs), 1)
    even = (token == 2 * pair).astype(BF16)
    odd = (token == 2 * pair + 1).astype(BF16)
    wait_all(copies)
    order = (lax.broadcasted_iota(I32, (keys, keys), 0) == pos[...] % keys).astype(BF16)
    sorted_latent = jnp.dot(order, latent[...], preferred_element_type=F32)
    spread_even = jnp.dot(even, rope[...], preferred_element_type=F32)
    spread_odd = jnp.dot(odd, rope[...], preferred_element_type=F32)
    rows = jnp.concatenate(
        [spread_even[:, :rope_width], spread_odd[:, rope_width:]], axis=1
    ).astype(BF16)
    ordered = jnp.dot(order, rows, preferred_element_type=F32)
    turned = jnp.transpose(ordered)
    pack[pl.ds(0, keys), :] = sorted_latent.astype(BF16)
    pack[pl.ds(keys, rope_width), :] = (turned[:rope_width] + turned[rope_width:]).astype(BF16)
    span = half_out.shape[0]
    start = pl.multiple_of(lax.axis_index("core") * span, span)
    wait_all(start_all([(pack.at[pl.ds(start, span), :], half_out), (pack, pack_out)], sems))


def pack_keys(latent, key_rope, k_pos):
    keys, width = latent.shape
    rows = keys + key_rope.shape[0] * key_rope.shape[1] // keys
    args = [latent, key_rope, k_pos.reshape(1, keys)]
    return call(
        pack_kernel,
        [shape((rows, width)), shape((rows // 2, width))],
        args,
        [room(a) for a in args] + [pltpu.VMEM((rows, width), BF16)],
        copies=3,
        flops=2 * keys * keys * width,
        moved=3 * keys * width * 2,
        vmem=58,
    )


def query_kernel(
    scale, q_nope_in, q_rope_in, w_uk_in, w_o, after, out, half, q_nope, q_rope, w_uk, query, held, sems
):
    columns = half.shape[1]
    start = pl.multiple_of((1 - lax.axis_index("core")) * columns, LANES)
    pairs = [(q_nope_in, q_nope), (q_rope_in, q_rope), (w_uk_in, w_uk)]
    copies = start_all(pairs, sems)
    slices = start_all([(w_o.at[:, pl.ds(start, columns)], held)], sems, len(pairs))
    wait_all(copies)
    heads, nope, width = w_uk.shape
    queries = q_nope.shape[0]
    rope = q_rope.shape[1] // heads
    for h in range(heads):
        rows = pl.ds(h * queries, queries)
        absorbed = jnp.dot(
            q_nope[:, h * nope : (h + 1) * nope], w_uk[h], preferred_element_type=F32
        )
        query[rows, pl.ds(0, width)] = (absorbed * scale).astype(BF16)
        rotary = q_rope[:, h * rope : (h + 1) * rope].astype(F32) * scale
        query[rows, pl.ds(width, rope)] = rotary.astype(BF16)
    wait_all(slices)
    wait_all(start_all([(query, out), (held, half)], sems))


def absorb(q_nope, q_rope, w_uk, w_o, after):
    heads, nope, width = w_uk.shape
    queries = q_nope.shape[0]
    rope = q_rope.shape[1] // heads
    scale = math.log2(math.e) / math.sqrt(nope + rope)
    result = shape((heads * queries, width + rope))
    half = shape((w_o.shape[0], w_o.shape[1] // 2))
    return call(
        functools.partial(query_kernel, scale),
        [result, half],
        [q_nope, q_rope, w_uk, w_o, after],
        [room(a) for a in (q_nope, q_rope, w_uk, result, half)],
        copies=4,
        flops=2 * queries * heads * nope * width,
        moved=2 * heads * queries * (nope + width) + 2 * w_o.shape[0] * w_o.shape[1],
        vmem=58,
    )


def attend_kernel(layout, first, last, heads, place, *refs):
    pieces = sum(len(block) for block in layout)
    blocks, refs = refs[:pieces], refs[pieces:]
    query_in, positions_in = refs[:2]
    refs = refs[2:]
    if not first:
        old, refs = refs[:3], refs[3:]
    if last:
        w_uv_in, out, refs = refs[0], refs[1], refs[2:]
    else:
        new, refs = refs[:3], refs[3:]
    top, total, acc, keys_in, turned, query, positions, *rest, sems = refs
    state = (top, total, acc)
    count, rows, width = keys_in.shape
    keys = width
    queries = query.shape[0] // heads
    rope = rows - keys
    core = lax.axis_index("core")
    pairs = [(query_in, query), (positions_in, positions)]
    for b, block in enumerate(layout):
        for side, start, size in block:
            offset = start
            if side != 2:
                offset = (core if side == 0 else 1 - core) * (rows // 2) + start
                offset = pl.multiple_of(offset, 16)
            pairs.append((blocks[len(pairs) - 2], keys_in.at[b, pl.ds(offset, size), :]))
    if not first:
        pairs += list(zip(old, state))
    if last:
        w_uv, result = rest
        pairs.append((w_uv_in, w_uv))
    copies = start_all(pairs, sems)
    if first:
        top[...] = jnp.full_like(top, LOW)
        total[...] = jnp.zeros_like(total)
        acc[...] = jnp.zeros_like(acc)
    ids, diagonal = place(keys, queries)
    wait_all(copies)

    def work(b, masked):
        latents = keys_in[b, pl.ds(0, keys), :]
        turned[pl.ds(0, width), :] = jnp.transpose(latents)
        turned[pl.ds(width, rope), :] = keys_in[b, pl.ds(keys, rope), :]
        for h in range(heads):
            part = pl.ds(h * queries, queries)
            scores = jnp.dot(query[part, :], turned[...], preferred_element_type=F32)
            if masked:
                limit = positions[...] - diagonal * keys
                where = lax.broadcasted_iota(I32, (queries, keys), 1)
                scores = jnp.where(where <= limit, scores, LOW)
            before = top[part, :]
            now = jnp.maximum(before, jnp.max(scores, axis=1, keepdims=True))
            factor = jnp.exp2(before - now)
            wide = jnp.concatenate([now] * (keys // LANES), axis=1)
            exps = jnp.exp2(scores - wide)
            sums = exps[:, :LANES]
            for t in range(1, keys // LANES):
                sums = sums + exps[:, t * LANES : (t + 1) * LANES]
            top[part, :] = now
            total[part, :] = total[part, :] * factor + sums
            stretch = jnp.concatenate([factor] * (width // LANES), axis=1)
            acc[part, :] = acc[part, :] * stretch + jnp.dot(
                exps.astype(BF16), latents, preferred_element_type=F32
            )

    def step(b, unused):
        block_id = ids[0]
        for at in range(1, count):
            block_id = jnp.where(b == at, ids[at], block_id)

        @pl.when(block_id < diagonal)
        def _():
            work(b, False)

        @pl.when(block_id == diagonal)
        def _():
            work(b, True)

        return unused

    lax.fori_loop(0, count, step, 0)
    if last:
        for h in range(heads):
            part = pl.ds(h * queries, queries)
            sums = jnp.sum(total[part, :], axis=1, keepdims=True)
            context = (acc[part, :] / sums).astype(BF16)
            value = w_uv.shape[2]
            result[:, pl.ds(h * value, value)] = jnp.dot(
                context, w_uv[h], preferred_element_type=F32
            ).astype(BF16)
        wait_all(start_all([(result, out)], sems))
    else:
        wait_all(start_all(list(zip(state, new)), sems))


def attend(layout, pieces, place, query, positions, state, w_uv, heads, rows):
    width = pieces[0].shape[1]
    total_rows = query.shape[0]
    queries = total_rows // heads
    first, last = state is None, w_uv is not None
    stats = [
        shape((total_rows, LANES), F32),
        shape((total_rows, LANES), F32),
        shape((total_rows, width), F32),
    ]
    args = [*pieces, query, positions]
    if not first:
        args += list(state)
    scratch = [room(s) for s in stats] + [
        pltpu.VMEM((len(layout), rows, width), BF16),
        pltpu.VMEM((query.shape[1], width), BF16),
        room(query),
        room(positions),
    ]
    outs = stats
    if last:
        args.append(w_uv)
        outs = shape((queries, heads * w_uv.shape[2]))
        scratch += [room(w_uv), room(outs)]
    return call(
        functools.partial(attend_kernel, layout, first, last, heads, place),
        outs,
        args,
        scratch,
        copies=len(args),
        flops=16 * total_rows * width * width * len(layout),
        moved=2 * total_rows * width * 4,
    )


def project_kernel(ring, tile, mine_in, other_in, w_o, w_other, out, mine, other, w_a, w_b, left, right, result, sems):
    queries, depth = mine.shape
    columns = out.shape[1]
    tiles = columns // tile
    chunk = queries // ring
    inputs = start_all([(mine_in, mine), (other_in, other)], sems)
    base = lax.axis_index("core") * columns
    weights = []
    for t in range(tiles):
        here = pl.ds(t * tile, tile)
        there = pl.ds(pl.multiple_of(base + t * tile, LANES), tile)
        weights.append(
            start_all(
                [(w_o.at[:, there], w_a.at[:, here]), (w_other.at[:, here], w_b.at[:, here])],
                sems,
                2 + 2 * t,
            )
        )
    wait_all(inputs)
    z = lax.axis_index("z")
    for d in range(ring):
        source = pl.ds(pl.multiple_of((z + d) % ring * chunk, chunk), chunk)
        left[pl.ds(d * chunk, chunk), :] = mine[source, :]
        right[pl.ds(d * chunk, chunk), :] = other[source, :]
    done = []
    for t in range(tiles):
        here = pl.ds(t * tile, tile)
        wait_all(weights[t])
        result[:, here] = (
            jnp.dot(left[...], w_a[:, here], preferred_element_type=F32)
            + jnp.dot(right[...], w_b[:, here], preferred_element_type=F32)
        ).astype(BF16)
        done += start_all([(result.at[:, here], out.at[:, here])], sems, 2 + 2 * t)
    wait_all(done)


def project(ring, mine, other, w_o, w_other):
    queries, depth = mine.shape
    columns = w_other.shape[1]
    tile = columns // 4
    result = shape((queries, columns))
    return call(
        functools.partial(project_kernel, ring, tile),
        result,
        [mine, other, w_o, w_other],
        [room(a) for a in (mine, other, w_other, w_other, mine, other, result)],
        copies=2 + 2 * (columns // tile),
        flops=4 * queries * depth * columns,
        moved=4 * depth * columns,
    )


def small_call(kernel, outs, arrays, whole=None, blocks=()):
    plain = lambda a: pl.BlockSpec(a.shape, lambda i: (0, 0))
    specs = [plain(a) for a in arrays]
    for block, size in blocks:
        specs.append(
            pl.BlockSpec((size, whole.shape[1]), functools.partial(lambda k, i: (k, 0), block))
        )
    moved = 2 * sum(math.prod(a.shape) for a in [*arrays, *outs])
    return pl.pallas_call(
        kernel,
        out_shape=outs,
        grid=(1,),
        in_specs=specs,
        out_specs=[plain(a) for a in outs],
        compiler_params=pltpu.CompilerParams(vmem_limit_bytes=16 * 2**20),
        cost_estimate=pl.CostEstimate(flops=0, bytes_accessed=moved, transcendentals=0),
    )(*arrays, *[whole] * len(blocks))


def wide(ref):
    return ref[...].astype(F32)


def sides(columns):
    half, xh = columns // 2, lax.axis_index("xh")
    return tuple(pl.ds(pl.multiple_of(k * half, LANES), half) for k in (xh, 1 - xh))


def sum_far_kernel(up, up_half, down, down_half, own, own_up, own_down, out_up, out_down, cross):
    cut = up_half.shape[0]
    for out, near, far, mine, first in (
        (out_up, up, up_half, own_up, True),
        (out_down, down, down_half, own_down, False),
    ):
        total = wide(near) + wide(mine)
        low, high = total[:cut], total[cut:]
        out[pl.ds(0, cut), :] = (low + wide(far) if first else low).astype(BF16)
        out[pl.ds(cut, cut), :] = (high if first else high + wide(far)).astype(BF16)
    cross[...] = own[:, sides(own.shape[1])[1]]


def sum_near_kernel(up, down, own_up, own_down, up_keep, up_cross, down_keep, down_cross):
    keep, cross = sides(up.shape[1])
    for source, mine, kept, crossed in (
        (up, own_up, up_keep, up_cross),
        (down, own_down, down_keep, down_cross),
    ):
        for out, lanes in ((kept, keep), (crossed, cross)):
            out[...] = (source[:, lanes].astype(F32) + mine[:, lanes].astype(F32)).astype(BF16)


def sum_last_kernel(*refs):
    *parts, own, out = refs
    total = own[:, sides(own.shape[1])[0]].astype(F32)
    for part in parts:
        total = total + wide(part)
    out[...] = total.astype(BF16)


def over(a, by, n, cross=False):
    return lax.ppermute(
        a,
        ("z", "xh"),
        [(z * 2 + x, (z + by) % n * 2 + (1 - x if cross else x)) for z in range(n) for x in (0, 1)],
    )


def ring_sum(rows, n):
    size, columns = rows.shape[0] // n, rows.shape[1]
    cut = size // 2
    chunk = lambda d: rows[d * size : (d + 1) * size]
    up, down = over(chunk(3), 1, n), over(chunk(5), -1, n)
    up_half = over(chunk(4)[:cut], 2, n)
    down_half = over(chunk(4)[cut:], -2, n)
    whole, half = shape((size, columns)), shape((size, columns // 2))
    up, down, cross = small_call(
        sum_far_kernel,
        [whole, whole, half],
        [up, up_half, down, down_half],
        rows,
        [(0, size), (2, size), (6, size)],
    )
    up, down, cross = over(up, 1, n), over(down, -1, n), over(cross, 0, n, True)
    up, up_cross, down, down_cross = small_call(
        sum_near_kernel, [half] * 4, [up, down], rows, [(1, size), (7, size)]
    )
    parts = [
        cross,
        over(up, 1, n),
        over(down, -1, n),
        over(up_cross, 1, n, True),
        over(down_cross, -1, n, True),
    ]
    return small_call(sum_last_kernel, [half], parts, rows, [(0, size)])[0]


def join_kernel(*refs):
    sources, outs = refs[: len(refs) * 2 // 3], refs[len(refs) * 2 // 3 :]
    keep, cross = sides(outs[0].shape[1])
    for i, out in enumerate(outs):
        out[:, keep] = sources[2 * i][...]
        out[:, cross] = sources[2 * i + 1][...]


def ring_gather(piece, n):
    cut = piece.shape[0] // 2
    halves = [
        over(piece, 1, n),
        over(piece, 1, n, True),
        over(piece, -1, n),
        over(piece, -1, n, True),
        piece,
        over(piece, 0, n, True),
    ]
    whole = shape((piece.shape[0], 2 * piece.shape[1]))
    up, down, own = small_call(join_kernel, [whole] * 3, halves)
    found = [(0, 0, own), (-1, 0, up), (1, 0, down)]
    up, down = over(up, 1, n), over(down, -1, n)
    found += [(-2, 0, up), (2, 0, down)]
    found += [(-3, 0, over(up, 1, n)), (3, 0, over(down, -1, n))]
    found += [(4, 0, over(up[:cut], 2, n)), (4, cut, over(down[cut:], -2, n))]
    return found


def place_kernel(n, where, *refs):
    count = len(where)
    mine, other = refs[:count], refs[count : 2 * count]
    out, sems = refs[2 * count :]
    chunk = out.shape[0] // n
    columns = out.shape[1] // 2
    core, z = lax.axis_index("core"), lax.axis_index("z")
    pairs = []
    for half, arrays in ((core, mine), (1 - core, other)):
        lanes = pl.ds(pl.multiple_of(half * columns, LANES), columns)
        for (d, row), array in zip(where, arrays):
            start = pl.multiple_of((z + d + n) % n * chunk + row, 16)
            pairs.append((array, out.at[pl.ds(start, array.shape[0]), lanes]))
    wait_all(start_all(pairs, sems))


def place_pieces(n, where, mine, other, dims):
    args = [*mine, *other]
    return call(
        functools.partial(place_kernel, n, where),
        shape(dims),
        args,
        copies=len(args),
        moved=4 * dims[0] * dims[1],
        vmem=8,
    )


def shift(x, axes, by, n):
    return lax.ppermute(x, axes, [(i, (i + by) % n) for i in range(n)])


def per_device(sizes, q_nope, q_rope, latent, key_rope, q_pos, k_pos, w_uk, w_uv, w_o):
    heads = w_uk.shape[0]
    queries = q_nope.shape[0]
    keys = latent.shape[0]
    columns = w_o.shape[1] // 2
    swap = lambda a: shift(a, "core", 1, 2)
    ny, nx = sizes["y"], sizes["xl"] * sizes["xh"]
    spot = lambda x: (x % nx % sizes["xl"]) * sizes["xh"] + x % nx // sizes["xl"]
    shift_x = lambda a, by: lax.ppermute(
        a, ("xl", "xh"), [(spot(x), spot(x + by)) for x in range(nx)]
    )

    spot_xy = lambda x, y: (spot(x) // sizes["xh"] * ny + y % ny) * sizes["xh"] + spot(x) % sizes["xh"]
    shift_xy = lambda a, by_x, by_y: lax.ppermute(
        a,
        ("xl", "y", "xh"),
        [(spot_xy(x, y), spot_xy(x + by_x, y + by_y)) for x in range(nx) for y in range(ny)],
    )

    pack, half = pack_keys(latent, key_rope, k_pos)
    rows = pack.shape[0]
    span = rows // 2
    below = shift(half, "y", 1, ny)
    above = shift(half, "y", -1, ny)
    across = shift_x(half, 1)
    query, w_half = absorb(q_nope, q_rope, w_uk, w_o, half)
    positions = q_pos.reshape(queries, 1)
    below, above, across, query, w_half = lax.optimization_barrier(
        (below, above, across, query, w_half)
    )
    across_below = shift_x(below, 1)
    across_above = shift_x(above, -1)
    near = [below, above, across]
    swapped, below, above = lax.optimization_barrier(([swap(a) for a in near], below, above))
    far = shift(below, "y", 1, ny)
    cut = span // 2
    across_far = (
        shift_xy(above[:cut], 1, -1),
        shift_xy(below[cut:], -1, 1),
    )

    def place(*blocks):
        def find(keys, queries):
            xl, y = lax.axis_index("xl"), lax.axis_index("y")
            ids = [
                (1 - xl if over else xl) * ny + (y + d + ny) % ny for over, d in blocks
            ]
            return ids, (sizes["q0"] + (xl * ny + y) * queries) // keys

        return find

    both = [(0, 0, span), (1, 0, span)]
    state = attend(
        [[(2, 0, rows)], both, both, both],
        [pack] + [a for pair in zip(near, swapped) for a in pair],
        place((0, 0), (0, -1), (0, 1), (1, 0)),
        query, positions, None, None, heads, rows,
    )
    later, state = lax.optimization_barrier(
        ([far, across_below, across_above, *across_far], state)
    )
    swapped, w_half = lax.optimization_barrier(([swap(a) for a in later], w_half))
    w_other = swap(w_half)
    quarters = [(0, 0, cut), (1, 0, cut), (0, cut, span - cut), (1, cut, span - cut)]
    head_out = attend(
        [both, both, both, quarters],
        [a for pair in zip(later, swapped) for a in pair],
        place((0, 2), (1, -1), (1, 1), (1, 2)),
        query, positions, state, w_uv, heads, rows,
    )
    nz = sizes["z"]
    partial_out = project(nz, head_out, swap(head_out), w_o, w_other)
    piece = ring_sum(partial_out, nz)
    found = ring_gather(piece, nz)
    mine = lax.optimization_barrier([array for _, _, array in found])
    where = [(d, row) for d, row, _ in found]
    return place_pieces(nz, where, mine, [swap(a) for a in mine], (queries, 2 * columns))


def solution(mesh):
    sizes = {"xl": 2, "y": 4, "z": 8, "xh": 2, "core": 2, "q0": 2048}
    names = ("xl", "y", "z", "xh", "core")
    fine = Mesh(mesh.devices.reshape([sizes[n] for n in names]), names)
    return jax.shard_map(
        functools.partial(per_device, sizes),
        mesh=fine,
        in_specs=(
            P(SEQ, HEAD),
            P(SEQ, HEAD),
            P(SEQ, None),
            P(SEQ, None),
            P(SEQ),
            P(SEQ),
            P(HEAD, None, None),
            P(HEAD, None, None),
            P(HEAD, None),
        ),
        out_specs=P(SEQ, None),
        check_vma=False,
    )
```

```python
import functools
import math

import jax
import jax.numpy as jnp
from jax import lax
from jax.experimental import pallas as pl
from jax.experimental.pallas import tpu as pltpu
from jax.sharding import Mesh, PartitionSpec as P

F32, BF16, I32 = jnp.float32, jnp.bfloat16, jnp.int32
LOW = -1e30
LANES = 128
SEQ = ("xl", "y")
HEAD = ("z", "xh", "core")


def call(kernel, outs, args, scratch=(), copies=1, flops=0, moved=0, vmem=24):
    anywhere = pl.BlockSpec(memory_space=pl.ANY)
    return pl.pallas_call(
        kernel,
        out_shape=outs,
        in_specs=[anywhere] * len(args),
        out_specs=jax.tree.map(lambda _: anywhere, outs),
        scratch_shapes=list(scratch) + [pltpu.SemaphoreType.DMA((copies,))],
        compiler_params=pltpu.CompilerParams(vmem_limit_bytes=vmem * 2**20),
        cost_estimate=pl.CostEstimate(flops=flops, bytes_accessed=moved, transcendentals=0),
    )(*args)


def start_all(pairs, sems, first=0):
    copies = [
        pltpu.make_async_copy(source, target, sems.at[first + i])
        for i, (source, target) in enumerate(pairs)
    ]
    for copy in copies:
        copy.start()
    return copies


def wait_all(copies):
    for copy in copies:
        copy.wait()


def room(array):
    return pltpu.VMEM(array.shape, array.dtype)


def shape(dims, dtype=BF16):
    return jax.ShapeDtypeStruct(tuple(dims), dtype)


def pack_kernel(latent_in, rope_in, pos_in, pack_out, half_out, latent, rope, pos, pack, sems):
    copies = start_all([(latent_in, latent), (rope_in, rope), (pos_in, pos)], sems)
    keys, width = latent.shape
    pairs, two = rope.shape
    rope_width = two // 2
    token = lax.broadcasted_iota(I32, (keys, pairs), 0)
    pair = lax.broadcasted_iota(I32, (keys, pairs), 1)
    even = (token == 2 * pair).astype(BF16)
    odd = (token == 2 * pair + 1).astype(BF16)
    wait_all(copies)
    order = (lax.broadcasted_iota(I32, (keys, keys), 0) == pos[...] % keys).astype(BF16)
    sorted_latent = jnp.dot(order, latent[...], preferred_element_type=F32)
    spread_even = jnp.dot(even, rope[...], preferred_element_type=F32)
    spread_odd = jnp.dot(odd, rope[...], preferred_element_type=F32)
    rows = jnp.concatenate(
        [spread_even[:, :rope_width], spread_odd[:, rope_width:]], axis=1
    ).astype(BF16)
    ordered = jnp.dot(order, rows, preferred_element_type=F32)
    turned = jnp.transpose(ordered)
    pack[pl.ds(0, keys), :] = sorted_latent.astype(BF16)
    pack[pl.ds(keys, rope_width), :] = (turned[:rope_width] + turned[rope_width:]).astype(BF16)
    span = half_out.shape[0]
    start = pl.multiple_of(lax.axis_index("core") * span, span)
    wait_all(start_all([(pack.at[pl.ds(start, span), :], half_out), (pack, pack_out)], sems))


def pack_keys(latent, key_rope, k_pos):
    keys, width = latent.shape
    rows = keys + key_rope.shape[0] * key_rope.shape[1] // keys
    args = [latent, key_rope, k_pos.reshape(1, keys)]
    return call(
        pack_kernel,
        [shape((rows, width)), shape((rows // 2, width))],
        args,
        [room(a) for a in args] + [pltpu.VMEM((rows, width), BF16)],
        copies=3,
        flops=2 * keys * keys * width,
        moved=3 * keys * width * 2,
        vmem=58,
    )


def query_kernel(
    scale, q_nope_in, q_rope_in, w_uk_in, w_o, after, out, half, q_nope, q_rope, w_uk, query, held, sems
):
    columns = half.shape[1]
    start = pl.multiple_of((1 - lax.axis_index("core")) * columns, LANES)
    pairs = [(q_nope_in, q_nope), (q_rope_in, q_rope), (w_uk_in, w_uk)]
    copies = start_all(pairs, sems)
    slices = start_all([(w_o.at[:, pl.ds(start, columns)], held)], sems, len(pairs))
    wait_all(copies)
    heads, nope, width = w_uk.shape
    queries = q_nope.shape[0]
    rope = q_rope.shape[1] // heads
    for h in range(heads):
        rows = pl.ds(h * queries, queries)
        absorbed = jnp.dot(
            q_nope[:, h * nope : (h + 1) * nope], w_uk[h], preferred_element_type=F32
        )
        query[rows, pl.ds(0, width)] = (absorbed * scale).astype(BF16)
        rotary = q_rope[:, h * rope : (h + 1) * rope].astype(F32) * scale
        query[rows, pl.ds(width, rope)] = rotary.astype(BF16)
    wait_all(slices)
    wait_all(start_all([(query, out), (held, half)], sems))


def absorb(q_nope, q_rope, w_uk, w_o, after):
    heads, nope, width = w_uk.shape
    queries = q_nope.shape[0]
    rope = q_rope.shape[1] // heads
    scale = math.log2(math.e) / math.sqrt(nope + rope)
    result = shape((heads * queries, width + rope))
    half = shape((w_o.shape[0], w_o.shape[1] // 2))
    return call(
        functools.partial(query_kernel, scale),
        [result, half],
        [q_nope, q_rope, w_uk, w_o, after],
        [room(a) for a in (q_nope, q_rope, w_uk, result, half)],
        copies=4,
        flops=2 * queries * heads * nope * width,
        moved=2 * heads * queries * (nope + width) + 2 * w_o.shape[0] * w_o.shape[1],
        vmem=58,
    )


def attend_kernel(layout, first, last, heads, place, *refs):
    pieces = sum(len(block) for block in layout)
    blocks, refs = refs[:pieces], refs[pieces:]
    query_in, positions_in = refs[:2]
    refs = refs[2:]
    if not first:
        old, refs = refs[:3], refs[3:]
    if last:
        w_uv_in, out, refs = refs[0], refs[1], refs[2:]
    else:
        new, refs = refs[:3], refs[3:]
    top, total, acc, keys_in, turned, query, positions, *rest, sems = refs
    state = (top, total, acc)
    count, rows, width = keys_in.shape
    keys = width
    queries = query.shape[0] // heads
    rope = rows - keys
    core = lax.axis_index("core")
    pairs = [(query_in, query), (positions_in, positions)]
    for b, block in enumerate(layout):
        for side, start, size in block:
            offset = start
            if side != 2:
                offset = (core if side == 0 else 1 - core) * (rows // 2) + start
                offset = pl.multiple_of(offset, 16)
            pairs.append((blocks[len(pairs) - 2], keys_in.at[b, pl.ds(offset, size), :]))
    if not first:
        pairs += list(zip(old, state))
    if last:
        w_uv, result = rest
        pairs.append((w_uv_in, w_uv))
    copies = start_all(pairs, sems)
    if first:
        top[...] = jnp.full_like(top, LOW)
        total[...] = jnp.zeros_like(total)
        acc[...] = jnp.zeros_like(acc)
    ids, diagonal = place(keys, queries)
    wait_all(copies)

    def work(b, masked):
        latents = keys_in[b, pl.ds(0, keys), :]
        turned[pl.ds(0, width), :] = jnp.transpose(latents)
        turned[pl.ds(width, rope), :] = keys_in[b, pl.ds(keys, rope), :]
        for h in range(heads):
            part = pl.ds(h * queries, queries)
            scores = jnp.dot(query[part, :], turned[...], preferred_element_type=F32)
            if masked:
                limit = positions[...] - diagonal * keys
                where = lax.broadcasted_iota(I32, (queries, keys), 1)
                scores = jnp.where(where <= limit, scores, LOW)
            before = top[part, :]
            now = jnp.maximum(before, jnp.max(scores, axis=1, keepdims=True))
            factor = jnp.exp2(before - now)
            wide = jnp.concatenate([now] * (keys // LANES), axis=1)
            exps = jnp.exp2(scores - wide)
            sums = exps[:, :LANES]
            for t in range(1, keys // LANES):
                sums = sums + exps[:, t * LANES : (t + 1) * LANES]
            top[part, :] = now
            total[part, :] = total[part, :] * factor + sums
            stretch = jnp.concatenate([factor] * (width // LANES), axis=1)
            acc[part, :] = acc[part, :] * stretch + jnp.dot(
                exps.astype(BF16), latents, preferred_element_type=F32
            )

    def step(b, unused):
        block_id = ids[0]
        for at in range(1, count):
            block_id = jnp.where(b == at, ids[at], block_id)

        @pl.when(block_id < diagonal)
        def _():
            work(b, False)

        @pl.when(block_id == diagonal)
        def _():
            work(b, True)

        return unused

    lax.fori_loop(0, count, step, 0)
    if last:
        for h in range(heads):
            part = pl.ds(h * queries, queries)
            sums = jnp.sum(total[part, :], axis=1, keepdims=True)
            context = (acc[part, :] / sums).astype(BF16)
            value = w_uv.shape[2]
            result[:, pl.ds(h * value, value)] = jnp.dot(
                context, w_uv[h], preferred_element_type=F32
            ).astype(BF16)
        wait_all(start_all([(result, out)], sems))
    else:
        wait_all(start_all(list(zip(state, new)), sems))


def attend(layout, pieces, place, query, positions, state, w_uv, heads, rows):
    width = pieces[0].shape[1]
    total_rows = query.shape[0]
    queries = total_rows // heads
    first, last = state is None, w_uv is not None
    stats = [
        shape((total_rows, LANES), F32),
        shape((total_rows, LANES), F32),
        shape((total_rows, width), F32),
    ]
    args = [*pieces, query, positions]
    if not first:
        args += list(state)
    scratch = [room(s) for s in stats] + [
        pltpu.VMEM((len(layout), rows, width), BF16),
        pltpu.VMEM((query.shape[1], width), BF16),
        room(query),
        room(positions),
    ]
    outs = stats
    if last:
        args.append(w_uv)
        outs = shape((queries, heads * w_uv.shape[2]))
        scratch += [room(w_uv), room(outs)]
    return call(
        functools.partial(attend_kernel, layout, first, last, heads, place),
        outs,
        args,
        scratch,
        copies=len(args),
        flops=16 * total_rows * width * width * len(layout),
        moved=2 * total_rows * width * 4,
    )


def project_kernel(order, cross, mine_in, other_in, w_o, w_other, *refs):
    outs, (mine, other, w_a, w_b, left, right, result, sems) = refs[:-8], refs[-8:]
    queries, depth = mine.shape
    columns = result.shape[1]
    tiles = 2
    tile = columns // tiles
    chunk = queries // len(order)
    inputs = start_all([(mine_in, mine), (other_in, other)], sems)
    xh = lax.axis_index("xh")
    base = (1 - xh if cross else xh) * columns
    start = lax.axis_index("core") * w_other.shape[1] + base
    weights = []
    for t in range(tiles):
        here = pl.ds(t * tile, tile)
        pairs = [
            (w_o.at[:, pl.ds(pl.multiple_of(start + t * tile, LANES), tile)], w_a.at[:, here]),
            (w_other.at[:, pl.ds(pl.multiple_of(base + t * tile, LANES), tile)], w_b.at[:, here]),
        ]
        weights.append(start_all(pairs, sems, 2 + 2 * t))
    wait_all(inputs)
    z = lax.axis_index("z")
    for i, d in enumerate(order):
        source = pl.ds(pl.multiple_of((z + d) % len(order) * chunk, chunk), chunk)
        left[pl.ds(i * chunk, chunk), :] = mine[source, :]
        right[pl.ds(i * chunk, chunk), :] = other[source, :]
    for t in range(tiles):
        here = pl.ds(t * tile, tile)
        wait_all(weights[t])
        result[:, here] = (
            jnp.dot(left[...], w_a[:, here], preferred_element_type=F32)
            + jnp.dot(right[...], w_b[:, here], preferred_element_type=F32)
        ).astype(BF16)
    pairs, row = [], 0
    for out in outs:
        pairs.append((result.at[pl.ds(row, out.shape[0]), :], out))
        row += out.shape[0]
    wait_all(start_all(pairs, sems))


def project(order, cross, sizes, mine, other, w_o, w_other):
    queries, depth = mine.shape
    columns = w_other.shape[1] // 2
    result = shape((queries, columns))
    weight = shape((depth, columns))
    return call(
        functools.partial(project_kernel, order, cross),
        [shape((size, columns)) for size in sizes],
        [mine, other, w_o, w_other],
        [room(a) for a in (mine, other, weight, weight, mine, other, result)],
        copies=6,
        flops=4 * queries * depth * columns,
        moved=4 * depth * columns,
    )


def small_call(kernel, outs, args):
    specs, arrays = [], []
    for arg in args:
        array, block, size = arg if isinstance(arg, tuple) else (arg, 0, arg.shape[0])
        arrays.append(array)
        specs.append(
            pl.BlockSpec((size, array.shape[1]), functools.partial(lambda k, i: (k, 0), block))
        )
    moved = 4 * sum(math.prod(a.shape) for a in outs)
    return pl.pallas_call(
        kernel,
        out_shape=outs,
        grid=(1,),
        in_specs=specs,
        out_specs=[pl.BlockSpec(a.shape, lambda i: (0, 0)) for a in outs],
        compiler_params=pltpu.CompilerParams(vmem_limit_bytes=16 * 2**20),
        cost_estimate=pl.CostEstimate(flops=0, bytes_accessed=moved, transcendentals=0),
    )(*arrays)


def wide(ref):
    return ref[...].astype(F32)


def split_kernel(one, two, up, down):
    total = (wide(one) + wide(two)).astype(BF16)
    up[...] = total[: up.shape[0]]
    down[...] = total[up.shape[0] :]


def pair_kernel(up, down, up_one, up_two, down_one, down_two, out_up, out_down):
    for out, moving, one, two, top in (
        (out_up, up, up_one, up_two, True),
        (out_down, down, down_one, down_two, False),
    ):
        total = wide(one) + wide(two)
        size, some = out.shape[0], moving.shape[0]
        if some == size:
            out[...] = (total + wide(moving)).astype(BF16)
        else:
            low, high = total[:some], total[some:]
            out[pl.ds(0, some), :] = (low + wide(moving) if top else low).astype(BF16)
            out[pl.ds(some, some), :] = (high if top else high + wide(moving)).astype(BF16)


def last_kernel(up, down, one, two, out):
    out[...] = (wide(one) + wide(two) + wide(up) + wide(down)).astype(BF16)


ORDER = (3, 4, 5, 6, 7, 0, 1, 2)
EARLY = 3


def ring_sum(own, early, late, n):
    size = own.shape[0] // n
    whole, part = shape((size, own.shape[1])), shape((size // 2, own.shape[1]))

    def both(d):
        at = ORDER.index(d)
        return [
            (own, at, size),
            (early, at, size) if at < EARLY else (late, at - EARLY, size),
        ]

    far = n // 2
    up, down = small_call(split_kernel, [part] * 2, both(far))
    up, down = shift(up, "z", 1, n), shift(down, "z", -1, n)
    for d in range(far - 1, 0, -1):
        up, down = small_call(pair_kernel, [whole] * 2, [up, down, *both(d), *both(n - d)])
        up, down = shift(up, "z", 1, n), shift(down, "z", -1, n)
    return small_call(last_kernel, [whole], [up, down, *both(0)])[0]


def join_kernel(mine, other, out):
    half, xh = mine.shape[1], lax.axis_index("xh")
    out[:, pl.ds(pl.multiple_of(xh * half, LANES), half)] = mine[...]
    out[:, pl.ds(pl.multiple_of((1 - xh) * half, LANES), half)] = other[...]


def ring_gather(piece, n):
    whole = shape((piece.shape[0], 2 * piece.shape[1]))
    piece = small_call(join_kernel, [whole], [piece, shift(piece, "xh", 1, 2)])[0]
    far = n // 2
    cut = piece.shape[0] // 2
    found = [(0, 0, piece)]
    up = down = piece
    for d in range(1, far):
        up, down = lax.optimization_barrier((shift(up, "z", 1, n), shift(down, "z", -1, n)))
        found += [(-d, 0, up), (d, 0, down)]
    found.append((far, 0, shift(up[:cut], "z", 1, n)))
    found.append((far, cut, shift(down[cut:], "z", -1, n)))
    return found


def place_kernel(n, where, *refs):
    count = len(where)
    mine, other = refs[:count], refs[count : 2 * count]
    out, sems = refs[2 * count :]
    chunk = out.shape[0] // n
    columns = out.shape[1] // 2
    core, z = lax.axis_index("core"), lax.axis_index("z")
    pairs = []
    for half, arrays in ((core, mine), (1 - core, other)):
        lanes = pl.ds(pl.multiple_of(half * columns, LANES), columns)
        for (d, row), array in zip(where, arrays):
            start = pl.multiple_of((z + d + n) % n * chunk + row, 16)
            pairs.append((array, out.at[pl.ds(start, array.shape[0]), lanes]))
    wait_all(start_all(pairs, sems))


def place_pieces(n, where, mine, other, dims):
    args = [*mine, *other]
    return call(
        functools.partial(place_kernel, n, where),
        shape(dims),
        args,
        copies=len(args),
        moved=4 * dims[0] * dims[1],
        vmem=8,
    )


def shift(x, axes, by, n):
    return lax.ppermute(x, axes, [(i, (i + by) % n) for i in range(n)])


def per_device(sizes, q_nope, q_rope, latent, key_rope, q_pos, k_pos, w_uk, w_uv, w_o):
    heads = w_uk.shape[0]
    queries = q_nope.shape[0]
    keys = latent.shape[0]
    columns = w_o.shape[1] // 2
    swap = lambda a: shift(a, "core", 1, 2)
    ny, nx = sizes["y"], sizes["xl"] * sizes["xh"]
    spot = lambda x: (x % nx % sizes["xl"]) * sizes["xh"] + x % nx // sizes["xl"]
    shift_x = lambda a, by: lax.ppermute(
        a, ("xl", "xh"), [(spot(x), spot(x + by)) for x in range(nx)]
    )

    spot_xy = lambda x, y: (spot(x) // sizes["xh"] * ny + y % ny) * sizes["xh"] + spot(x) % sizes["xh"]
    shift_xy = lambda a, by_x, by_y: lax.ppermute(
        a,
        ("xl", "y", "xh"),
        [(spot_xy(x, y), spot_xy(x + by_x, y + by_y)) for x in range(nx) for y in range(ny)],
    )

    pack, half = pack_keys(latent, key_rope, k_pos)
    rows = pack.shape[0]
    span = rows // 2
    below = shift(half, "y", 1, ny)
    above = shift(half, "y", -1, ny)
    across = shift_x(half, 1)
    query, w_half = absorb(q_nope, q_rope, w_uk, w_o, half)
    positions = q_pos.reshape(queries, 1)
    below, above, across, query, w_half = lax.optimization_barrier(
        (below, above, across, query, w_half)
    )
    across_below = shift_x(below, 1)
    across_above = shift_x(above, -1)
    near = [below, above, across]
    swapped, below, above = lax.optimization_barrier(([swap(a) for a in near], below, above))
    far = shift(below, "y", 1, ny)
    cut = span // 2
    across_far = (
        shift_xy(above[:cut], 1, -1),
        shift_xy(below[cut:], -1, 1),
    )

    def place(*blocks):
        def find(keys, queries):
            xl, y = lax.axis_index("xl"), lax.axis_index("y")
            ids = [
                (1 - xl if over else xl) * ny + (y + d + ny) % ny for over, d in blocks
            ]
            return ids, (sizes["q0"] + (xl * ny + y) * queries) // keys

        return find

    both = [(0, 0, span), (1, 0, span)]
    state = attend(
        [[(2, 0, rows)], both, both, both],
        [pack] + [a for pair in zip(near, swapped) for a in pair],
        place((0, 0), (0, -1), (0, 1), (1, 0)),
        query, positions, None, None, heads, rows,
    )
    later, state = lax.optimization_barrier(
        ([far, across_below, across_above, *across_far], state)
    )
    swapped, w_half = lax.optimization_barrier(([swap(a) for a in later], w_half))
    w_other = swap(w_half)
    quarters = [(0, 0, cut), (1, 0, cut), (0, cut, span - cut), (1, cut, span - cut)]
    head_out = attend(
        [both, both, both, quarters],
        [a for pair in zip(later, swapped) for a in pair],
        place((0, 2), (1, -1), (1, 1), (1, 2)),
        query, positions, state, w_uv, heads, rows,
    )
    nz = sizes["z"]
    other = swap(head_out)
    chunk = queries // nz
    early, late = project(
        ORDER, True, [EARLY * chunk, queries - EARLY * chunk], head_out, other, w_o, w_other
    )
    early = shift(early, "xh", 1, 2)
    own = project(ORDER, False, [queries], head_out, other, w_o, w_other)[0]
    late, own = lax.optimization_barrier((late, own))
    late = shift(late, "xh", 1, 2)
    piece = ring_sum(own, early, late, nz)
    found = ring_gather(piece, nz)
    mine = lax.optimization_barrier([array for _, _, array in found])
    where = [(d, row) for d, row, _ in found]
    return place_pieces(nz, where, mine, [swap(a) for a in mine], (queries, 2 * columns))


def solution(mesh):
    sizes = {"xl": 2, "y": 4, "z": 8, "xh": 2, "core": 2, "q0": 2048}
    names = ("xl", "y", "z", "xh", "core")
    fine = Mesh(mesh.devices.reshape([sizes[n] for n in names]), names)
    return jax.shard_map(
        functools.partial(per_device, sizes),
        mesh=fine,
        in_specs=(
            P(SEQ, HEAD),
            P(SEQ, HEAD),
            P(SEQ, None),
            P(SEQ, None),
            P(SEQ),
            P(SEQ),
            P(HEAD, None, None),
            P(HEAD, None, None),
            P(HEAD, None),
        ),
        out_specs=P(SEQ, None),
        check_vma=False,
    )
```

```python
import functools
import math

import jax
import jax.numpy as jnp
from jax import lax
from jax.experimental import pallas as pl
from jax.experimental.pallas import tpu as pltpu
from jax.sharding import Mesh, PartitionSpec as P

F32, BF16, I32 = jnp.float32, jnp.bfloat16, jnp.int32
LOW = -1e30
LANES = 128
SEQ = ("xl", "y")
HEAD = ("z", "xh", "core")


def call(kernel, outs, args, scratch=(), copies=1, flops=0, moved=0, vmem=24):
    anywhere = pl.BlockSpec(memory_space=pl.ANY)
    return pl.pallas_call(
        kernel,
        out_shape=outs,
        in_specs=[anywhere] * len(args),
        out_specs=jax.tree.map(lambda _: anywhere, outs),
        scratch_shapes=list(scratch) + [pltpu.SemaphoreType.DMA((copies,))],
        compiler_params=pltpu.CompilerParams(vmem_limit_bytes=vmem * 2**20),
        cost_estimate=pl.CostEstimate(flops=flops, bytes_accessed=moved, transcendentals=0),
    )(*args)


def start_all(pairs, sems, first=0):
    copies = [
        pltpu.make_async_copy(source, target, sems.at[first + i])
        for i, (source, target) in enumerate(pairs)
    ]
    for copy in copies:
        copy.start()
    return copies


def wait_all(copies):
    for copy in copies:
        copy.wait()


def room(array):
    return pltpu.VMEM(array.shape, array.dtype)


def shape(dims, dtype=BF16):
    return jax.ShapeDtypeStruct(tuple(dims), dtype)


def pack_kernel(latent_in, rope_in, pos_in, pack_out, half_out, latent, rope, pos, pack, sems):
    copies = start_all([(latent_in, latent), (rope_in, rope), (pos_in, pos)], sems)
    keys, width = latent.shape
    pairs, two = rope.shape
    rope_width = two // 2
    token = lax.broadcasted_iota(I32, (keys, pairs), 0)
    pair = lax.broadcasted_iota(I32, (keys, pairs), 1)
    even = (token == 2 * pair).astype(BF16)
    odd = (token == 2 * pair + 1).astype(BF16)
    wait_all(copies)
    order = (lax.broadcasted_iota(I32, (keys, keys), 0) == pos[...] % keys).astype(BF16)
    sorted_latent = jnp.dot(order, latent[...], preferred_element_type=F32)
    spread_even = jnp.dot(even, rope[...], preferred_element_type=F32)
    spread_odd = jnp.dot(odd, rope[...], preferred_element_type=F32)
    rows = jnp.concatenate(
        [spread_even[:, :rope_width], spread_odd[:, rope_width:]], axis=1
    ).astype(BF16)
    ordered = jnp.dot(order, rows, preferred_element_type=F32)
    turned = jnp.transpose(ordered)
    pack[pl.ds(0, keys), :] = sorted_latent.astype(BF16)
    pack[pl.ds(keys, rope_width), :] = (turned[:rope_width] + turned[rope_width:]).astype(BF16)
    span = half_out.shape[0]
    start = pl.multiple_of(lax.axis_index("core") * span, span)
    wait_all(start_all([(pack.at[pl.ds(start, span), :], half_out), (pack, pack_out)], sems))


def pack_keys(latent, key_rope, k_pos):
    keys, width = latent.shape
    rows = keys + key_rope.shape[0] * key_rope.shape[1] // keys
    args = [latent, key_rope, k_pos.reshape(1, keys)]
    return call(
        pack_kernel,
        [shape((rows, width)), shape((rows // 2, width))],
        args,
        [room(a) for a in args] + [pltpu.VMEM((rows, width), BF16)],
        copies=3,
        flops=2 * keys * keys * width,
        moved=3 * keys * width * 2,
        vmem=58,
    )


def query_kernel(
    scale, q_nope_in, q_rope_in, w_uk_in, w_o, after, out, half, q_nope, q_rope, w_uk, query, held, sems
):
    columns = half.shape[1]
    start = pl.multiple_of((1 - lax.axis_index("core")) * columns, LANES)
    pairs = [(q_nope_in, q_nope), (q_rope_in, q_rope), (w_uk_in, w_uk)]
    copies = start_all(pairs, sems)
    slices = start_all([(w_o.at[:, pl.ds(start, columns)], held)], sems, len(pairs))
    wait_all(copies)
    heads, nope, width = w_uk.shape
    queries = q_nope.shape[0]
    rope = q_rope.shape[1] // heads
    for h in range(heads):
        rows = pl.ds(h * queries, queries)
        absorbed = jnp.dot(
            q_nope[:, h * nope : (h + 1) * nope], w_uk[h], preferred_element_type=F32
        )
        query[rows, pl.ds(0, width)] = (absorbed * scale).astype(BF16)
        rotary = q_rope[:, h * rope : (h + 1) * rope].astype(F32) * scale
        query[rows, pl.ds(width, rope)] = rotary.astype(BF16)
    wait_all(slices)
    wait_all(start_all([(query, out), (held, half)], sems))


def absorb(q_nope, q_rope, w_uk, w_o, after):
    heads, nope, width = w_uk.shape
    queries = q_nope.shape[0]
    rope = q_rope.shape[1] // heads
    scale = math.log2(math.e) / math.sqrt(nope + rope)
    result = shape((heads * queries, width + rope))
    half = shape((w_o.shape[0], w_o.shape[1] // 2))
    return call(
        functools.partial(query_kernel, scale),
        [result, half],
        [q_nope, q_rope, w_uk, w_o, after],
        [room(a) for a in (q_nope, q_rope, w_uk, result, half)],
        copies=4,
        flops=2 * queries * heads * nope * width,
        moved=2 * heads * queries * (nope + width) + 2 * w_o.shape[0] * w_o.shape[1],
        vmem=58,
    )


def attend_kernel(layout, first, last, heads, place, *refs):
    pieces = sum(len(block) for block in layout)
    blocks, refs = refs[:pieces], refs[pieces:]
    query_in, positions_in = refs[:2]
    refs = refs[2:]
    if not first:
        old, refs = refs[:3], refs[3:]
    if last:
        w_uv_in, out, refs = refs[0], refs[1], refs[2:]
    else:
        new, refs = refs[:3], refs[3:]
    top, total, acc, keys_in, query, positions, *rest, sems = refs
    state = (top, total, acc)
    count, rows, width = keys_in.shape
    keys = width
    queries = query.shape[0] // heads
    rope = rows - keys
    core = lax.axis_index("core")
    pairs = [(query_in, query), (positions_in, positions)]
    for b, block in enumerate(layout):
        for side, start, size in block:
            offset = start
            if side != 2:
                offset = (core if side == 0 else 1 - core) * (rows // 2) + start
                offset = pl.multiple_of(offset, 16)
            pairs.append((blocks[len(pairs) - 2], keys_in.at[b, pl.ds(offset, size), :]))
    if not first:
        pairs += list(zip(old, state))
    if last:
        w_uv, result = rest
        pairs.append((w_uv_in, w_uv))
    copies = start_all(pairs, sems)
    if first:
        top[...] = jnp.full_like(top, LOW)
        total[...] = jnp.zeros_like(total)
        acc[...] = jnp.zeros_like(acc)
    ids, diagonal = place(keys, queries)
    wait_all(copies)

    def work(b, masked):
        latents = keys_in[b, pl.ds(0, keys), :]
        def score(h):
            part = pl.ds(h * queries, queries)
            return lax.dot_general(
                query[part, pl.ds(0, width)], latents, (((1,), (1,)), ((), ())), preferred_element_type=F32
            ) + jnp.dot(query[part, pl.ds(width, rope)], keys_in[b, pl.ds(keys, rope), :], preferred_element_type=F32)

        def soften(h, scores):
            part = pl.ds(h * queries, queries)
            if masked:
                limit = positions[...] - diagonal * keys
                where = lax.broadcasted_iota(I32, (queries, keys), 1)
                scores = jnp.where(where <= limit, scores, LOW)
            before = top[part, :]
            now = jnp.maximum(before, jnp.max(scores, axis=1, keepdims=True))
            factor = jnp.exp2(before - now)
            wide = jnp.concatenate([now] * (keys // LANES), axis=1)
            exps = jnp.exp2(scores - wide)
            sums = exps[:, :LANES]
            for t in range(1, keys // LANES):
                sums = sums + exps[:, t * LANES : (t + 1) * LANES]
            top[part, :] = now
            total[part, :] = total[part, :] * factor + sums
            return exps.astype(BF16), factor

        def gather(h, probs, factor):
            part = pl.ds(h * queries, queries)
            stretch = jnp.concatenate([factor] * (width // LANES), axis=1)
            acc[part, :] = acc[part, :] * stretch + jnp.dot(
                probs, latents, preferred_element_type=F32
            )

        scores = score(0)
        for h in range(heads):
            following = score(h + 1) if h + 1 < heads else None
            gather(h, *soften(h, scores))
            scores = following

    def step(b, unused):
        block_id = ids[b]

        @pl.when(block_id < diagonal)
        def _():
            work(b, False)

        @pl.when(block_id == diagonal)
        def _():
            work(b, True)

        return unused

    for b in range(count):
        step(b, 0)
    if last:
        for h in range(heads):
            part = pl.ds(h * queries, queries)
            sums = jnp.sum(total[part, :], axis=1, keepdims=True)
            context = (acc[part, :] / sums).astype(BF16)
            value = w_uv.shape[2]
            result[:, pl.ds(h * value, value)] = jnp.dot(
                context, w_uv[h], preferred_element_type=F32
            ).astype(BF16)
        wait_all(start_all([(result, out)], sems))
    else:
        wait_all(start_all(list(zip(state, new)), sems))


def attend(layout, pieces, place, query, positions, state, w_uv, heads, rows):
    width = pieces[0].shape[1]
    total_rows = query.shape[0]
    queries = total_rows // heads
    first, last = state is None, w_uv is not None
    stats = [
        shape((total_rows, LANES), F32),
        shape((total_rows, LANES), F32),
        shape((total_rows, width), F32),
    ]
    args = [*pieces, query, positions]
    if not first:
        args += list(state)
    scratch = [room(s) for s in stats] + [
        pltpu.VMEM((len(layout), rows, width), BF16),
        room(query),
        room(positions),
    ]
    outs = stats
    if last:
        args.append(w_uv)
        outs = shape((queries, heads * w_uv.shape[2]))
        scratch += [room(w_uv), room(outs)]
    return call(
        functools.partial(attend_kernel, layout, first, last, heads, place),
        outs,
        args,
        scratch,
        copies=len(args),
        flops=16 * total_rows * width * width * len(layout),
        moved=2 * total_rows * width * 4,
    )


def project_kernel(ring, tile, mine_in, other_in, w_o, w_other, out, mine, other, w_a, w_b, left, right, result, sems):
    queries, depth = mine.shape
    columns = out.shape[1]
    tiles = columns // tile
    chunk = queries // ring
    inputs = start_all([(mine_in, mine), (other_in, other)], sems)
    base = lax.axis_index("core") * columns
    weights = []
    for t in range(tiles):
        here = pl.ds(t * tile, tile)
        there = pl.ds(pl.multiple_of(base + t * tile, LANES), tile)
        weights.append(
            start_all(
                [(w_o.at[:, there], w_a.at[:, here]), (w_other.at[:, here], w_b.at[:, here])],
                sems,
                2 + 2 * t,
            )
        )
    wait_all(inputs)
    z = lax.axis_index("z")
    for d in range(ring):
        source = pl.ds(pl.multiple_of((z + d) % ring * chunk, chunk), chunk)
        left[pl.ds(d * chunk, chunk), :] = mine[source, :]
        right[pl.ds(d * chunk, chunk), :] = other[source, :]
    done = []
    for t in range(tiles):
        here = pl.ds(t * tile, tile)
        wait_all(weights[t])
        result[:, here] = (
            jnp.dot(left[...], w_a[:, here], preferred_element_type=F32)
            + jnp.dot(right[...], w_b[:, here], preferred_element_type=F32)
        ).astype(BF16)
        done += start_all([(result.at[:, here], out.at[:, here])], sems, 2 + 2 * t)
    wait_all(done)


def project(ring, mine, other, w_o, w_other):
    queries, depth = mine.shape
    columns = w_other.shape[1]
    tile = columns // 4
    result = shape((queries, columns))
    return call(
        functools.partial(project_kernel, ring, tile),
        result,
        [mine, other, w_o, w_other],
        [room(a) for a in (mine, other, w_other, w_other, mine, other, result)],
        copies=2 + 2 * (columns // tile),
        flops=4 * queries * depth * columns,
        moved=4 * depth * columns,
    )


def small_call(kernel, outs, args):
    specs, arrays = [], []
    for arg in args:
        array, block, size = arg if isinstance(arg, tuple) else (arg, 0, arg.shape[0])
        arrays.append(array)
        specs.append(
            pl.BlockSpec((size, array.shape[1]), functools.partial(lambda k, i: (k, 0), block))
        )
    moved = 4 * sum(math.prod(a.shape) for a in outs)
    return pl.pallas_call(
        kernel,
        out_shape=outs,
        grid=(1,),
        in_specs=specs,
        out_specs=[pl.BlockSpec(a.shape, lambda i: (0, 0)) for a in outs],
        compiler_params=pltpu.CompilerParams(vmem_limit_bytes=16 * 2**20),
        cost_estimate=pl.CostEstimate(flops=0, bytes_accessed=moved, transcendentals=0),
    )(*arrays)


def wide(ref):
    return ref[...].astype(F32)


def pair_kernel(up, down, own_up, own_down, out_up, out_down):
    for out, moving, own, top in ((out_up, up, own_up, True), (out_down, down, own_down, False)):
        size, some = out.shape[0], moving.shape[0]
        if some == size:
            out[...] = (wide(own) + wide(moving)).astype(BF16)
        else:
            met = pl.ds(0 if top else some, some)
            out[...] = own[...]
            out[met, :] = (own[met, :].astype(F32) + wide(moving)).astype(BF16)


def sum_kernel(*refs):
    *parts, out = refs
    out[...] = sum(wide(part) for part in parts).astype(BF16)


def ring_sum(rows, n):
    size = rows.shape[0] // n
    whole = shape((size, rows.shape[1]))
    far, cut = n // 2, size // 2
    up = shift(rows[far * size : far * size + cut], "z", 1, n)
    down = shift(rows[far * size + cut : (far + 1) * size], "z", -1, n)
    for d in range(far - 1, 0, -1):
        args = [up, down, (rows, d, size), (rows, n - d, size)]
        up, down = small_call(pair_kernel, [whole] * 2, args)
        up, down = shift(up, "z", 1, n), shift(down, "z", -1, n)
    return small_call(sum_kernel, [whole], [up, down, (rows, 0, size)])[0]


def ring_gather(piece, n):
    far = n // 2
    cut = piece.shape[0] // 2
    found = [(0, 0, piece)]
    up = down = piece
    for d in range(1, far - 1):
        up, down = lax.optimization_barrier((shift(up, "z", 1, n), shift(down, "z", -1, n)))
        found += [(-d, 0, up), (d, 0, down)]
    found += [(1 - far, 0, shift(up, "z", 1, n)), (far - 1, 0, shift(down, "z", -1, n))]
    found.append((far, 0, shift(up[:cut], "z", 2, n)))
    found.append((far, cut, shift(down[cut:], "z", -2, n)))
    return found


def place_kernel(n, where, *refs):
    count = len(where)
    mine, other = refs[:count], refs[count : 2 * count]
    out, sems = refs[2 * count :]
    chunk = out.shape[0] // n
    columns = out.shape[1] // 2
    core, z = lax.axis_index("core"), lax.axis_index("z")
    pairs = []
    for half, arrays in ((core, mine), (1 - core, other)):
        lanes = pl.ds(pl.multiple_of(half * columns, LANES), columns)
        for (d, row), array in zip(where, arrays):
            start = pl.multiple_of((z + d + n) % n * chunk + row, 16)
            pairs.append((array, out.at[pl.ds(start, array.shape[0]), lanes]))
    wait_all(start_all(pairs, sems))


def place_pieces(n, where, mine, other, dims):
    args = [*mine, *other]
    return call(
        functools.partial(place_kernel, n, where),
        shape(dims),
        args,
        copies=len(args),
        moved=4 * dims[0] * dims[1],
        vmem=8,
    )


def shift(x, axes, by, n):
    return lax.ppermute(x, axes, [(i, (i + by) % n) for i in range(n)])


def per_device(sizes, q_nope, q_rope, latent, key_rope, q_pos, k_pos, w_uk, w_uv, w_o):
    heads = w_uk.shape[0]
    queries = q_nope.shape[0]
    keys = latent.shape[0]
    columns = w_o.shape[1] // 2
    swap = lambda a: shift(a, "core", 1, 2)
    ny, nx = sizes["y"], sizes["xl"] * sizes["xh"]
    spot = lambda x: (x % nx % sizes["xl"]) * sizes["xh"] + x % nx // sizes["xl"]
    shift_x = lambda a, by: lax.ppermute(
        a, ("xl", "xh"), [(spot(x), spot(x + by)) for x in range(nx)]
    )

    spot_xy = lambda x, y: (spot(x) // sizes["xh"] * ny + y % ny) * sizes["xh"] + spot(x) % sizes["xh"]
    shift_xy = lambda a, by_x, by_y: lax.ppermute(
        a,
        ("xl", "y", "xh"),
        [(spot_xy(x, y), spot_xy(x + by_x, y + by_y)) for x in range(nx) for y in range(ny)],
    )

    pack, half = pack_keys(latent, key_rope, k_pos)
    rows = pack.shape[0]
    span = rows // 2
    below = shift(half, "y", 1, ny)
    above = shift(half, "y", -1, ny)
    across = shift_x(half, 1)
    query, w_half = absorb(q_nope, q_rope, w_uk, w_o, half)
    positions = q_pos.reshape(queries, 1)
    below, above, across, query, w_half = lax.optimization_barrier(
        (below, above, across, query, w_half)
    )
    across_below = shift_x(below, 1)
    across_above = shift_x(above, -1)
    near = [below, above, across]
    swapped, below, above = lax.optimization_barrier(([swap(a) for a in near], below, above))
    far = shift(below, "y", 1, ny)
    cut = span // 2
    across_far = (
        shift_xy(above[:cut], 1, -1),
        shift_xy(below[cut:], -1, 1),
    )

    def place(*blocks):
        def find(keys, queries):
            xl, y = lax.axis_index("xl"), lax.axis_index("y")
            ids = [
                (1 - xl if over else xl) * ny + (y + d + ny) % ny for over, d in blocks
            ]
            return ids, (sizes["q0"] + (xl * ny + y) * queries) // keys

        return find

    both = [(0, 0, span), (1, 0, span)]
    state = attend(
        [[(2, 0, rows)], both, both, both],
        [pack] + [a for pair in zip(near, swapped) for a in pair],
        place((0, 0), (0, -1), (0, 1), (1, 0)),
        query, positions, None, None, heads, rows,
    )
    later, state = lax.optimization_barrier(
        ([far, across_below, across_above, *across_far], state)
    )
    swapped, w_half = lax.optimization_barrier(([swap(a) for a in later], w_half))
    w_other = swap(w_half)
    quarters = [(0, 0, cut), (1, 0, cut), (0, cut, span - cut), (1, cut, span - cut)]
    head_out = attend(
        [both, both, both, quarters],
        [a for pair in zip(later, swapped) for a in pair],
        place((0, 2), (1, -1), (1, 1), (1, 2)),
        query, positions, state, w_uv, heads, rows,
    )
    nz = sizes["z"]
    partial_out = project(nz, head_out, swap(head_out), w_o, w_other)
    piece = ring_sum(partial_out, nz)
    piece = small_call(
        sum_kernel, [shape(piece.shape)], [piece, shift(piece, "xh", 1, sizes["xh"])]
    )[0]
    found = ring_gather(piece, nz)
    mine = lax.optimization_barrier([array for _, _, array in found])
    where = [(d, row) for d, row, _ in found]
    return place_pieces(nz, where, mine, [swap(a) for a in mine], (queries, 2 * columns))


def solution(mesh):
    sizes = {"xl": 2, "y": 4, "z": 8, "xh": 2, "core": 2, "q0": 2048}
    names = ("xl", "y", "z", "xh", "core")
    fine = Mesh(mesh.devices.reshape([sizes[n] for n in names]), names)
    return jax.shard_map(
        functools.partial(per_device, sizes),
        mesh=fine,
        in_specs=(
            P(SEQ, HEAD),
            P(SEQ, HEAD),
            P(SEQ, None),
            P(SEQ, None),
            P(SEQ),
            P(SEQ),
            P(HEAD, None, None),
            P(HEAD, None, None),
            P(HEAD, None),
        ),
        out_specs=P(SEQ, None),
        check_vma=False,
    )
```

```python
import functools
import math

import jax
import jax.numpy as jnp
from jax import lax
from jax.experimental import pallas as pl
from jax.experimental.pallas import tpu as pltpu
from jax.sharding import Mesh, PartitionSpec as P

F32, BF16, I32 = jnp.float32, jnp.bfloat16, jnp.int32
LOW = -1e30
LANES = 128
SEQ = ("xl", "y")
HEAD = ("z", "xh", "core")


def call(kernel, outs, args, scratch=(), copies=1, flops=0, moved=0, vmem=24):
    anywhere = pl.BlockSpec(memory_space=pl.ANY)
    return pl.pallas_call(
        kernel,
        out_shape=outs,
        in_specs=[anywhere] * len(args),
        out_specs=jax.tree.map(lambda _: anywhere, outs),
        scratch_shapes=list(scratch) + [pltpu.SemaphoreType.DMA((copies,))],
        compiler_params=pltpu.CompilerParams(vmem_limit_bytes=vmem * 2**20),
        cost_estimate=pl.CostEstimate(flops=flops, bytes_accessed=moved, transcendentals=0),
    )(*args)


def start_all(pairs, sems, first=0):
    copies = [
        pltpu.make_async_copy(source, target, sems.at[first + i])
        for i, (source, target) in enumerate(pairs)
    ]
    for copy in copies:
        copy.start()
    return copies


def wait_all(copies):
    for copy in copies:
        copy.wait()


def room(array):
    return pltpu.VMEM(array.shape, array.dtype)


def place_of(axis):
    place = lax.axis_index(axis)
    return place, 1 - 2 * (place % 2)


def partner(place, n, which):
    step = (0, 1, -1)[which]
    return (place + (step if place % 2 == 0 else -step)) % n


def shape(dims, dtype=BF16):
    return jax.ShapeDtypeStruct(tuple(dims), dtype)


def pack_kernel(latent_in, rope_in, pos_in, pack_out, half_out, latent, rope, pos, pack, sems):
    copies = start_all([(latent_in, latent), (rope_in, rope), (pos_in, pos)], sems)
    keys, width = latent.shape
    pairs, two = rope.shape
    rope_width = two // 2
    token = lax.broadcasted_iota(I32, (keys, pairs), 0)
    pair = lax.broadcasted_iota(I32, (keys, pairs), 1)
    even = (token == 2 * pair).astype(BF16)
    odd = (token == 2 * pair + 1).astype(BF16)
    wait_all(copies)
    order = (lax.broadcasted_iota(I32, (keys, keys), 0) == pos[...] % keys).astype(BF16)
    sorted_latent = jnp.dot(order, latent[...], preferred_element_type=F32)
    spread_even = jnp.dot(even, rope[...], preferred_element_type=F32)
    spread_odd = jnp.dot(odd, rope[...], preferred_element_type=F32)
    rows = jnp.concatenate(
        [spread_even[:, :rope_width], spread_odd[:, rope_width:]], axis=1
    ).astype(BF16)
    ordered = jnp.dot(order, rows, preferred_element_type=F32)
    turned = jnp.transpose(ordered)
    pack[pl.ds(0, keys), :] = sorted_latent.astype(BF16)
    pack[pl.ds(keys, rope_width), :] = (turned[:rope_width] + turned[rope_width:]).astype(BF16)
    span = half_out.shape[0]
    start = pl.multiple_of(lax.axis_index("core") * span, span)
    wait_all(start_all([(pack.at[pl.ds(start, span), :], half_out), (pack, pack_out)], sems))


def pack_keys(latent, key_rope, k_pos):
    keys, width = latent.shape
    rows = keys + key_rope.shape[0] * key_rope.shape[1] // keys
    args = [latent, key_rope, k_pos.reshape(1, keys)]
    return call(
        pack_kernel,
        [shape((rows, width)), shape((rows // 2, width))],
        args,
        [room(a) for a in args] + [pltpu.VMEM((rows, width), BF16)],
        copies=3,
        flops=2 * keys * keys * width,
        moved=3 * keys * width * 2,
        vmem=58,
    )


def query_kernel(
    scale, q_nope_in, q_rope_in, w_uk_in, w_o, after, out, half, q_nope, q_rope, w_uk, query, held, sems
):
    columns = half.shape[1]
    start = pl.multiple_of((1 - lax.axis_index("core")) * columns, LANES)
    pairs = [(q_nope_in, q_nope), (q_rope_in, q_rope), (w_uk_in, w_uk)]
    copies = start_all(pairs, sems)
    slices = start_all([(w_o.at[:, pl.ds(start, columns)], held)], sems, len(pairs))
    wait_all(copies)
    heads, nope, width = w_uk.shape
    queries = q_nope.shape[0]
    rope = q_rope.shape[1] // heads
    for h in range(heads):
        rows = pl.ds(h * queries, queries)
        absorbed = jnp.dot(
            q_nope[:, h * nope : (h + 1) * nope], w_uk[h], preferred_element_type=F32
        )
        query[rows, pl.ds(0, width)] = (absorbed * scale).astype(BF16)
        rotary = q_rope[:, h * rope : (h + 1) * rope].astype(F32) * scale
        query[rows, pl.ds(width, rope)] = rotary.astype(BF16)
    wait_all(slices)
    wait_all(start_all([(query, out), (held, half)], sems))


def absorb(q_nope, q_rope, w_uk, w_o, after):
    heads, nope, width = w_uk.shape
    queries = q_nope.shape[0]
    rope = q_rope.shape[1] // heads
    scale = math.log2(math.e) / math.sqrt(nope + rope)
    result = shape((heads * queries, width + rope))
    half = shape((w_o.shape[0], w_o.shape[1] // 2))
    return call(
        functools.partial(query_kernel, scale),
        [result, half],
        [q_nope, q_rope, w_uk, w_o, after],
        [room(a) for a in (q_nope, q_rope, w_uk, result, half)],
        copies=4,
        flops=2 * queries * heads * nope * width,
        moved=2 * heads * queries * (nope + width) + 2 * w_o.shape[0] * w_o.shape[1],
        vmem=58,
    )


def attend_kernel(layout, first, last, heads, place, *refs):
    pieces = sum(len(block) for block in layout)
    blocks, refs = refs[:pieces], refs[pieces:]
    query_in, positions_in = refs[:2]
    refs = refs[2:]
    if not first:
        old, refs = refs[:3], refs[3:]
    if last:
        w_uv_in, out, refs = refs[0], refs[1], refs[2:]
    else:
        new, refs = refs[:3], refs[3:]
    top, total, acc, keys_in, query, positions, *rest, sems = refs
    state = (top, total, acc)
    count, rows, width = keys_in.shape
    keys = width
    queries = query.shape[0] // heads
    rope = rows - keys
    core = lax.axis_index("core")
    pairs = [(query_in, query), (positions_in, positions)]
    for b, block in enumerate(layout):
        for side, start, size in block:
            offset = start
            if side != 2:
                offset = (core if side == 0 else 1 - core) * (rows // 2) + start
                offset = pl.multiple_of(offset, 16)
            pairs.append((blocks[len(pairs) - 2], keys_in.at[b, pl.ds(offset, size), :]))
    if not first:
        pairs += list(zip(old, state))
    if last:
        w_uv, result = rest
        pairs.append((w_uv_in, w_uv))
    copies = start_all(pairs, sems)
    if first:
        top[...] = jnp.full_like(top, LOW)
        total[...] = jnp.zeros_like(total)
        acc[...] = jnp.zeros_like(acc)
    ids, diagonal = place(keys, queries)
    wait_all(copies)

    def work(b, masked):
        latents = keys_in[b, pl.ds(0, keys), :]
        def score(h):
            part = pl.ds(h * queries, queries)
            return lax.dot_general(
                query[part, pl.ds(0, width)], latents, (((1,), (1,)), ((), ())), preferred_element_type=F32
            ) + jnp.dot(query[part, pl.ds(width, rope)], keys_in[b, pl.ds(keys, rope), :], preferred_element_type=F32)

        def soften(h, scores):
            part = pl.ds(h * queries, queries)
            if masked:
                limit = positions[...] - diagonal * keys
                where = lax.broadcasted_iota(I32, (queries, keys), 1)
                scores = jnp.where(where <= limit, scores, LOW)
            before = top[part, :]
            now = jnp.maximum(before, jnp.max(scores, axis=1, keepdims=True))
            factor = jnp.exp2(before - now)
            wide = jnp.concatenate([now] * (keys // LANES), axis=1)
            exps = jnp.exp2(scores - wide)
            sums = exps[:, :LANES]
            for t in range(1, keys // LANES):
                sums = sums + exps[:, t * LANES : (t + 1) * LANES]
            top[part, :] = now
            total[part, :] = total[part, :] * factor + sums
            return exps.astype(BF16), factor

        def gather(h, probs, factor):
            part = pl.ds(h * queries, queries)
            stretch = jnp.concatenate([factor] * (width // LANES), axis=1)
            acc[part, :] = acc[part, :] * stretch + jnp.dot(
                probs, latents, preferred_element_type=F32
            )

        scores = score(0)
        for h in range(heads):
            following = score(h + 1) if h + 1 < heads else None
            gather(h, *soften(h, scores))
            scores = following

    def step(b, unused):
        block_id = ids[b]

        @pl.when(block_id < diagonal)
        def _():
            work(b, False)

        @pl.when(block_id == diagonal)
        def _():
            work(b, True)

        return unused

    for b in range(count):
        step(b, 0)
    if last:
        for h in range(heads):
            part = pl.ds(h * queries, queries)
            sums = jnp.sum(total[part, :], axis=1, keepdims=True)
            context = (acc[part, :] / sums).astype(BF16)
            value = w_uv.shape[2]
            result[:, pl.ds(h * value, value)] = jnp.dot(
                context, w_uv[h], preferred_element_type=F32
            ).astype(BF16)
        wait_all(start_all([(result, out)], sems))
    else:
        wait_all(start_all(list(zip(state, new)), sems))


def attend(layout, pieces, place, query, positions, state, w_uv, heads, rows):
    width = pieces[0].shape[1]
    total_rows = query.shape[0]
    queries = total_rows // heads
    first, last = state is None, w_uv is not None
    stats = [
        shape((total_rows, LANES), F32),
        shape((total_rows, LANES), F32),
        shape((total_rows, width), F32),
    ]
    args = [*pieces, query, positions]
    if not first:
        args += list(state)
    scratch = [room(s) for s in stats] + [
        pltpu.VMEM((len(layout), rows, width), BF16),
        room(query),
        room(positions),
    ]
    outs = stats
    if last:
        args.append(w_uv)
        outs = shape((queries, heads * w_uv.shape[2]))
        scratch += [room(w_uv), room(outs)]
    return call(
        functools.partial(attend_kernel, layout, first, last, heads, place),
        outs,
        args,
        scratch,
        copies=len(args),
        flops=16 * total_rows * width * width * len(layout),
        moved=2 * total_rows * width * 4,
    )


PARTS = 2


def project_kernel(ring, tile, mine_in, other_in, w_o, w_other, *refs):
    outs, (mine, other, w_a, w_b, left, right, result, sems) = refs[:-8], refs[-8:]
    queries, depth = mine.shape
    columns = result.shape[1]
    tiles = columns // tile
    per_out = tiles // len(outs)
    chunk = queries // ring
    inputs = start_all([(mine_in, mine), (other_in, other)], sems)
    base = lax.axis_index("core") * columns
    weights = []
    for t in range(tiles):
        here = pl.ds(t * tile, tile)
        there = pl.ds(pl.multiple_of(base + t * tile, LANES), tile)
        weights.append(
            start_all(
                [(w_o.at[:, there], w_a.at[:, here]), (w_other.at[:, here], w_b.at[:, here])],
                sems,
                2 + 2 * t,
            )
        )
    wait_all(inputs)
    z, way = place_of("z")
    for d in range(ring):
        source = pl.ds(pl.multiple_of((z + way * d + ring) % ring * chunk, chunk), chunk)
        left[pl.ds(d * chunk, chunk), :] = mine[source, :]
        right[pl.ds(d * chunk, chunk), :] = other[source, :]
    done = []
    for t in range(tiles):
        here = pl.ds(t * tile, tile)
        wait_all(weights[t])
        result[:, here] = (
            jnp.dot(left[...], w_a[:, here], preferred_element_type=F32)
            + jnp.dot(right[...], w_b[:, here], preferred_element_type=F32)
        ).astype(BF16)
        there = pl.ds(t % per_out * tile, tile)
        done += start_all([(result.at[:, here], outs[t // per_out].at[:, there])], sems, 2 + 2 * t)
    wait_all(done)


def project(ring, mine, other, w_o, w_other):
    queries, depth = mine.shape
    columns = w_other.shape[1]
    tile = columns // 4
    result = shape((queries, columns))
    return call(
        functools.partial(project_kernel, ring, tile),
        [shape((queries, columns // PARTS))] * PARTS,
        [mine, other, w_o, w_other],
        [room(a) for a in (mine, other, w_other, w_other, mine, other, result)],
        copies=2 + 2 * (columns // tile),
        flops=4 * queries * depth * columns,
        moved=4 * depth * columns,
    )


def small_call(kernel, outs, args):
    specs, arrays = [], []
    for arg in args:
        array, block, size = arg if isinstance(arg, tuple) else (arg, 0, arg.shape[0])
        arrays.append(array)
        specs.append(
            pl.BlockSpec((size, array.shape[1]), functools.partial(lambda k, i: (k, 0), block))
        )
    moved = 4 * sum(math.prod(a.shape) for a in outs)
    return pl.pallas_call(
        kernel,
        out_shape=outs,
        grid=(1,),
        in_specs=specs,
        out_specs=[pl.BlockSpec(a.shape, lambda i: (0, 0)) for a in outs],
        compiler_params=pltpu.CompilerParams(vmem_limit_bytes=16 * 2**20),
        cost_estimate=pl.CostEstimate(flops=0, bytes_accessed=moved, transcendentals=0),
    )(*arrays)


def wide(ref):
    return ref[...].astype(F32)


def pair_kernel(up, down, own_up, own_down, out_up, out_down):
    for out, moving, own, top in ((out_up, up, own_up, True), (out_down, down, own_down, False)):
        size, some = out.shape[0], moving.shape[0]
        if some == size:
            out[...] = (wide(own) + wide(moving)).astype(BF16)
        else:
            met = pl.ds(0 if top else some, some)
            out[...] = own[...]
            out[met, :] = (own[met, :].astype(F32) + wide(moving)).astype(BF16)


def sum_kernel(*refs):
    *parts, out = refs
    out[...] = sum(wide(part) for part in parts).astype(BF16)


def exchange_z(a, n, which):
    return lax.ppermute(a, "z", [(z, partner(z, n, which)) for z in range(n)])


def ring_sum(rows, n):
    size = rows.shape[0] // n
    whole = shape((size, rows.shape[1]))
    far, cut = n // 2, size // 2
    one = exchange_z(rows[far * size : far * size + cut], n, 1)
    two = exchange_z(rows[far * size + cut : (far + 1) * size], n, 2)
    for d in range(far - 1, 0, -1):
        args = [one, two, (rows, n - d, size), (rows, d, size)]
        for_two, for_one = small_call(pair_kernel, [whole] * 2, args)
        one, two = exchange_z(for_one, n, 1), exchange_z(for_two, n, 2)
    return small_call(sum_kernel, [whole], [one, two, (rows, 0, size)])[0]


def ring_gather(piece, n):
    far = n // 2
    cut = piece.shape[0] // 2
    found = [(0, 0, piece)]
    one = two = piece
    for d in range(1, far):
        one, two = lax.optimization_barrier((exchange_z(two, n, 1), exchange_z(one, n, 2)))
        found += [(d, 0, one), (-d, 0, two)]
    found.append((far, cut, exchange_z(two[cut:], n, 1)))
    found.append((far, 0, exchange_z(one[:cut], n, 2)))
    return found


def place_kernel(n, where, *refs):
    count = len(where)
    mine, other = refs[:count], refs[count : 2 * count]
    out, sems = refs[2 * count :]
    chunk = out.shape[0] // n
    columns = out.shape[1] // 2
    core = lax.axis_index("core")
    z, way = place_of("z")
    pairs = []
    for half, arrays in ((core, mine), (1 - core, other)):
        for (d, row, column), array in zip(where, arrays):
            lanes = pl.ds(pl.multiple_of(half * columns + column, LANES), array.shape[1])
            start = pl.multiple_of((z + way * d + n) % n * chunk + row, 16)
            pairs.append((array, out.at[pl.ds(start, array.shape[0]), lanes]))
    wait_all(start_all(pairs, sems))


def place_pieces(n, where, mine, other, dims):
    args = [*mine, *other]
    return call(
        functools.partial(place_kernel, n, where),
        shape(dims),
        args,
        copies=len(args),
        moved=4 * dims[0] * dims[1],
        vmem=8,
    )


def shift(x, axes, by, n):
    return lax.ppermute(x, axes, [(i, (i + by) % n) for i in range(n)])


def per_device(sizes, q_nope, q_rope, latent, key_rope, q_pos, k_pos, w_uk, w_uv, w_o):
    heads = w_uk.shape[0]
    queries = q_nope.shape[0]
    keys = latent.shape[0]
    columns = w_o.shape[1] // 2
    swap = lambda a: shift(a, "core", 1, 2)
    ny, nx = sizes["y"], sizes["xl"] * sizes["xh"]

    def exchange(a, by_x, by_y):
        pairs = []
        spot = lambda x, y: (x % sizes["xl"] * ny + y) * sizes["xh"] + x // sizes["xl"]
        for x in range(nx):
            for y in range(ny):
                pairs.append((spot(x, y), spot(partner(x, nx, by_x), partner(y, ny, by_y))))
        return lax.ppermute(a, ("xl", "y", "xh"), pairs)

    pack, half = pack_keys(latent, key_rope, k_pos)
    rows = pack.shape[0]
    span = rows // 2
    first = exchange(half, 0, 1)
    second = exchange(half, 0, 2)
    across = exchange(half, 1, 0)
    query, w_half = absorb(q_nope, q_rope, w_uk, w_o, half)
    positions = q_pos.reshape(queries, 1)
    first, second, across, query, w_half = lax.optimization_barrier(
        (first, second, across, query, w_half)
    )
    across_first = exchange(first, 1, 0)
    across_second = exchange(second, 2, 0)
    near = [first, second, across]
    swapped, first, second = lax.optimization_barrier(([swap(a) for a in near], first, second))
    far = exchange(second, 0, 1)
    cut = span // 2
    across_far = (exchange(first[:cut], 1, 2), exchange(second[cut:], 2, 1))

    def place(*blocks):
        def find(keys, queries):
            xl = lax.axis_index("xl")
            y, way = place_of("y")
            ids = [
                (1 - xl if over else xl) * ny + (y + way * d + ny) % ny for over, d in blocks
            ]
            return ids, (sizes["q0"] + (xl * ny + y) * queries) // keys

        return find

    both = [(0, 0, span), (1, 0, span)]
    state = attend(
        [[(2, 0, rows)], both, both, both],
        [pack] + [a for pair in zip(near, swapped) for a in pair],
        place((0, 0), (0, 1), (0, -1), (1, 0)),
        query, positions, None, None, heads, rows,
    )
    later, state = lax.optimization_barrier(
        ([far, across_first, across_second, *across_far], state)
    )
    swapped, w_half = lax.optimization_barrier(([swap(a) for a in later], w_half))
    w_other = swap(w_half)
    quarters = [(0, 0, cut), (1, 0, cut), (0, cut, span - cut), (1, cut, span - cut)]
    head_out = attend(
        [both, both, both, quarters],
        [a for pair in zip(later, swapped) for a in pair],
        place((0, 2), (1, 1), (1, -1), (1, 2)),
        query, positions, state, w_uv, heads, rows,
    )
    nz = sizes["z"]
    found = []
    for part in project(nz, head_out, swap(head_out), w_o, w_other):
        piece = ring_sum(part, nz)
        crossed = shift(piece, "xh", 1, sizes["xh"])
        piece = small_call(sum_kernel, [shape(piece.shape)], [piece, crossed])[0]
        column = len(found) // (nz + 1) * part.shape[1]
        found += [(d, row, column, array) for d, row, array in ring_gather(piece, nz)]
    mine = lax.optimization_barrier([array for *_, array in found])
    where = [at for *at, _ in found]
    return place_pieces(nz, where, mine, [swap(a) for a in mine], (queries, 2 * columns))


def solution(mesh):
    sizes = {"xl": 2, "y": 4, "z": 8, "xh": 2, "core": 2, "q0": 2048}
    names = ("xl", "y", "z", "xh", "core")
    fine = Mesh(mesh.devices.reshape([sizes[n] for n in names]), names)
    return jax.shard_map(
        functools.partial(per_device, sizes),
        mesh=fine,
        in_specs=(
            P(SEQ, HEAD),
            P(SEQ, HEAD),
            P(SEQ, None),
            P(SEQ, None),
            P(SEQ),
            P(SEQ),
            P(HEAD, None, None),
            P(HEAD, None, None),
            P(HEAD, None),
        ),
        out_specs=P(SEQ, None),
        check_vma=False,
    )
```

```python
import functools
import math

import jax
import jax.numpy as jnp
from jax import lax
from jax.experimental import pallas as pl
from jax.experimental.pallas import tpu as pltpu
from jax.sharding import Mesh, PartitionSpec as P

F32, BF16, I32 = jnp.float32, jnp.bfloat16, jnp.int32
LOW = -1e30
LANES = 128
SEQ = ("xl", "y")
HEAD = ("z", "xh", "core")


def call(kernel, outs, args, scratch=(), copies=1, flops=0, moved=0, vmem=24):
    anywhere = pl.BlockSpec(memory_space=pl.ANY)
    return pl.pallas_call(
        kernel,
        out_shape=outs,
        in_specs=[anywhere] * len(args),
        out_specs=jax.tree.map(lambda _: anywhere, outs),
        scratch_shapes=list(scratch) + [pltpu.SemaphoreType.DMA((copies,))],
        compiler_params=pltpu.CompilerParams(vmem_limit_bytes=vmem * 2**20),
        cost_estimate=pl.CostEstimate(flops=flops, bytes_accessed=moved, transcendentals=0),
    )(*args)


def start_all(pairs, sems, first=0):
    copies = [
        pltpu.make_async_copy(source, target, sems.at[first + i])
        for i, (source, target) in enumerate(pairs)
    ]
    for copy in copies:
        copy.start()
    return copies


def wait_all(copies):
    for copy in copies:
        copy.wait()


def room(array):
    return pltpu.VMEM(array.shape, array.dtype)


def place_of(axis):
    place = lax.axis_index(axis)
    return place, 1 - 2 * (place % 2)


def partner(place, n, which):
    step = (0, 1, -1)[which]
    return (place + (step if place % 2 == 0 else -step)) % n


def shape(dims, dtype=BF16):
    return jax.ShapeDtypeStruct(tuple(dims), dtype)


def pack_kernel(latent_in, rope_in, pos_in, pack_out, half_out, latent, rope, pos, pack, sems):
    copies = start_all([(latent_in, latent), (rope_in, rope), (pos_in, pos)], sems)
    keys, width = latent.shape
    pairs, two = rope.shape
    rope_width = two // 2
    token = lax.broadcasted_iota(I32, (keys, pairs), 0)
    pair = lax.broadcasted_iota(I32, (keys, pairs), 1)
    even = (token == 2 * pair).astype(BF16)
    odd = (token == 2 * pair + 1).astype(BF16)
    wait_all(copies)
    order = (lax.broadcasted_iota(I32, (keys, keys), 0) == pos[...] % keys).astype(BF16)
    sorted_latent = jnp.dot(order, latent[...], preferred_element_type=F32)
    spread_even = jnp.dot(even, rope[...], preferred_element_type=F32)
    spread_odd = jnp.dot(odd, rope[...], preferred_element_type=F32)
    rows = jnp.concatenate(
        [spread_even[:, :rope_width], spread_odd[:, rope_width:]], axis=1
    ).astype(BF16)
    ordered = jnp.dot(order, rows, preferred_element_type=F32)
    turned = jnp.transpose(ordered)
    pack[pl.ds(0, keys), :] = sorted_latent.astype(BF16)
    pack[pl.ds(keys, rope_width), :] = (turned[:rope_width] + turned[rope_width:]).astype(BF16)
    span = half_out.shape[0]
    start = pl.multiple_of(lax.axis_index("core") * span, span)
    wait_all(start_all([(pack.at[pl.ds(start, span), :], half_out), (pack, pack_out)], sems))


def pack_keys(latent, key_rope, k_pos):
    keys, width = latent.shape
    rows = keys + key_rope.shape[0] * key_rope.shape[1] // keys
    args = [latent, key_rope, k_pos.reshape(1, keys)]
    return call(
        pack_kernel,
        [shape((rows, width)), shape((rows // 2, width))],
        args,
        [room(a) for a in args] + [pltpu.VMEM((rows, width), BF16)],
        copies=3,
        flops=2 * keys * keys * width,
        moved=3 * keys * width * 2,
        vmem=58,
    )


def query_kernel(scale, q_nope_in, q_rope_in, w_uk_in, out, q_nope, q_rope, w_uk, query, sems):
    pairs = [(q_nope_in, q_nope), (q_rope_in, q_rope), (w_uk_in, w_uk)]
    wait_all(start_all(pairs, sems))
    heads, nope, width = w_uk.shape
    queries = q_nope.shape[0]
    rope = q_rope.shape[1] // heads
    for h in range(heads):
        rows = pl.ds(h * queries, queries)
        absorbed = jnp.dot(
            q_nope[:, h * nope : (h + 1) * nope], w_uk[h], preferred_element_type=F32
        )
        query[rows, pl.ds(0, width)] = (absorbed * scale).astype(BF16)
        rotary = q_rope[:, h * rope : (h + 1) * rope].astype(F32) * scale
        query[rows, pl.ds(width, rope)] = rotary.astype(BF16)
    wait_all(start_all([(query, out)], sems))


def absorb(q_nope, q_rope, w_uk):
    heads, nope, width = w_uk.shape
    queries = q_nope.shape[0]
    rope = q_rope.shape[1] // heads
    scale = math.log2(math.e) / math.sqrt(nope + rope)
    result = shape((heads * queries, width + rope))
    return call(
        functools.partial(query_kernel, scale),
        result,
        [q_nope, q_rope, w_uk],
        [room(a) for a in (q_nope, q_rope, w_uk, result)],
        copies=3,
        flops=2 * queries * heads * nope * width,
        moved=2 * heads * queries * (nope + width),
    )


def half_kernel(w_o, half, held, sems):
    columns = half.shape[1]
    start = pl.multiple_of((1 - lax.axis_index("core")) * columns, LANES)
    wait_all(start_all([(w_o.at[:, pl.ds(start, columns)], held)], sems))
    wait_all(start_all([(held, half)], sems))


def other_half(w_o):
    half = shape((w_o.shape[0], w_o.shape[1] // 2))
    return call(
        half_kernel, half, [w_o], [room(half)], moved=2 * w_o.shape[0] * w_o.shape[1], vmem=58
    )


def attend_kernel(layout, first, last, heads, place, *refs):
    pieces = sum(len(block) for block in layout)
    blocks, refs = refs[:pieces], refs[pieces:]
    query_in, positions_in = refs[:2]
    refs = refs[2:]
    if not first:
        old, refs = refs[:3], refs[3:]
    if last:
        w_uv_in, out, refs = refs[0], refs[1], refs[2:]
    else:
        new, refs = refs[:3], refs[3:]
    top, total, acc, keys_in, query, positions, *rest, sems = refs
    state = (top, total, acc)
    count, rows, width = keys_in.shape
    keys = width
    queries = query.shape[0] // heads
    rope = rows - keys
    core = lax.axis_index("core")
    pairs = [(query_in, query), (positions_in, positions)]
    for b, block in enumerate(layout):
        for side, start, size in block:
            offset = start
            if side != 2:
                offset = (core if side == 0 else 1 - core) * (rows // 2) + start
                offset = pl.multiple_of(offset, 16)
            pairs.append((blocks[len(pairs) - 2], keys_in.at[b, pl.ds(offset, size), :]))
    if not first:
        pairs += list(zip(old, state))
    if last:
        w_uv, result = rest
        pairs.append((w_uv_in, w_uv))
    copies = start_all(pairs, sems)
    if first:
        top[...] = jnp.full_like(top, LOW)
        total[...] = jnp.zeros_like(total)
        acc[...] = jnp.zeros_like(acc)
    ids, diagonal = place(keys, queries)
    wait_all(copies)

    def work(b, masked):
        latents = keys_in[b, pl.ds(0, keys), :]
        def score(h):
            part = pl.ds(h * queries, queries)
            return lax.dot_general(
                query[part, pl.ds(0, width)], latents, (((1,), (1,)), ((), ())), preferred_element_type=F32
            ) + jnp.dot(query[part, pl.ds(width, rope)], keys_in[b, pl.ds(keys, rope), :], preferred_element_type=F32)

        def soften(h, scores):
            part = pl.ds(h * queries, queries)
            if masked:
                limit = positions[...] - diagonal * keys
                where = lax.broadcasted_iota(I32, (queries, keys), 1)
                scores = jnp.where(where <= limit, scores, LOW)
            before = top[part, :]
            now = jnp.maximum(before, jnp.max(scores, axis=1, keepdims=True))
            factor = jnp.exp2(before - now)
            wide = jnp.concatenate([now] * (keys // LANES), axis=1)
            exps = jnp.exp2(scores - wide)
            sums = exps[:, :LANES]
            for t in range(1, keys // LANES):
                sums = sums + exps[:, t * LANES : (t + 1) * LANES]
            top[part, :] = now
            total[part, :] = total[part, :] * factor + sums
            return exps.astype(BF16), factor

        def gather(h, probs, factor):
            part = pl.ds(h * queries, queries)
            stretch = jnp.concatenate([factor] * (width // LANES), axis=1)
            acc[part, :] = acc[part, :] * stretch + jnp.dot(
                probs, latents, preferred_element_type=F32
            )

        scores = score(0)
        for h in range(heads):
            following = score(h + 1) if h + 1 < heads else None
            gather(h, *soften(h, scores))
            scores = following

    def step(b, unused):
        block_id = ids[b]

        @pl.when(block_id < diagonal)
        def _():
            work(b, False)

        @pl.when(block_id == diagonal)
        def _():
            work(b, True)

        return unused

    for b in range(count):
        step(b, 0)
    if last:
        for h in range(heads):
            part = pl.ds(h * queries, queries)
            sums = jnp.sum(total[part, :], axis=1, keepdims=True)
            context = (acc[part, :] / sums).astype(BF16)
            value = w_uv.shape[2]
            result[:, pl.ds(h * value, value)] = jnp.dot(
                context, w_uv[h], preferred_element_type=F32
            ).astype(BF16)
        wait_all(start_all([(result, out)], sems))
    else:
        wait_all(start_all(list(zip(state, new)), sems))


def attend(layout, pieces, place, query, positions, state, w_uv, heads, rows):
    width = pieces[0].shape[1]
    total_rows = query.shape[0]
    queries = total_rows // heads
    first, last = state is None, w_uv is not None
    stats = [
        shape((total_rows, LANES), F32),
        shape((total_rows, LANES), F32),
        shape((total_rows, width), F32),
    ]
    args = [*pieces, query, positions]
    if not first:
        args += list(state)
    scratch = [room(s) for s in stats] + [
        pltpu.VMEM((len(layout), rows, width), BF16),
        room(query),
        room(positions),
    ]
    outs = stats
    if last:
        args.append(w_uv)
        outs = shape((queries, heads * w_uv.shape[2]))
        scratch += [room(w_uv), room(outs)]
    return call(
        functools.partial(attend_kernel, layout, first, last, heads, place),
        outs,
        args,
        scratch,
        copies=len(args),
        flops=16 * total_rows * width * width * len(layout),
        moved=2 * total_rows * width * 4,
    )


PARTS = 2


def project_kernel(ring, mine, other, w_o, w_other, *refs):
    outs, (left, right) = refs[:-2], refs[-2:]
    queries, depth = mine.shape
    columns = w_other.shape[1]
    chunk = queries // ring
    base = lax.axis_index("core") * columns
    z, way = place_of("z")
    for d in range(ring):
        source = pl.ds(pl.multiple_of((z + way * d + ring) % ring * chunk, chunk), chunk)
        left[pl.ds(d * chunk, chunk), :] = mine[source, :]
        right[pl.ds(d * chunk, chunk), :] = other[source, :]
    tile = 256
    per_out = columns // len(outs) // tile
    for t in range(columns // tile):
        here = pl.ds(t * tile, tile)
        there = pl.ds(pl.multiple_of(base + t * tile, LANES), tile)
        outs[t // per_out][:, pl.ds(t % per_out * tile, tile)] = (
            jnp.dot(left[...], w_o[:, there], preferred_element_type=F32)
            + jnp.dot(right[...], w_other[:, here], preferred_element_type=F32)
        ).astype(BF16)


def project(ring, mine, other, w_o, w_other):
    queries, depth = mine.shape
    columns = w_other.shape[1]
    vmem = pl.BlockSpec(memory_space=pltpu.VMEM)
    return pl.pallas_call(
        functools.partial(project_kernel, ring),
        out_shape=[shape((queries, columns // PARTS))] * PARTS,
        in_specs=[vmem] * 4,
        out_specs=[vmem] * PARTS,
        scratch_shapes=[room(mine), room(other)],
        compiler_params=pltpu.CompilerParams(vmem_limit_bytes=24 * 2**20),
        cost_estimate=pl.CostEstimate(
            flops=4 * queries * depth * columns, bytes_accessed=4 * depth * columns, transcendentals=0
        ),
    )(mine, other, w_o, w_other)


def small_call(kernel, outs, args):
    specs, arrays = [], []
    for arg in args:
        array, block, size = arg if isinstance(arg, tuple) else (arg, 0, arg.shape[0])
        arrays.append(array)
        specs.append(
            pl.BlockSpec((size, array.shape[1]), functools.partial(lambda k, i: (k, 0), block))
        )
    moved = 4 * sum(math.prod(a.shape) for a in outs)
    return pl.pallas_call(
        kernel,
        out_shape=outs,
        grid=(1,),
        in_specs=specs,
        out_specs=[pl.BlockSpec(a.shape, lambda i: (0, 0)) for a in outs],
        compiler_params=pltpu.CompilerParams(vmem_limit_bytes=16 * 2**20),
        cost_estimate=pl.CostEstimate(flops=0, bytes_accessed=moved, transcendentals=0),
    )(*arrays)


def wide(ref):
    return ref[...].astype(F32)


def pair_kernel(up, down, own_up, own_down, out_up, out_down):
    for out, moving, own, top in ((out_up, up, own_up, True), (out_down, down, own_down, False)):
        size, some = out.shape[0], moving.shape[0]
        if some == size:
            out[...] = (wide(own) + wide(moving)).astype(BF16)
        else:
            met = pl.ds(0 if top else some, some)
            out[...] = own[...]
            out[met, :] = (own[met, :].astype(F32) + wide(moving)).astype(BF16)


def sum_kernel(*refs):
    *parts, out = refs
    out[...] = sum(wide(part) for part in parts).astype(BF16)


def exchange_z(a, n, which):
    return lax.ppermute(a, "z", [(z, partner(z, n, which)) for z in range(n)])


def ring_sum(rows, n):
    size = rows.shape[0] // n
    whole = shape((size, rows.shape[1]))
    far, cut = n // 2, size // 2
    one = exchange_z(rows[far * size : far * size + cut], n, 1)
    two = exchange_z(rows[far * size + cut : (far + 1) * size], n, 2)
    for d in range(far - 1, 0, -1):
        args = [one, two, (rows, n - d, size), (rows, d, size)]
        for_two, for_one = small_call(pair_kernel, [whole] * 2, args)
        one, two = exchange_z(for_one, n, 1), exchange_z(for_two, n, 2)
    return small_call(sum_kernel, [whole], [one, two, (rows, 0, size)])[0]


def ring_gather(piece, n):
    far = n // 2
    cut = piece.shape[0] // 2
    found = [(0, 0, piece)]
    one = two = piece
    for d in range(1, far):
        one, two = lax.optimization_barrier((exchange_z(two, n, 1), exchange_z(one, n, 2)))
        found += [(d, 0, one), (-d, 0, two)]
    found.append((far, cut, exchange_z(two[cut:], n, 1)))
    found.append((far, 0, exchange_z(one[:cut], n, 2)))
    return found


def join_kernel(n, where, *refs):
    pieces, out = refs[:-1], refs[-1]
    chunk = out.shape[0] // n
    z, way = place_of("z")
    for (d, row), piece in zip(where, pieces):
        start = pl.multiple_of((z + way * d + n) % n * chunk + row, 16)
        out[pl.ds(start, piece.shape[0]), :] = piece[...]


def join(n, found):
    where = [(d, row) for d, row, _ in found]
    pieces = [array for *_, array in found]
    chunk, columns = pieces[0].shape
    result = shape((n * chunk, columns))
    return small_call(functools.partial(join_kernel, n, where), [result], pieces)[0]


def place_kernel(mine, count, *refs):
    parts, (out, sems) = refs[:count], refs[-2:]
    columns = out.shape[1] // 2
    core = lax.axis_index("core")
    half = core if mine else 1 - core
    pairs = []
    for i, part in enumerate(parts):
        width = part.shape[1]
        lanes = pl.ds(pl.multiple_of(half * columns + i * width, LANES), width)
        pairs.append((part, out.at[:, lanes]))
    wait_all(start_all(pairs, sems))


def place_parts(parts, dims, filled=None):
    anywhere = pl.BlockSpec(memory_space=pl.ANY)
    args = [*parts] + ([] if filled is None else [filled])
    return pl.pallas_call(
        functools.partial(place_kernel, filled is None, len(parts)),
        out_shape=shape(dims),
        in_specs=[anywhere] * len(args),
        out_specs=anywhere,
        scratch_shapes=[pltpu.SemaphoreType.DMA((len(parts),))],
        input_output_aliases={} if filled is None else {len(parts): 0},
        compiler_params=pltpu.CompilerParams(vmem_limit_bytes=8 * 2**20),
        cost_estimate=pl.CostEstimate(
            flops=0, bytes_accessed=2 * dims[0] * dims[1], transcendentals=0
        ),
    )(*args)


def shift(x, axes, by, n):
    return lax.ppermute(x, axes, [(i, (i + by) % n) for i in range(n)])


def per_device(sizes, q_nope, q_rope, latent, key_rope, q_pos, k_pos, w_uk, w_uv, w_o):
    heads = w_uk.shape[0]
    queries = q_nope.shape[0]
    keys = latent.shape[0]
    columns = w_o.shape[1] // 2
    swap = lambda a: shift(a, "core", 1, 2)
    ny, nx = sizes["y"], sizes["xl"] * sizes["xh"]

    def exchange(a, by_x, by_y):
        pairs = []
        spot = lambda x, y: (x % sizes["xl"] * ny + y) * sizes["xh"] + x // sizes["xl"]
        for x in range(nx):
            for y in range(ny):
                pairs.append((spot(x, y), spot(partner(x, nx, by_x), partner(y, ny, by_y))))
        return lax.ppermute(a, ("xl", "y", "xh"), pairs)

    pack, half = pack_keys(latent, key_rope, k_pos)
    rows = pack.shape[0]
    span = rows // 2
    first = exchange(half, 0, 1)
    second = exchange(half, 0, 2)
    across = exchange(half, 1, 0)
    q_nope, q_rope, w_uk, w_o, half = lax.optimization_barrier((q_nope, q_rope, w_uk, w_o, half))
    w_half = other_half(w_o)
    query = absorb(q_nope, q_rope, w_uk)
    positions = q_pos.reshape(queries, 1)
    first, second, across, query, w_half = lax.optimization_barrier(
        (first, second, across, query, w_half)
    )
    across_first = exchange(first, 1, 0)
    across_second = exchange(second, 2, 0)
    near = [first, second, across]
    swapped, first, second = lax.optimization_barrier(([swap(a) for a in near], first, second))
    far = exchange(second, 0, 1)
    cut = span // 2
    across_far = (exchange(first[:cut], 1, 2), exchange(second[cut:], 2, 1))

    def place(*blocks):
        def find(keys, queries):
            xl = lax.axis_index("xl")
            y, way = place_of("y")
            ids = [
                (1 - xl if over else xl) * ny + (y + way * d + ny) % ny for over, d in blocks
            ]
            return ids, (sizes["q0"] + (xl * ny + y) * queries) // keys

        return find

    both = [(0, 0, span), (1, 0, span)]
    state = attend(
        [[(2, 0, rows)], both, both, both],
        [pack] + [a for pair in zip(near, swapped) for a in pair],
        place((0, 0), (0, 1), (0, -1), (1, 0)),
        query, positions, None, None, heads, rows,
    )
    later, state = lax.optimization_barrier(
        ([far, across_first, across_second, *across_far], state)
    )
    swapped, w_half = lax.optimization_barrier(([swap(a) for a in later], w_half))
    w_other = swap(w_half)
    quarters = [(0, 0, cut), (1, 0, cut), (0, cut, span - cut), (1, cut, span - cut)]
    head_out = attend(
        [both, both, both, quarters],
        [a for pair in zip(later, swapped) for a in pair],
        place((0, 2), (1, 1), (1, -1), (1, 2)),
        query, positions, state, w_uv, heads, rows,
    )
    nz = sizes["z"]
    parts = []
    for part in project(nz, head_out, swap(head_out), w_o, w_other):
        piece = ring_sum(part, nz)
        crossed = shift(piece, "xh", 1, sizes["xh"])
        piece = small_call(sum_kernel, [shape(piece.shape)], [piece, crossed])[0]
        parts.append(join(nz, ring_gather(piece, nz)))
    dims = (queries, 2 * columns)
    return place_parts([swap(a) for a in parts], dims, place_parts(parts, dims))


def solution(mesh):
    sizes = {"xl": 2, "y": 4, "z": 8, "xh": 2, "core": 2, "q0": 2048}
    names = ("xl", "y", "z", "xh", "core")
    fine = Mesh(mesh.devices.reshape([sizes[n] for n in names]), names)
    return jax.shard_map(
        functools.partial(per_device, sizes),
        mesh=fine,
        in_specs=(
            P(SEQ, HEAD),
            P(SEQ, HEAD),
            P(SEQ, None),
            P(SEQ, None),
            P(SEQ),
            P(SEQ),
            P(HEAD, None, None),
            P(HEAD, None, None),
            P(HEAD, None),
        ),
        out_specs=P(SEQ, None),
        check_vma=False,
    )
```

```python
import functools
import math

import jax
import jax.numpy as jnp
from jax import lax
from jax.experimental import pallas as pl
from jax.experimental.pallas import tpu as pltpu
from jax.sharding import Mesh, PartitionSpec as P

F32, BF16, I32 = jnp.float32, jnp.bfloat16, jnp.int32
LOW = -1e30
LANES = 128
SEQ = ("xl", "y")
HEAD = ("z", "xh", "core")


def call(kernel, outs, args, scratch=(), copies=1, flops=0, moved=0, vmem=24):
    anywhere = pl.BlockSpec(memory_space=pl.ANY)
    return pl.pallas_call(
        kernel,
        out_shape=outs,
        in_specs=[anywhere] * len(args),
        out_specs=jax.tree.map(lambda _: anywhere, outs),
        scratch_shapes=list(scratch) + [pltpu.SemaphoreType.DMA((copies,))],
        compiler_params=pltpu.CompilerParams(vmem_limit_bytes=vmem * 2**20),
        cost_estimate=pl.CostEstimate(flops=flops, bytes_accessed=moved, transcendentals=0),
    )(*args)


def start_all(pairs, sems, first=0):
    copies = [
        pltpu.make_async_copy(source, target, sems.at[first + i])
        for i, (source, target) in enumerate(pairs)
    ]
    for copy in copies:
        copy.start()
    return copies


def wait_all(copies):
    for copy in copies:
        copy.wait()


def room(array):
    return pltpu.VMEM(array.shape, array.dtype)


def place_of(axis):
    place = lax.axis_index(axis)
    return place, 1 - 2 * (place % 2)


def partner(place, n, which):
    step = (0, 1, -1)[which]
    return (place + (step if place % 2 == 0 else -step)) % n


def shape(dims, dtype=BF16):
    return jax.ShapeDtypeStruct(tuple(dims), dtype)


def pack_kernel(latent_in, rope_in, pos_in, pack_out, half_out, latent, rope, pos, pack, sems):
    copies = start_all([(latent_in, latent), (rope_in, rope), (pos_in, pos)], sems)
    keys, width = latent.shape
    pairs, two = rope.shape
    rope_width = two // 2
    token = lax.broadcasted_iota(I32, (keys, pairs), 0)
    pair = lax.broadcasted_iota(I32, (keys, pairs), 1)
    even = (token == 2 * pair).astype(BF16)
    odd = (token == 2 * pair + 1).astype(BF16)
    wait_all(copies)
    order = (lax.broadcasted_iota(I32, (keys, keys), 0) == pos[...] % keys).astype(BF16)
    sorted_latent = jnp.dot(order, latent[...], preferred_element_type=F32)
    spread_even = jnp.dot(even, rope[...], preferred_element_type=F32)
    spread_odd = jnp.dot(odd, rope[...], preferred_element_type=F32)
    rows = jnp.concatenate(
        [spread_even[:, :rope_width], spread_odd[:, rope_width:]], axis=1
    ).astype(BF16)
    ordered = jnp.dot(order, rows, preferred_element_type=F32)
    turned = jnp.transpose(ordered)
    pack[pl.ds(0, keys), :] = sorted_latent.astype(BF16)
    pack[pl.ds(keys, rope_width), :] = (turned[:rope_width] + turned[rope_width:]).astype(BF16)
    span = half_out.shape[0]
    start = pl.multiple_of(lax.axis_index("core") * span, span)
    wait_all(start_all([(pack.at[pl.ds(start, span), :], half_out), (pack, pack_out)], sems))


def pack_keys(latent, key_rope, k_pos):
    keys, width = latent.shape
    rows = keys + key_rope.shape[0] * key_rope.shape[1] // keys
    args = [latent, key_rope, k_pos.reshape(1, keys)]
    return call(
        pack_kernel,
        [shape((rows, width)), shape((rows // 2, width))],
        args,
        [room(a) for a in args] + [pltpu.VMEM((rows, width), BF16)],
        copies=3,
        flops=2 * keys * keys * width,
        moved=3 * keys * width * 2,
        vmem=58,
    )


def query_kernel(scale, q_nope_in, q_rope_in, w_uk_in, out, q_nope, q_rope, w_uk, query, sems):
    pairs = [(q_nope_in, q_nope), (q_rope_in, q_rope), (w_uk_in, w_uk)]
    wait_all(start_all(pairs, sems))
    heads, nope, width = w_uk.shape
    queries = q_nope.shape[0]
    rope = q_rope.shape[1] // heads
    for h in range(heads):
        rows = pl.ds(h * queries, queries)
        absorbed = jnp.dot(
            q_nope[:, h * nope : (h + 1) * nope], w_uk[h], preferred_element_type=F32
        )
        query[rows, pl.ds(0, width)] = (absorbed * scale).astype(BF16)
        rotary = q_rope[:, h * rope : (h + 1) * rope].astype(F32) * scale
        query[rows, pl.ds(width, rope)] = rotary.astype(BF16)
    wait_all(start_all([(query, out)], sems))


def absorb(q_nope, q_rope, w_uk):
    heads, nope, width = w_uk.shape
    queries = q_nope.shape[0]
    rope = q_rope.shape[1] // heads
    scale = math.log2(math.e) / math.sqrt(nope + rope)
    result = shape((heads * queries, width + rope))
    return call(
        functools.partial(query_kernel, scale),
        result,
        [q_nope, q_rope, w_uk],
        [room(a) for a in (q_nope, q_rope, w_uk, result)],
        copies=3,
        flops=2 * queries * heads * nope * width,
        moved=2 * heads * queries * (nope + width),
    )


def half_kernel(w_o, half, held, sems):
    columns = half.shape[1]
    start = pl.multiple_of((1 - lax.axis_index("core")) * columns, LANES)
    wait_all(start_all([(w_o.at[:, pl.ds(start, columns)], held)], sems))
    wait_all(start_all([(held, half)], sems))


def other_half(w_o):
    half = shape((w_o.shape[0], w_o.shape[1] // 2))
    return call(
        half_kernel, half, [w_o], [room(half)], moved=2 * w_o.shape[0] * w_o.shape[1], vmem=58
    )


def attend_kernel(layout, first, last, heads, place, *refs):
    pieces = sum(len(block) for block in layout)
    blocks, refs = refs[:pieces], refs[pieces:]
    query_in, positions_in = refs[:2]
    refs = refs[2:]
    if not first:
        old, refs = refs[:3], refs[3:]
    if last:
        w_uv_in, out, refs = refs[0], refs[1], refs[2:]
    else:
        new, refs = refs[:3], refs[3:]
    top, total, acc, keys_in, query, positions, *rest, sems = refs
    state = (top, total, acc)
    count, rows, width = keys_in.shape
    keys = width
    queries = query.shape[0] // heads
    rope = rows - keys
    core = lax.axis_index("core")
    pairs = [(query_in, query), (positions_in, positions)]
    for b, block in enumerate(layout):
        for side, start, size in block:
            offset = start
            if side != 2:
                offset = (core if side == 0 else 1 - core) * (rows // 2) + start
                offset = pl.multiple_of(offset, 16)
            pairs.append((blocks[len(pairs) - 2], keys_in.at[b, pl.ds(offset, size), :]))
    if not first:
        pairs += list(zip(old, state))
    if last:
        w_uv, result = rest
        pairs.append((w_uv_in, w_uv))
    copies = start_all(pairs, sems)
    ids, diagonal = place(keys, queries)
    wait_all(copies)

    def work(group, masked, fresh):
        def score(h):
            part = pl.ds(h * queries, queries)
            found = []
            for b in group:
                latents = keys_in[b, pl.ds(0, keys), :]
                found.append(
                    lax.dot_general(
                        query[part, pl.ds(0, width)],
                        latents,
                        (((1,), (1,)), ((), ())),
                        preferred_element_type=F32,
                    )
                    + jnp.dot(
                        query[part, pl.ds(width, rope)],
                        keys_in[b, pl.ds(keys, rope), :],
                        preferred_element_type=F32,
                    )
                )
            return found

        def soften(h, found):
            part = pl.ds(h * queries, queries)
            if masked:
                limit = positions[...] - diagonal * keys
                where = lax.broadcasted_iota(I32, (queries, keys), 1)
                found = [jnp.where(where <= limit, scores, LOW) for scores in found]
            largest = functools.reduce(jnp.maximum, found)
            highest = jnp.max(largest, axis=1, keepdims=True)
            if fresh:
                now = jnp.broadcast_to(highest, (queries, LANES))
                factor = None
            else:
                before = top[part, :]
                now = jnp.maximum(before, highest)
                factor = jnp.exp2(before - now)
            wide_top = jnp.concatenate([now] * (keys // LANES), axis=1)
            probs, sums = [], None
            for scores in found:
                exps = jnp.exp2(scores - wide_top)
                for t in range(keys // LANES):
                    some = exps[:, t * LANES : (t + 1) * LANES]
                    sums = some if sums is None else sums + some
                probs.append(exps.astype(BF16))
            top[part, :] = now
            total[part, :] = sums if fresh else total[part, :] * factor + sums
            return probs, factor

        def gather(h, probs, factor):
            part = pl.ds(h * queries, queries)
            added = None
            for b, prob in zip(group, probs):
                more = jnp.dot(prob, keys_in[b, pl.ds(0, keys), :], preferred_element_type=F32)
                added = more if added is None else added + more
            if fresh:
                acc[part, :] = added
            else:
                stretch = jnp.concatenate([factor] * (width // LANES), axis=1)
                acc[part, :] = acc[part, :] * stretch + added

        found = score(0)
        for h in range(heads):
            following = score(h + 1) if h + 1 < heads else None
            gather(h, *soften(h, found))
            found = following

    def step(b, fresh=False):
        @pl.when(ids[b] < diagonal)
        def _():
            work([b], False, fresh)

        @pl.when(ids[b] == diagonal)
        def _():
            work([b], True, fresh)

    def pair(b):
        full = jnp.logical_and(ids[b] < diagonal, ids[b + 1] < diagonal)

        @pl.when(full)
        def _():
            work([b, b + 1], False, False)

        @pl.when(jnp.logical_not(full))
        def _():
            step(b)
            step(b + 1)

    begin = 0
    if first:
        step(0, True)
        begin = 1
    for b in range(begin, count):
        step(b)
    if last:
        for h in range(heads):
            part = pl.ds(h * queries, queries)
            sums = jnp.sum(total[part, :], axis=1, keepdims=True)
            context = (acc[part, :] / sums).astype(BF16)
            value = w_uv.shape[2]
            result[:, pl.ds(h * value, value)] = jnp.dot(
                context, w_uv[h], preferred_element_type=F32
            ).astype(BF16)
        wait_all(start_all([(result, out)], sems))
    else:
        wait_all(start_all(list(zip(state, new)), sems))


def attend(layout, pieces, place, query, positions, state, w_uv, heads, rows):
    width = pieces[0].shape[1]
    total_rows = query.shape[0]
    queries = total_rows // heads
    first, last = state is None, w_uv is not None
    stats = [
        shape((total_rows, LANES), F32),
        shape((total_rows, LANES), F32),
        shape((total_rows, width), F32),
    ]
    args = [*pieces, query, positions]
    if not first:
        args += list(state)
    scratch = [room(s) for s in stats] + [
        pltpu.VMEM((len(layout), rows, width), BF16),
        room(query),
        room(positions),
    ]
    outs = stats
    if last:
        args.append(w_uv)
        outs = shape((queries, heads * w_uv.shape[2]))
        scratch += [room(w_uv), room(outs)]
    return call(
        functools.partial(attend_kernel, layout, first, last, heads, place),
        outs,
        args,
        scratch,
        copies=len(args),
        flops=16 * total_rows * width * width * len(layout),
        moved=2 * total_rows * width * 4,
    )


PARTS = 2


def project_kernel(ring, mine, other, w_o, w_other, *refs):
    outs, (left, right) = refs[:-2], refs[-2:]
    queries, depth = mine.shape
    columns = w_other.shape[1]
    chunk = queries // ring
    base = lax.axis_index("core") * columns
    z, way = place_of("z")
    for d in range(ring):
        source = pl.ds(pl.multiple_of((z + way * d + ring) % ring * chunk, chunk), chunk)
        left[pl.ds(d * chunk, chunk), :] = mine[source, :]
        right[pl.ds(d * chunk, chunk), :] = other[source, :]
    tile = 256
    per_out = columns // len(outs) // tile
    for t in range(columns // tile):
        here = pl.ds(t * tile, tile)
        there = pl.ds(pl.multiple_of(base + t * tile, LANES), tile)
        outs[t // per_out][:, pl.ds(t % per_out * tile, tile)] = (
            jnp.dot(left[...], w_o[:, there], preferred_element_type=F32)
            + jnp.dot(right[...], w_other[:, here], preferred_element_type=F32)
        ).astype(BF16)


def project(ring, mine, other, w_o, w_other):
    queries, depth = mine.shape
    columns = w_other.shape[1]
    vmem = pl.BlockSpec(memory_space=pltpu.VMEM)
    return pl.pallas_call(
        functools.partial(project_kernel, ring),
        out_shape=[shape((queries, columns // PARTS))] * PARTS,
        in_specs=[vmem] * 4,
        out_specs=[vmem] * PARTS,
        scratch_shapes=[room(mine), room(other)],
        compiler_params=pltpu.CompilerParams(vmem_limit_bytes=24 * 2**20),
        cost_estimate=pl.CostEstimate(
            flops=4 * queries * depth * columns, bytes_accessed=4 * depth * columns, transcendentals=0
        ),
    )(mine, other, w_o, w_other)


def small_call(kernel, outs, args):
    specs, arrays = [], []
    for arg in args:
        array, block, size = arg if isinstance(arg, tuple) else (arg, 0, arg.shape[0])
        arrays.append(array)
        specs.append(
            pl.BlockSpec((size, array.shape[1]), functools.partial(lambda k, i: (k, 0), block))
        )
    moved = 4 * sum(math.prod(a.shape) for a in outs)
    return pl.pallas_call(
        kernel,
        out_shape=outs,
        grid=(1,),
        in_specs=specs,
        out_specs=[pl.BlockSpec(a.shape, lambda i: (0, 0)) for a in outs],
        compiler_params=pltpu.CompilerParams(vmem_limit_bytes=16 * 2**20),
        cost_estimate=pl.CostEstimate(flops=0, bytes_accessed=moved, transcendentals=0),
    )(*arrays)


def wide(ref):
    return ref[...].astype(F32)


def meet_kernel(start, moving, own, out):
    met = pl.ds(start, moving.shape[0])
    if moving.shape[0] != out.shape[0]:
        out[...] = own[...]
    out[met, :] = (own[met, :].astype(F32) + wide(moving)).astype(BF16)


def sum_kernel(*refs):
    *parts, out = refs
    out[...] = sum(wide(part) for part in parts).astype(BF16)


def exchange_z(a, n, which):
    return lax.ppermute(a, "z", [(z, partner(z, n, which)) for z in range(n)])


def ring_sum(rows, n):
    size = rows.shape[0] // n
    whole = shape((size, rows.shape[1]))
    far, cut = n // 2, size // 2
    one = exchange_z(rows[far * size : far * size + cut], n, 1)
    two = exchange_z(rows[far * size + cut : (far + 1) * size], n, 2)
    for d in range(far - 1, 0, -1):
        for_two = small_call(
            functools.partial(meet_kernel, 0), [whole], [one, (rows, n - d, size)]
        )[0]
        for_one = small_call(
            functools.partial(meet_kernel, size - two.shape[0]), [whole], [two, (rows, d, size)]
        )[0]
        one, two = exchange_z(for_one, n, 1), exchange_z(for_two, n, 2)
    return small_call(sum_kernel, [whole], [one, two, (rows, 0, size)])[0]


def ring_gather(piece, n):
    far = n // 2
    cut = piece.shape[0] // 2
    found = [(0, 0, piece)]
    one = two = piece
    for d in range(1, far):
        one, two = exchange_z(two, n, 1), exchange_z(one, n, 2)
        found += [(d, 0, one), (-d, 0, two)]
    found.append((far, cut, exchange_z(two[cut:], n, 1)))
    found.append((far, 0, exchange_z(one[:cut], n, 2)))
    return found


def join_kernel(n, where, *refs):
    pieces, out = refs[:-1], refs[-1]
    chunk = out.shape[0] // n
    z, way = place_of("z")
    for (d, row), piece in zip(where, pieces):
        start = pl.multiple_of((z + way * d + n) % n * chunk + row, 16)
        out[pl.ds(start, piece.shape[0]), :] = piece[...]


def join(n, found):
    where = [(d, row) for d, row, _ in found]
    pieces = [array for *_, array in found]
    chunk, columns = pieces[0].shape
    result = shape((n * chunk, columns))
    return small_call(functools.partial(join_kernel, n, where), [result], pieces)[0]


def place_kernel(mine, count, *refs):
    parts, (out, sems) = refs[:count], refs[-2:]
    columns = out.shape[1] // 2
    core = lax.axis_index("core")
    half = core if mine else 1 - core
    pairs = []
    for i, part in enumerate(parts):
        width = part.shape[1]
        lanes = pl.ds(pl.multiple_of(half * columns + i * width, LANES), width)
        pairs.append((part, out.at[:, lanes]))
    wait_all(start_all(pairs, sems))


def place_parts(parts, dims, filled=None):
    anywhere = pl.BlockSpec(memory_space=pl.ANY)
    args = [*parts] + ([] if filled is None else [filled])
    return pl.pallas_call(
        functools.partial(place_kernel, filled is None, len(parts)),
        out_shape=shape(dims),
        in_specs=[anywhere] * len(args),
        out_specs=anywhere,
        scratch_shapes=[pltpu.SemaphoreType.DMA((len(parts),))],
        input_output_aliases={} if filled is None else {len(parts): 0},
        compiler_params=pltpu.CompilerParams(vmem_limit_bytes=8 * 2**20),
        cost_estimate=pl.CostEstimate(
            flops=0, bytes_accessed=2 * dims[0] * dims[1], transcendentals=0
        ),
    )(*args)


def shift(x, axes, by, n):
    return lax.ppermute(x, axes, [(i, (i + by) % n) for i in range(n)])


def per_device(sizes, q_nope, q_rope, latent, key_rope, q_pos, k_pos, w_uk, w_uv, w_o):
    heads = w_uk.shape[0]
    queries = q_nope.shape[0]
    keys = latent.shape[0]
    columns = w_o.shape[1] // 2
    swap = lambda a: shift(a, "core", 1, 2)
    ny, nx = sizes["y"], sizes["xl"] * sizes["xh"]

    def exchange(a, by_x, by_y):
        pairs = []
        spot = lambda x, y: (x % sizes["xl"] * ny + y) * sizes["xh"] + x // sizes["xl"]
        for x in range(nx):
            for y in range(ny):
                pairs.append((spot(x, y), spot(partner(x, nx, by_x), partner(y, ny, by_y))))
        return lax.ppermute(a, ("xl", "y", "xh"), pairs)

    pack, half = pack_keys(latent, key_rope, k_pos)
    rows = pack.shape[0]
    span = rows // 2
    first = exchange(half, 0, 1)
    second = exchange(half, 0, 2)
    across = exchange(half, 1, 0)
    q_nope, q_rope, w_uk, w_o, half = lax.optimization_barrier((q_nope, q_rope, w_uk, w_o, half))
    w_half = other_half(w_o)
    query = absorb(q_nope, q_rope, w_uk)
    positions = q_pos.reshape(queries, 1)
    first, second, across, query, w_half = lax.optimization_barrier(
        (first, second, across, query, w_half)
    )
    across_first = exchange(first, 1, 0)
    across_second = exchange(second, 2, 0)
    near = [first, second, across]
    swapped, first, second = lax.optimization_barrier(([swap(a) for a in near], first, second))
    far = exchange(second, 0, 1)
    cut = span // 2
    across_far = (exchange(first[:cut], 1, 2), exchange(second[cut:], 2, 1))

    def place(*blocks):
        def find(keys, queries):
            xl = lax.axis_index("xl")
            y, way = place_of("y")
            ids = [
                (1 - xl if over else xl) * ny + (y + way * d + ny) % ny for over, d in blocks
            ]
            return ids, (sizes["q0"] + (xl * ny + y) * queries) // keys

        return find

    both = [(0, 0, span), (1, 0, span)]
    state = attend(
        [[(2, 0, rows)], both, both, both],
        [pack] + [a for pair in zip(near, swapped) for a in pair],
        place((0, 0), (0, 1), (0, -1), (1, 0)),
        query, positions, None, None, heads, rows,
    )
    later, state = lax.optimization_barrier(
        ([far, across_first, across_second, *across_far], state)
    )
    swapped, w_half = lax.optimization_barrier(([swap(a) for a in later], w_half))
    w_other = swap(w_half)
    quarters = [(0, 0, cut), (1, 0, cut), (0, cut, span - cut), (1, cut, span - cut)]
    head_out = attend(
        [both, both, both, quarters],
        [a for pair in zip(later, swapped) for a in pair],
        place((0, 2), (1, 1), (1, -1), (1, 2)),
        query, positions, state, w_uv, heads, rows,
    )
    nz = sizes["z"]
    parts = []
    for part in project(nz, head_out, swap(head_out), w_o, w_other):
        piece = ring_sum(part, nz)
        crossed = shift(piece, "xh", 1, sizes["xh"])
        piece = small_call(sum_kernel, [shape(piece.shape)], [piece, crossed])[0]
        parts.append(join(nz, ring_gather(piece, nz)))
    dims = (queries, 2 * columns)
    return place_parts([swap(a) for a in parts], dims, place_parts(parts, dims))


def solution(mesh):
    sizes = {"xl": 2, "y": 4, "z": 8, "xh": 2, "core": 2, "q0": 2048}
    names = ("xl", "y", "z", "xh", "core")
    fine = Mesh(mesh.devices.reshape([sizes[n] for n in names]), names)
    return jax.shard_map(
        functools.partial(per_device, sizes),
        mesh=fine,
        in_specs=(
            P(SEQ, HEAD),
            P(SEQ, HEAD),
            P(SEQ, None),
            P(SEQ, None),
            P(SEQ),
            P(SEQ),
            P(HEAD, None, None),
            P(HEAD, None, None),
            P(HEAD, None),
        ),
        out_specs=P(SEQ, None),
        check_vma=False,
    )
```

```python
import functools
import math

import jax
import jax.numpy as jnp
from jax import lax
from jax.experimental import pallas as pl
from jax.experimental.pallas import tpu as pltpu
from jax.sharding import Mesh, PartitionSpec as P

F32, BF16, I32 = jnp.float32, jnp.bfloat16, jnp.int32
LOW = -1e30
LANES = 128
SEQ = ("xl", "y")
HEAD = ("z", "xh", "core")


def call(kernel, outs, args, scratch=(), copies=1, flops=0, moved=0, vmem=24):
    anywhere = pl.BlockSpec(memory_space=pl.ANY)
    return pl.pallas_call(
        kernel,
        out_shape=outs,
        in_specs=[anywhere] * len(args),
        out_specs=jax.tree.map(lambda _: anywhere, outs),
        scratch_shapes=list(scratch) + [pltpu.SemaphoreType.DMA((copies,))],
        compiler_params=pltpu.CompilerParams(vmem_limit_bytes=vmem * 2**20),
        cost_estimate=pl.CostEstimate(flops=flops, bytes_accessed=moved, transcendentals=0),
    )(*args)


def start_all(pairs, sems, first=0):
    copies = [
        pltpu.make_async_copy(source, target, sems.at[first + i])
        for i, (source, target) in enumerate(pairs)
    ]
    for copy in copies:
        copy.start()
    return copies


def wait_all(copies):
    for copy in copies:
        copy.wait()


def room(array):
    return pltpu.VMEM(array.shape, array.dtype)


def place_of(axis):
    place = lax.axis_index(axis)
    return place, 1 - 2 * (place % 2)


def partner(place, n, which):
    step = (0, 1, -1)[which]
    return (place + (step if place % 2 == 0 else -step)) % n


def shape(dims, dtype=BF16):
    return jax.ShapeDtypeStruct(tuple(dims), dtype)


def pack_kernel(latent_in, rope_in, pos_in, pack_out, half_out, latent, rope, pos, pack, sems):
    copies = start_all([(latent_in, latent), (rope_in, rope), (pos_in, pos)], sems)
    keys, width = latent.shape
    pairs, two = rope.shape
    rope_width = two // 2
    token = lax.broadcasted_iota(I32, (keys, pairs), 0)
    pair = lax.broadcasted_iota(I32, (keys, pairs), 1)
    even = (token == 2 * pair).astype(BF16)
    odd = (token == 2 * pair + 1).astype(BF16)
    wait_all(copies)
    order = (lax.broadcasted_iota(I32, (keys, keys), 0) == pos[...] % keys).astype(BF16)
    sorted_latent = jnp.dot(order, latent[...], preferred_element_type=F32)
    spread_even = jnp.dot(even, rope[...], preferred_element_type=F32)
    spread_odd = jnp.dot(odd, rope[...], preferred_element_type=F32)
    rows = jnp.concatenate(
        [spread_even[:, :rope_width], spread_odd[:, rope_width:]], axis=1
    ).astype(BF16)
    ordered = jnp.dot(order, rows, preferred_element_type=F32)
    turned = jnp.transpose(ordered)
    pack[pl.ds(0, keys), :] = sorted_latent.astype(BF16)
    pack[pl.ds(keys, rope_width), :] = (turned[:rope_width] + turned[rope_width:]).astype(BF16)
    span = half_out.shape[0]
    start = pl.multiple_of(lax.axis_index("core") * span, span)
    wait_all(start_all([(pack.at[pl.ds(start, span), :], half_out), (pack, pack_out)], sems))


def pack_keys(latent, key_rope, k_pos):
    keys, width = latent.shape
    rows = keys + key_rope.shape[0] * key_rope.shape[1] // keys
    args = [latent, key_rope, k_pos.reshape(1, keys)]
    return call(
        pack_kernel,
        [shape((rows, width)), shape((rows // 2, width))],
        args,
        [room(a) for a in args] + [pltpu.VMEM((rows, width), BF16)],
        copies=3,
        flops=2 * keys * keys * width,
        moved=3 * keys * width * 2,
        vmem=58,
    )


def query_kernel(scale, q_nope_in, q_rope_in, w_uk_in, out, q_nope, q_rope, w_uk, query, sems):
    pairs = [(q_nope_in, q_nope), (q_rope_in, q_rope), (w_uk_in, w_uk)]
    wait_all(start_all(pairs, sems))
    heads, nope, width = w_uk.shape
    queries = q_nope.shape[0]
    rope = q_rope.shape[1] // heads
    for h in range(heads):
        rows = pl.ds(h * queries, queries)
        absorbed = jnp.dot(
            q_nope[:, h * nope : (h + 1) * nope], w_uk[h], preferred_element_type=F32
        )
        query[rows, pl.ds(0, width)] = (absorbed * scale).astype(BF16)
        rotary = q_rope[:, h * rope : (h + 1) * rope].astype(F32) * scale
        query[rows, pl.ds(width, rope)] = rotary.astype(BF16)
    wait_all(start_all([(query, out)], sems))


def absorb(q_nope, q_rope, w_uk):
    heads, nope, width = w_uk.shape
    queries = q_nope.shape[0]
    rope = q_rope.shape[1] // heads
    scale = math.log2(math.e) / math.sqrt(nope + rope)
    result = shape((heads * queries, width + rope))
    return call(
        functools.partial(query_kernel, scale),
        result,
        [q_nope, q_rope, w_uk],
        [room(a) for a in (q_nope, q_rope, w_uk, result)],
        copies=3,
        flops=2 * queries * heads * nope * width,
        moved=2 * heads * queries * (nope + width),
    )


def half_kernel(w_o, half, held, sems):
    columns = half.shape[1]
    start = pl.multiple_of((1 - lax.axis_index("core")) * columns, LANES)
    wait_all(start_all([(w_o.at[:, pl.ds(start, columns)], held)], sems))
    wait_all(start_all([(held, half)], sems))


def other_half(w_o):
    half = shape((w_o.shape[0], w_o.shape[1] // 2))
    return call(
        half_kernel, half, [w_o], [room(half)], moved=2 * w_o.shape[0] * w_o.shape[1], vmem=58
    )


def attend_kernel(layout, first, last, heads, place, *refs):
    pieces = sum(len(block) for block in layout)
    blocks, refs = refs[:pieces], refs[pieces:]
    query_in, positions_in = refs[:2]
    refs = refs[2:]
    if not first:
        old, refs = refs[:3], refs[3:]
    if last:
        w_uv_in, out, refs = refs[0], refs[1], refs[2:]
    else:
        new, refs = refs[:3], refs[3:]
    top, total, acc, keys_in, query, positions, *rest, sems = refs
    state = (top, total, acc)
    count, rows, width = keys_in.shape
    keys = width
    queries = query.shape[0] // heads
    rope = rows - keys
    core = lax.axis_index("core")
    pairs = [(query_in, query), (positions_in, positions)]
    for b, block in enumerate(layout):
        for side, start, size in block:
            offset = start
            if side != 2:
                offset = (core if side == 0 else 1 - core) * (rows // 2) + start
                offset = pl.multiple_of(offset, 16)
            pairs.append((blocks[len(pairs) - 2], keys_in.at[b, pl.ds(offset, size), :]))
    if not first:
        pairs += list(zip(old, state))
    if last:
        w_uv, result = rest
        pairs.append((w_uv_in, w_uv))
    copies = start_all(pairs, sems)
    ids, diagonal = place(keys, queries)
    wait_all(copies)

    def work(group, masked, fresh):
        def score(h):
            part = pl.ds(h * queries, queries)
            found = []
            for b in group:
                latents = keys_in[b, pl.ds(0, keys), :]
                found.append(
                    lax.dot_general(
                        query[part, pl.ds(0, width)],
                        latents,
                        (((1,), (1,)), ((), ())),
                        preferred_element_type=F32,
                    )
                    + jnp.dot(
                        query[part, pl.ds(width, rope)],
                        keys_in[b, pl.ds(keys, rope), :],
                        preferred_element_type=F32,
                    )
                )
            return found

        def soften(h, found):
            part = pl.ds(h * queries, queries)
            if masked:
                limit = positions[...] - diagonal * keys
                where = lax.broadcasted_iota(I32, (queries, keys), 1)
                found = [jnp.where(where <= limit, scores, LOW) for scores in found]
            largest = functools.reduce(jnp.maximum, found)
            highest = jnp.max(largest, axis=1, keepdims=True)
            if fresh:
                now = jnp.broadcast_to(highest, (queries, LANES))
                factor = None
            else:
                before = top[part, :]
                now = jnp.maximum(before, highest)
                factor = jnp.exp2(before - now)
            wide_top = jnp.concatenate([now] * (keys // LANES), axis=1)
            probs, sums = [], None
            for scores in found:
                exps = jnp.exp2(scores - wide_top)
                for t in range(keys // LANES):
                    some = exps[:, t * LANES : (t + 1) * LANES]
                    sums = some if sums is None else sums + some
                probs.append(exps.astype(BF16))
            top[part, :] = now
            total[part, :] = sums if fresh else total[part, :] * factor + sums
            return probs, factor

        def gather(h, probs, factor):
            part = pl.ds(h * queries, queries)
            added = None
            for b, prob in zip(group, probs):
                more = jnp.dot(prob, keys_in[b, pl.ds(0, keys), :], preferred_element_type=F32)
                added = more if added is None else added + more
            if fresh:
                acc[part, :] = added
            else:
                stretch = jnp.concatenate([factor] * (width // LANES), axis=1)
                acc[part, :] = acc[part, :] * stretch + added

        found = score(0)
        for h in range(heads):
            following = score(h + 1) if h + 1 < heads else None
            gather(h, *soften(h, found))
            found = following

    def step(b, fresh=False):
        @pl.when(ids[b] < diagonal)
        def _():
            work([b], False, fresh)

        @pl.when(ids[b] == diagonal)
        def _():
            work([b], True, fresh)

    def pair(b):
        full = jnp.logical_and(ids[b] < diagonal, ids[b + 1] < diagonal)

        @pl.when(full)
        def _():
            work([b, b + 1], False, False)

        @pl.when(jnp.logical_not(full))
        def _():
            step(b)
            step(b + 1)

    begin = 0
    if first:
        step(0, True)
        begin = 1
    for b in range(begin, count):
        step(b)
    if last:
        for h in range(heads):
            part = pl.ds(h * queries, queries)
            sums = jnp.sum(total[part, :], axis=1, keepdims=True)
            context = (acc[part, :] / sums).astype(BF16)
            value = w_uv.shape[2]
            result[:, pl.ds(h * value, value)] = jnp.dot(
                context, w_uv[h], preferred_element_type=F32
            ).astype(BF16)
        wait_all(start_all([(result, out)], sems))
    else:
        wait_all(start_all(list(zip(state, new)), sems))


def attend(layout, pieces, place, query, positions, state, w_uv, heads, rows):
    width = pieces[0].shape[1]
    total_rows = query.shape[0]
    queries = total_rows // heads
    first, last = state is None, w_uv is not None
    stats = [
        shape((total_rows, LANES), F32),
        shape((total_rows, LANES), F32),
        shape((total_rows, width), F32),
    ]
    args = [*pieces, query, positions]
    if not first:
        args += list(state)
    scratch = [room(s) for s in stats] + [
        pltpu.VMEM((len(layout), rows, width), BF16),
        room(query),
        room(positions),
    ]
    outs = stats
    if last:
        args.append(w_uv)
        outs = shape((queries, heads * w_uv.shape[2]))
        scratch += [room(w_uv), room(outs)]
    return call(
        functools.partial(attend_kernel, layout, first, last, heads, place),
        outs,
        args,
        scratch,
        copies=len(args),
        flops=16 * total_rows * width * width * len(layout),
        moved=2 * total_rows * width * 4,
    )


PARTS = 2


def project_kernel(ring, first, mine, other, w_o, w_other, out, left, right):
    queries, depth = mine.shape
    chunk = queries // ring
    base = lax.axis_index("core") * w_other.shape[1] + first
    z, way = place_of("z")
    for d in range(ring):
        source = pl.ds(pl.multiple_of((z + way * d + ring) % ring * chunk, chunk), chunk)
        left[pl.ds(d * chunk, chunk), :] = mine[source, :]
        right[pl.ds(d * chunk, chunk), :] = other[source, :]
    tile = 256
    for t in range(out.shape[1] // tile):
        here = pl.ds(first + t * tile, tile)
        there = pl.ds(pl.multiple_of(base + t * tile, LANES), tile)
        out[:, pl.ds(t * tile, tile)] = (
            jnp.dot(left[...], w_o[:, there], preferred_element_type=F32)
            + jnp.dot(right[...], w_other[:, here], preferred_element_type=F32)
        ).astype(BF16)


def project(ring, part, mine, other, w_o, w_other):
    queries, depth = mine.shape
    columns = w_other.shape[1] // PARTS
    vmem = pl.BlockSpec(memory_space=pltpu.VMEM)
    return pl.pallas_call(
        functools.partial(project_kernel, ring, part * columns),
        out_shape=shape((queries, columns)),
        in_specs=[vmem] * 4,
        out_specs=vmem,
        scratch_shapes=[room(mine), room(other)],
        compiler_params=pltpu.CompilerParams(vmem_limit_bytes=24 * 2**20),
        cost_estimate=pl.CostEstimate(
            flops=4 * queries * depth * columns, bytes_accessed=4 * depth * columns, transcendentals=0
        ),
    )(mine, other, w_o, w_other)


def small_call(kernel, outs, args):
    specs, arrays = [], []
    for arg in args:
        array, block, size = arg if isinstance(arg, tuple) else (arg, 0, arg.shape[0])
        arrays.append(array)
        specs.append(
            pl.BlockSpec((size, array.shape[1]), functools.partial(lambda k, i: (k, 0), block))
        )
    moved = 4 * sum(math.prod(a.shape) for a in outs)
    return pl.pallas_call(
        kernel,
        out_shape=outs,
        grid=(1,),
        in_specs=specs,
        out_specs=[pl.BlockSpec(a.shape, lambda i: (0, 0)) for a in outs],
        compiler_params=pltpu.CompilerParams(vmem_limit_bytes=16 * 2**20),
        cost_estimate=pl.CostEstimate(flops=0, bytes_accessed=moved, transcendentals=0),
    )(*arrays)


def wide(ref):
    return ref[...].astype(F32)


def meet_kernel(start, moving, own, out):
    met = pl.ds(start, moving.shape[0])
    if moving.shape[0] != out.shape[0]:
        out[...] = own[...]
    out[met, :] = (own[met, :].astype(F32) + wide(moving)).astype(BF16)


def sum_kernel(*refs):
    *parts, out = refs
    out[...] = sum(wide(part) for part in parts).astype(BF16)


def exchange_z(a, n, which):
    return lax.ppermute(a, "z", [(z, partner(z, n, which)) for z in range(n)])


def ring_sum(rows, n):
    size = rows.shape[0] // n
    whole = shape((size, rows.shape[1]))
    far, cut = n // 2, size // 2
    one = exchange_z(rows[far * size : far * size + cut], n, 1)
    two = exchange_z(rows[far * size + cut : (far + 1) * size], n, 2)
    for d in range(far - 1, 0, -1):
        for_two = small_call(
            functools.partial(meet_kernel, 0), [whole], [one, (rows, n - d, size)]
        )[0]
        for_one = small_call(
            functools.partial(meet_kernel, size - two.shape[0]), [whole], [two, (rows, d, size)]
        )[0]
        one, two = exchange_z(for_one, n, 1), exchange_z(for_two, n, 2)
    return small_call(sum_kernel, [whole], [one, two, (rows, 0, size)])[0]


def ring_gather(piece, n):
    far = n // 2
    cut = piece.shape[0] // 2
    found = [(0, 0, piece)]
    one = two = piece
    for d in range(1, far):
        one, two = exchange_z(two, n, 1), exchange_z(one, n, 2)
        found += [(d, 0, one), (-d, 0, two)]
    found.append((far, cut, exchange_z(two[cut:], n, 1)))
    found.append((far, 0, exchange_z(one[:cut], n, 2)))
    return found


def join_kernel(n, where, *refs):
    pieces, out = refs[:-1], refs[-1]
    chunk = out.shape[0] // n
    z, way = place_of("z")
    for (d, row), piece in zip(where, pieces):
        start = pl.multiple_of((z + way * d + n) % n * chunk + row, 16)
        out[pl.ds(start, piece.shape[0]), :] = piece[...]


def join(n, found):
    where = [(d, row) for d, row, _ in found]
    pieces = [array for *_, array in found]
    chunk, columns = pieces[0].shape
    result = shape((n * chunk, columns))
    return small_call(functools.partial(join_kernel, n, where), [result], pieces)[0]


def place_kernel(mine, index, part, *refs):
    out, sem = refs[-2:]
    columns, width = out.shape[1] // 2, part.shape[1]
    core = lax.axis_index("core")
    half = core if mine else 1 - core
    lanes = pl.ds(pl.multiple_of(half * columns + index * width, LANES), width)
    wait_all(start_all([(part, out.at[:, lanes])], sem))


def place_part(mine, index, part, dims, filled=None):
    anywhere = pl.BlockSpec(memory_space=pl.ANY)
    args = [part] + ([] if filled is None else [filled])
    return pl.pallas_call(
        functools.partial(place_kernel, mine, index),
        out_shape=shape(dims),
        in_specs=[anywhere] * len(args),
        out_specs=anywhere,
        scratch_shapes=[pltpu.SemaphoreType.DMA((1,))],
        input_output_aliases={} if filled is None else {1: 0},
        compiler_params=pltpu.CompilerParams(vmem_limit_bytes=8 * 2**20),
        cost_estimate=pl.CostEstimate(
            flops=0, bytes_accessed=dims[0] * dims[1], transcendentals=0
        ),
    )(*args)


def shift(x, axes, by, n):
    return lax.ppermute(x, axes, [(i, (i + by) % n) for i in range(n)])


def per_device(sizes, q_nope, q_rope, latent, key_rope, q_pos, k_pos, w_uk, w_uv, w_o):
    heads = w_uk.shape[0]
    queries = q_nope.shape[0]
    keys = latent.shape[0]
    columns = w_o.shape[1] // 2
    swap = lambda a: shift(a, "core", 1, 2)
    ny, nx = sizes["y"], sizes["xl"] * sizes["xh"]

    def exchange(a, by_x, by_y):
        pairs = []
        spot = lambda x, y: (x % sizes["xl"] * ny + y) * sizes["xh"] + x // sizes["xl"]
        for x in range(nx):
            for y in range(ny):
                pairs.append((spot(x, y), spot(partner(x, nx, by_x), partner(y, ny, by_y))))
        return lax.ppermute(a, ("xl", "y", "xh"), pairs)

    pack, half = pack_keys(latent, key_rope, k_pos)
    rows = pack.shape[0]
    span = rows // 2
    first = exchange(half, 0, 1)
    second = exchange(half, 0, 2)
    across = exchange(half, 1, 0)
    q_nope, q_rope, w_uk, w_o, half = lax.optimization_barrier((q_nope, q_rope, w_uk, w_o, half))
    w_half = other_half(w_o)
    query = absorb(q_nope, q_rope, w_uk)
    positions = q_pos.reshape(queries, 1)
    first, second, across, query, w_half = lax.optimization_barrier(
        (first, second, across, query, w_half)
    )
    across_first = exchange(first, 1, 0)
    across_second = exchange(second, 2, 0)
    near = [first, second, across]
    swapped, first, second = lax.optimization_barrier(([swap(a) for a in near], first, second))
    far = exchange(second, 0, 1)
    cut = span // 2
    across_far = (exchange(first[:cut], 1, 2), exchange(second[cut:], 2, 1))

    def place(*blocks):
        def find(keys, queries):
            xl = lax.axis_index("xl")
            y, way = place_of("y")
            ids = [
                (1 - xl if over else xl) * ny + (y + way * d + ny) % ny for over, d in blocks
            ]
            return ids, (sizes["q0"] + (xl * ny + y) * queries) // keys

        return find

    both = [(0, 0, span), (1, 0, span)]
    state = attend(
        [[(2, 0, rows)], both, both, both],
        [pack] + [a for pair in zip(near, swapped) for a in pair],
        place((0, 0), (0, 1), (0, -1), (1, 0)),
        query, positions, None, None, heads, rows,
    )
    later, state = lax.optimization_barrier(
        ([far, across_first, across_second, *across_far], state)
    )
    swapped, w_half = lax.optimization_barrier(([swap(a) for a in later], w_half))
    w_other = swap(w_half)
    quarters = [(0, 0, cut), (1, 0, cut), (0, cut, span - cut), (1, cut, span - cut)]
    head_out = attend(
        [both, both, both, quarters],
        [a for pair in zip(later, swapped) for a in pair],
        place((0, 2), (1, 1), (1, -1), (1, 2)),
        query, positions, state, w_uv, heads, rows,
    )
    nz = sizes["z"]
    parts = []
    other = swap(head_out)
    for index in range(PARTS):
        part = project(nz, index, head_out, other, w_o, w_other)
        piece = ring_sum(part, nz)
        crossed = shift(piece, "xh", 1, sizes["xh"])
        piece = small_call(sum_kernel, [shape(piece.shape)], [piece, crossed])[0]
        parts.append(join(nz, ring_gather(piece, nz)))
    result = None
    for mine, arrays in ((True, parts), (False, [swap(a) for a in parts])):
        for index, part in enumerate(arrays):
            result = place_part(mine, index, part, (queries, 2 * columns), result)
    return result


def solution(mesh):
    sizes = {"xl": 2, "y": 4, "z": 8, "xh": 2, "core": 2, "q0": 2048}
    names = ("xl", "y", "z", "xh", "core")
    fine = Mesh(mesh.devices.reshape([sizes[n] for n in names]), names)
    return jax.shard_map(
        functools.partial(per_device, sizes),
        mesh=fine,
        in_specs=(
            P(SEQ, HEAD),
            P(SEQ, HEAD),
            P(SEQ, None),
            P(SEQ, None),
            P(SEQ),
            P(SEQ),
            P(HEAD, None, None),
            P(HEAD, None, None),
            P(HEAD, None),
        ),
        out_specs=P(SEQ, None),
        check_vma=False,
    )
```
